32 devices in a mesh: dp: 8 (over z, x), seq: 4 (over y, core).
Axes of the slice: x: 2, y: 2, z: 4, core: 2. Of those that a mesh axis runs over, the one named last changes fastest.
Arguments:
- text_input: bfloat16 [16, 512, 768], P('dp', 'seq'), may hold values from -6 to 6
- layout_input: bfloat16 [16, 512, 192], P('dp', 'seq'), may hold values from -6 to 6
- segments: int32 [16, 512], P('dp', 'seq'), may hold values from 0 to 4, as said below
- text_cotangent: bfloat16 [16, 512, 768], P('dp', 'seq'), may hold values from -6 to 6
- layout_cotangent: bfloat16 [16, 512, 192], P('dp', 'seq'), may hold values from -6 to 6
- text_project: bfloat16 [768, 2304], replicated, may hold values from -0.21875 to 0.21875
- text_biases: bfloat16 [6, 768], replicated, may hold values from -3 to 3
- text_gains: bfloat16 [2, 768], replicated, may hold values from 0.5 to 1.5
- text_merge: bfloat16 [768, 768], replicated, may hold values from -1.5 to 1.5
- text_expand: bfloat16 [768, 3072], replicated, may hold values from -0.21875 to 0.21875
- text_offsets: bfloat16 [3072], replicated, may hold values from -3 to 3
- text_shrink: bfloat16 [3072, 768], replicated, may hold values from -0.109375 to 0.109375
- layout_project: bfloat16 [192, 576], replicated, may hold values from -0.4375 to 0.4375
- layout_biases: bfloat16 [6, 192], replicated, may hold values from -3 to 3
- layout_gains: bfloat16 [2, 192], replicated, may hold values from 0.5 to 1.5
- layout_merge: bfloat16 [192, 192], replicated, may hold values from -3 to 3
- layout_expand: bfloat16 [192, 768], replicated, may hold values from -0.4375 to 0.4375
- layout_offsets: bfloat16 [768], replicated, may hold values from -3 to 3
- layout_shrink: bfloat16 [768, 192], replicated, may hold values from -0.21875 to 0.21875
Outputs:
- text_result: bfloat16 [16, 512, 768], P('dp', 'seq')
- layout_result: bfloat16 [16, 512, 192], P('dp', 'seq')
- text_sensitivity: float32 [16, 512, 768], P('dp', 'seq')
- layout_sensitivity: float32 [16, 512, 192], P('dp', 'seq')
- text_project_delta: float32 [768, 2304], P(None, 'seq')
- text_biases_delta: float32 [6, 768], P(None, 'seq')
- text_gains_delta: float32 [2, 768], P(None, 'seq')
- text_merge_delta: float32 [768, 768], P(None, 'seq')
- text_expand_delta: float32 [768, 3072], P(None, 'seq')
- text_offsets_delta: float32 [3072], P('seq')
- text_shrink_delta: float32 [3072, 768], P(None, 'seq')
- layout_project_delta: float32 [192, 576], P(None, 'seq')
- layout_biases_delta: float32 [6, 192], P(None, 'seq')
- layout_gains_delta: float32 [2, 192], P(None, 'seq')
- layout_merge_delta: float32 [192, 192], P(None, 'seq')
- layout_expand_delta: float32 [192, 768], P(None, 'seq')
- layout_offsets_delta: float32 [768], P('seq')
- layout_shrink_delta: float32 [768, 192], P(None, 'seq')
The draws below stay inside these ranges and needn't reach their ends.
Inputs may be any that keep to these rules, and one draw needn't show every extreme that they name: `segments`: along the 512 rows of a pack the segment ids never fall; rows with equal ids form one document. Each pack holds one long document through its middle and up to four short ones at its ends.
All inputs are finite; a program needn't handle non-finite values.
Results may differ from the reference program's by a relative error of at most 0.014.
Values may be sent and summed in bfloat16 or wider, within the bound.
No kernel may reach another device: no remote copies, remote signals or barrier semaphores. Data moves between devices by JAX's collectives and lax.ppermute only.
A program may use at most 192 MiB of HBM per device.

```python
import math
import jax
import jax.numpy as jnp
from jax import lax

DT = 768
HEADS = 12
FT = 3072
DL = 192
FL = 768
BLK = 128
ET = 64
EL = 16
LEN = 512
PACKS = 16


def draw_segments(key, part):
    key = jax.random.fold_in(key, 11)
    keys_list = jax.random.split(key, 4)
    first = jax.random.randint(keys_list[0], (PACKS, 1), 2, BLK // 2 + 2)
    last = jax.random.randint(keys_list[1], (PACKS, 1), LEN - BLK // 2, LEN - 1)
    early = jax.random.randint(keys_list[2], (PACKS, 1), 0, 1048576) % (first - 1) + 1
    late = last + 1 + jax.random.randint(keys_list[3], (PACKS, 1), 0, 1048576) % (LEN - 1 - last)
    places = lax.broadcasted_iota(jnp.int32, (PACKS, LEN), 1)
    total = (places >= early).astype(jnp.int32) + (places >= first).astype(jnp.int32)
    total = total + (places >= last).astype(jnp.int32) + (places >= late).astype(jnp.int32)
    return total.astype(jnp.int32)


def levels(rng, extent, cuts, smallest, largest):
    loudness = 1.0
    for axis_at, blocks in cuts:
        steps = jax.random.uniform(jax.random.fold_in(jax.random.fold_in(rng, 6), axis_at), (blocks,), jnp.float32, smallest / len(cuts), largest / len(cuts))
        loudness = loudness * jnp.repeat(jnp.exp(steps), extent[axis_at] // blocks).reshape((-1,) + (1,) * (len(extent) - 1 - axis_at))
    return loudness


def scatter_about(stream_key, extent, scale, most, cuts=(), kind=jnp.bfloat16):
    factor_of = levels(stream_key, extent, cuts, -0.22, 0.18) if cuts else 1.0
    entries = jax.random.normal(stream_key, extent, jnp.float32) * scale * factor_of
    return jnp.minimum(jnp.maximum(entries, -most), most).astype(kind)


def setup_inputs(seed: int = 0) -> dict:
    splits = jax.random.split(jax.random.key(seed), 20)
    return {
        "text_input": scatter_about(splits[0], (PACKS, LEN, DT), 1.0, 6.0, ((0, 8), (1, 4))),
        "layout_input": scatter_about(splits[1], (PACKS, LEN, DL), 1.0, 6.0, ((0, 8), (1, 4))),
        "segments": draw_segments(jax.random.fold_in(splits[19], 71), 0),
        "text_cotangent": scatter_about(splits[3], (PACKS, LEN, DT), 1.0, 6.0, ((0, 8), (1, 4))),
        "layout_cotangent": scatter_about(splits[4], (PACKS, LEN, DL), 1.0, 6.0, ((0, 8), (1, 4))),
        "text_project": scatter_about(splits[5], (DT, 3 * DT), DT ** -0.5, 0.21875),
        "text_biases": scatter_about(splits[6], (6, DT), 0.5, 3.0),
        "text_gains": jnp.clip(1.0 + 0.1 * jax.random.normal(splits[7], (2, DT), jnp.float32), 0.5, 1.5).astype(jnp.bfloat16),
        "text_merge": scatter_about(splits[8], (DT, DT), (max(DT // 48, 1)) ** -0.5, 1.5),
        "text_expand": scatter_about(splits[9], (DT, FT), DT ** -0.5, 0.21875),
        "text_offsets": scatter_about(splits[10], (FT,), 0.5, 3.0),
        "text_shrink": scatter_about(splits[11], (FT, DT), FT ** -0.5, 0.109375),
        "layout_project": scatter_about(splits[12], (DL, 3 * DL), DL ** -0.5, 0.4375),
        "layout_biases": scatter_about(splits[13], (6, DL), 0.5, 3.0),
        "layout_gains": jnp.clip(1.0 + 0.1 * jax.random.normal(splits[14], (2, DL), jnp.float32), 0.5, 1.5).astype(jnp.bfloat16),
        "layout_merge": scatter_about(splits[15], (DL, DL), (max(DL // 48, 1)) ** -0.5, 3.0),
        "layout_expand": scatter_about(splits[16], (DL, FL), DL ** -0.5, 0.4375),
        "layout_offsets": scatter_about(splits[17], (FL,), 0.5, 3.0),
        "layout_shrink": scatter_about(splits[18], (FL, DL), FL ** -0.5, 0.21875),
    }


HIGHEST = lax.Precision.HIGHEST
EPSILON = 1e-05
MASKED = -1000000000.0

@jax.custom_vjp
def low(v):
    return lax.optimization_barrier(v.astype(jnp.bfloat16)).astype(jnp.float32)

@jax.custom_vjp
def low_back(v):
    return v

def low_keep(v):
    return (low(v), None)

def low_pass(kept, grad):
    return (grad,)

def back_keep(v):
    return (v, None)

def back_low(kept, grad):
    return (low(grad),)
low.defvjp(low_keep, low_pass)
low_back.defvjp(back_keep, back_low)

def layer_norm(values, gains, shifts):
    centre = values - lax.optimization_barrier(jnp.mean(values, axis=-1, keepdims=True))
    spread = lax.optimization_barrier(jnp.mean(centre * centre, axis=-1, keepdims=True))
    return centre * lax.rsqrt(spread + EPSILON) * gains + shifts

def matmul(left, right):
    return jnp.dot(left, right, precision=HIGHEST)

def head_split(array, heads):
    return array.reshape(array.shape[0], array.shape[1], heads, array.shape[2] // heads)

def project(flat_rows, weight, biases):
    model_width = flat_rows.shape[1]
    joined = matmul(flat_rows, weight)
    queries = low_back(low(joined[:, :model_width] + biases[0]))
    key_rows = low_back(low(joined[:, model_width:2 * model_width]))
    value_rows = low_back(low(joined[:, 2 * model_width:] + biases[1]))
    return (queries, key_rows, value_rows)

def scores(queries, key_rows, head_size):
    raw = jnp.einsum('gihe,gjhe->ghij', head_split(queries, HEADS), head_split(key_rows, HEADS), precision=HIGHEST)
    return raw * head_size ** (-0.5)

def mixing(probs, value_rows):
    mixed = jnp.einsum('ghij,gjhe->gihe', low(probs), head_split(value_rows, HEADS), precision=HIGHEST)
    return low_back(low(mixed.reshape(mixed.shape[0], mixed.shape[1], -1)))

def attend(text_query, text_key, text_value, layout_query, layout_key, layout_value, fixed_query, fixed_key, segment_rows):
    text_score = low_back(scores(text_query, text_key, ET))
    layout_score = low_back(scores(layout_query, layout_key, EL))
    fixed_score = scores(fixed_query, fixed_key, EL)
    allowed = segment_rows[:, None, :, None] == segment_rows[:, None, None, :]
    text_prob = jax.nn.softmax(jnp.where(allowed, text_score + fixed_score, MASKED), axis=-1)
    layout_prob = jax.nn.softmax(jnp.where(allowed, layout_score + text_score, MASKED), axis=-1)
    return (mixing(text_prob, text_value), mixing(layout_prob, layout_value))

def attend_all(members):
    group_size = math.gcd(PACKS, max(1, 4096 // LEN))
    stacked = tuple((member.reshape((PACKS // group_size, group_size) + member.shape[1:]) for member in members))
    checked = jax.checkpoint(attend)

    def attend_step(unused, block_inputs):
        return (unused, checked(*block_inputs))
    unused, contexts = lax.scan(attend_step, jnp.zeros((), jnp.float32), stacked)
    return (contexts[0].reshape(PACKS * LEN, -1), contexts[1].reshape(PACKS * LEN, -1))

def stream_tail(flat_rows, context, biases, gains, merge, expand, offsets, shrink):
    attention_rows = low_back(matmul(context, merge) + biases[2])
    hidden = layer_norm(flat_rows + attention_rows, gains[0], biases[3])
    before = low_back(matmul(low(hidden), expand) + offsets)
    branch = low_back(matmul(low(jax.nn.gelu(before, approximate=False)), shrink) + biases[4])
    return layer_norm(hidden + branch, gains[1], biases[5])

def reference(text_input, layout_input, segments, text_cotangent, layout_cotangent, text_project, text_biases, text_gains, text_merge, text_expand, text_offsets, text_shrink, layout_project, layout_biases, layout_gains, layout_merge, layout_expand, layout_offsets, layout_shrink):
    floats = tuple((member.astype(jnp.float32) for member in (text_input, layout_input, text_project, text_biases, text_gains, text_merge, text_expand, text_offsets, text_shrink, layout_project, layout_biases, layout_gains, layout_merge, layout_expand, layout_offsets, layout_shrink)))
    fixed_query, fixed_key, unused = project(floats[1].reshape(PACKS * LEN, DL), floats[9], floats[10])

    def forward(text_rows, layout_rows, t_project, t_biases, t_gains, t_merge, t_expand, t_offsets, t_shrink, l_project, l_biases, l_gains, l_merge, l_expand, l_offsets, l_shrink):
        text_flat = text_rows.reshape(PACKS * LEN, DT)
        layout_flat = layout_rows.reshape(PACKS * LEN, DL)
        text_query, text_key, text_value = project(text_flat, t_project, t_biases)
        layout_query, layout_key, layout_value = project(layout_flat, l_project, l_biases)
        members = (text_query, text_key, text_value, layout_query, layout_key, layout_value, fixed_query, fixed_key)
        shaped = tuple((member.reshape(PACKS, LEN, -1) for member in members)) + (segments,)
        text_context, layout_context = attend_all(shaped)
        text_output = stream_tail(text_flat, text_context, t_biases, t_gains, t_merge, t_expand, t_offsets, t_shrink)
        layout_output = stream_tail(layout_flat, layout_context, l_biases, l_gains, l_merge, l_expand, l_offsets, l_shrink)
        return (text_output.reshape(PACKS, LEN, DT), layout_output.reshape(PACKS, LEN, DL))
    results, backward = jax.vjp(forward, *floats)
    grads = backward((text_cotangent.astype(jnp.float32), layout_cotangent.astype(jnp.float32)))
    return (results[0].astype(jnp.bfloat16), results[1].astype(jnp.bfloat16), grads[0], grads[1], grads[2], grads[3], grads[4], grads[5], grads[6], grads[7], grads[8], grads[9], grads[10], grads[11], grads[12], grads[13], grads[14], grads[15])
```

```python
import functools

import jax
import jax.numpy as jnp
from jax import lax
from jax.experimental import pallas as pl
from jax.experimental.pallas import tpu as pltpu
from jax.sharding import PartitionSpec as P

HEADS = 12
EPSILON = 1e-05
MASKED = -1000000000.0
F32 = jnp.float32
BF16 = jnp.bfloat16
DT = 768
DL = 192
FT = 3072
FL = 768
LANES = 128
SLAB = 256
MIB = 1024 * 1024

VMEM = pl.BlockSpec(memory_space=pltpu.VMEM)
ANY = pl.BlockSpec(memory_space=pl.ANY)
SMEM = pl.BlockSpec(memory_space=pltpu.SMEM)


def dot(left, right):
    return jnp.dot(left, right, preferred_element_type=F32)


def dot_nt(left, right):
    return lax.dot_general(left, right, (((1,), (1,)), ((), ())), preferred_element_type=F32)


def shape_of(shape, dtype):
    return jax.ShapeDtypeStruct(shape, dtype)


def copies_of(pairs, sems, base):
    made = []
    for at, (source, target) in enumerate(pairs):
        copy = pltpu.make_async_copy(source, target, sems.at[base + at])
        copy.start()
        made.append(copy)
    return made


def wait_all(made):
    for copy in made:
        copy.wait()


def gather_pairs(blocks, rows, packs, target):
    span = rows * len(blocks)
    pairs = []
    for at, block in enumerate(blocks):
        for pack in range(packs):
            pairs.append(
                (
                    block.at[pl.ds(pack * rows, rows), :],
                    target.at[pl.ds(pack * span + at * rows, rows), :],
                )
            )
    return pairs


def lane_masks(pair_at):
    lanes = lax.broadcasted_iota(jnp.int32, (1, LANES), 1)
    low_half = lanes < 64
    group_of_16 = lax.shift_right_logical(lanes, 4)
    first = group_of_16 == 2 * lax.rem(pair_at, 4)
    second = group_of_16 == 2 * lax.rem(pair_at, 4) + 1
    return (low_half, first, second)


def stacked_heads(text_rows, layout_rows, masks):
    low_half, first, second = masks
    zero_text = jnp.zeros_like(text_rows)
    zero_layout = jnp.zeros_like(layout_rows)
    top = jnp.concatenate(
        [jnp.where(low_half, text_rows, zero_text), jnp.where(first, layout_rows, zero_layout)],
        axis=1,
    )
    bottom = jnp.concatenate(
        [jnp.where(low_half, zero_text, text_rows), jnp.where(second, layout_rows, zero_layout)],
        axis=1,
    )
    return jnp.concatenate([top, bottom], axis=0)


def normalized(values):
    centre = values - jnp.mean(values, axis=-1, keepdims=True)
    spread = jnp.mean(centre * centre, axis=-1, keepdims=True)
    inverse = lax.rsqrt(spread + EPSILON)
    return (centre * inverse, inverse)


def norm_back(delta, unit, inverse):
    return inverse * (
        delta
        - jnp.mean(delta, axis=-1, keepdims=True)
        - unit * jnp.mean(delta * unit, axis=-1, keepdims=True)
    )


def column_sum(values):
    return jnp.sum(values, axis=0, keepdims=True)


def feed_forward(hidden_low, expand, offsets, shrink, active, slope, chunk, branch_ref):
    width = expand.shape[1]
    for at in range(width // chunk):
        part = pl.ds(at * chunk, chunk)
        before = dot(hidden_low, expand[:, part]) + offsets[:, part].astype(F32)
        share = 0.5 + 0.5 * lax.erf(before * (0.5**0.5))
        density = jnp.exp(-0.5 * (before * before)) * 0.3989422804014327
        active_part = (before * share).astype(BF16)
        active[:, part] = active_part
        slope[:, part] = (share + before * density).astype(BF16)
        product = dot(active_part, shrink[part, :])
        if at == 0:
            branch_ref[...] = product
        else:
            branch_ref[...] += product


def forward_kernel(
    packs,
    rows,
    place,
    x0,
    x1,
    x2,
    x3,
    wt_in,
    wl_in,
    mt_in,
    et_in,
    st_in,
    ml,
    el,
    sl,
    cot_t,
    cot_l,
    bt,
    gt,
    ot,
    bl,
    gl,
    ol,
    res_t,
    res_l,
    q_t,
    q_l,
    kt_out,
    kl_out,
    vt_out,
    vl_out,
    p_out,
    ctx_t,
    ctx_l,
    hid_t,
    unit_t,
    inv_t,
    sum_t,
    slope_t,
    hid_l,
    unit_l,
    inv_l,
    sum_l,
    slope_l,
    act_l,
    sv_t,
    sv_l,
    g0,
    g1,
    g2,
    g3,
    xs,
    wt,
    wl,
    mt,
    et,
    st,
    k_t,
    k_l,
    v_t,
    v_l,
    prob,
    bias,
    act_t,
    turned,
    branch_t,
    branch_l,
    grads,
    sems,
):
    blocks = (x0, x1, x2, x3)
    keys = rows * len(blocks)
    tokens = packs * rows
    x_copies = copies_of(gather_pairs(blocks, rows, packs, xs), sems, 0)
    base = len(x_copies)
    w_copies = copies_of(((wt_in, wt), (wl_in, wl), (mt_in, mt), (et_in, et), (st_in, st)), sems, base)
    base += 5
    wait_all(x_copies)
    wait_all(w_copies[:2])

    text_bias = bt[...].astype(F32)
    layout_bias = bl[...].astype(F32)
    for pack in range(packs):
        own = pl.ds(pack * keys, rows)
        mine = pl.ds(pack * rows, rows)
        q_t[mine, :] = (dot(xs[own, :DT], wt[:, :DT]) + text_bias[0:1, :]).astype(BF16) * 0.125
        q_l[mine, :] = (dot(xs[own, DT:], wl[:, :SLAB]) + layout_bias[0:1, :]).astype(BF16) * 0.25

    step = 256

    def key_rows(at, unused):
        span = pl.ds(pl.multiple_of(at * step, step), step)
        k_t[span, :] = dot(xs[span, :DT], wt[:, DT : 2 * DT]).astype(BF16)
        v_t[span, :] = (dot(xs[span, :DT], wt[:, 2 * DT :]) + text_bias[1:2, :]).astype(BF16)
        k_l[span, :] = dot(xs[span, DT:], wl[:, SLAB : 2 * SLAB]).astype(BF16)
        v_l[span, :] = (dot(xs[span, DT:], wl[:, 2 * SLAB :]) + layout_bias[1:2, :]).astype(BF16)
        return unused

    lax.fori_loop(0, packs * keys // step, key_rows, 0)
    kv_copies = copies_of(((k_t, kt_out), (k_l, kl_out), (v_t, vt_out), (v_l, vl_out)), sems, base)
    base += 4

    marks = lax.broadcasted_iota(jnp.int32, (1, LANES), 1) - 64
    for pack in range(packs):
        slab = xs[pl.ds(pack * keys, keys), DT + LANES : DT + 2 * LANES].astype(F32)
        hot = jnp.where((slab == marks.astype(F32)) & (marks >= 0), 1.0, 0.0).astype(BF16)
        same = dot_nt(hot[:rows], hot)
        bias[pack] = jnp.where(same > 0.5, 0.0, MASKED)

    ctx_l[...] = jnp.zeros_like(ctx_l)

    def head_pair(pair_at, unused):
        masks = lane_masks(pair_at)
        text_lanes = pl.ds(pl.multiple_of(pair_at * LANES, LANES), LANES)
        layout_lanes = pl.ds(pl.multiple_of(pair_at // 4 * LANES, LANES), LANES)
        for pack in range(packs):
            mine = pl.ds(pack * rows, rows)
            span = pl.ds(pack * keys, keys)
            queries = stacked_heads(q_t[mine, text_lanes], q_l[mine, layout_lanes], masks)
            both_keys = jnp.concatenate([k_t[span, text_lanes], k_l[span, layout_lanes]], axis=1)
            both_values = jnp.concatenate([v_t[span, text_lanes], v_l[span, layout_lanes]], axis=1)
            allowed = bias[pack]
            logit = dot_nt(queries, both_keys) + jnp.concatenate([allowed, allowed], axis=0)
            raised = jnp.exp(logit - jnp.max(logit, axis=1, keepdims=True))
            low = (raised * (1.0 / jnp.sum(raised, axis=1, keepdims=True))).astype(BF16)
            prob[pair_at, pack] = low
            mixed = dot(low, both_values).astype(BF16)
            ctx_t[mine, text_lanes] = jnp.where(masks[0], mixed[:rows, :LANES], mixed[rows:, :LANES])
            kept = ctx_l[mine, layout_lanes]
            kept = jnp.where(masks[1], mixed[:rows, LANES:], kept)
            ctx_l[mine, layout_lanes] = jnp.where(masks[2], mixed[rows:, LANES:], kept)
        return unused

    lax.fori_loop(0, HEADS // 2, head_pair, 0)
    p_copies = copies_of(((prob, p_out),), sems, base)
    base += 1

    wait_all(w_copies[2:])

    def own_rows(lanes):
        return jnp.concatenate(
            [xs[pl.ds(pack * keys, rows), lanes].astype(F32) for pack in range(packs)], axis=0
        )

    def tail(x, ctx, merge, expand, offsets, shrink, b, g, cot, active, slope, branch, chunk, out, hid, unit, inv, delta, sv):
        width = merge.shape[1]
        middle = x + dot(ctx, merge[...]) + b[2:3, :width]
        unit_first, inverse_first = normalized(middle)
        hidden = unit_first * g[0:1, :] + b[3:4, :width]
        hidden_low = hidden.astype(BF16)
        hid[...] = hidden_low
        unit[...] = unit_first
        inv[...] = inverse_first
        feed_forward(hidden_low, expand, offsets, shrink, active, slope, chunk, branch)
        unit_second, inverse_second = normalized(hidden + branch[...] + b[4:5, :width])
        out[...] = (unit_second * g[1:2, :] + b[5:6, :width]).astype(BF16)
        cotangent = cot[...].astype(F32)
        sv[1:2, :] = column_sum(cotangent)
        sv[2:3, :] = column_sum(cotangent * unit_second)
        sum_delta = norm_back(cotangent * g[1:2, :], unit_second, inverse_second)
        delta[...] = sum_delta
        rounded = sum_delta.astype(BF16).astype(F32)
        sv[0:1, :] = column_sum(rounded)
        return rounded

    rounded = tail(
        own_rows(slice(0, DT)), ctx_t[...], mt, et, ot, st, text_bias, gt[...].astype(F32),
        cot_t, act_t, slope_t, branch_t, 512, res_t, hid_t, unit_t, inv_t, sum_t, sv_t,
    )
    turned[...] = rounded.T.astype(BF16)
    s = place[0]
    out_copies = []
    share = DT // 4
    for at, target in ((3, g3), (1, g1), (2, g2), (0, g0)):
        mark = pl.multiple_of(jnp.bitwise_xor(s, at) * share, share)
        own = turned[pl.ds(mark, share), :]
        for block in range(FT // DT):
            grads[at, pl.ds(block * share, share), :] = dot(
                own, act_t[:, block * DT : (block + 1) * DT]
            ).astype(BF16)
        out_copies += copies_of(((grads.at[at], target),), sems, base)
        base += 1
    tail(
        own_rows(slice(DT, DT + DL)), ctx_l[...], ml, el, ol, sl, layout_bias, gl[...].astype(F32),
        cot_l, act_l, slope_l, branch_l, 256, res_l, hid_l, unit_l, inv_l, sum_l, sv_l,
    )
    wait_all(kv_copies)
    wait_all(p_copies)
    wait_all(out_copies)


def forward_call(place, blocks, wt, wl, mt, et, st, ml, el, sl, cot_t, cot_l, bt, gt, ot, bl, gl, ol, packs, rows):
    tokens = packs * rows
    every = tokens * len(blocks)
    keys = rows * len(blocks)
    pairs = HEADS // 2
    outs = (
        shape_of((tokens, DT), BF16),
        shape_of((tokens, DL), BF16),
        shape_of((tokens, DT), BF16),
        shape_of((tokens, SLAB), BF16),
        shape_of((every, DT), BF16),
        shape_of((every, SLAB), BF16),
        shape_of((every, DT), BF16),
        shape_of((every, SLAB), BF16),
        shape_of((pairs, packs, 2 * rows, keys), BF16),
        shape_of((tokens, DT), BF16),
        shape_of((tokens, SLAB), BF16),
        shape_of((tokens, DT), BF16),
        shape_of((tokens, DT), F32),
        shape_of((tokens, 1), F32),
        shape_of((tokens, DT), F32),
        shape_of((tokens, FT), BF16),
        shape_of((tokens, DL), BF16),
        shape_of((tokens, DL), F32),
        shape_of((tokens, 1), F32),
        shape_of((tokens, DL), F32),
        shape_of((tokens, FL), BF16),
        shape_of((tokens, FL), BF16),
        shape_of((8, DT), F32),
        shape_of((8, DL), F32),
    ) + (shape_of((DT, DT), BF16),) * 4
    out_specs = [VMEM] * 4 + [ANY] * 5 + [VMEM] * 15 + [ANY] * 4
    scratch = [
        pltpu.VMEM((every, DT + SLAB), BF16),
        pltpu.VMEM(wt.shape, BF16),
        pltpu.VMEM(wl.shape, BF16),
        pltpu.VMEM(mt.shape, BF16),
        pltpu.VMEM(et.shape, BF16),
        pltpu.VMEM(st.shape, BF16),
        pltpu.VMEM((every, DT), BF16),
        pltpu.VMEM((every, SLAB), BF16),
        pltpu.VMEM((every, DT), BF16),
        pltpu.VMEM((every, SLAB), BF16),
        pltpu.VMEM((pairs, packs, 2 * rows, keys), BF16),
        pltpu.VMEM((packs, rows, keys), F32),
        pltpu.VMEM((tokens, FT), BF16),
        pltpu.VMEM((DT, tokens), BF16),
        pltpu.VMEM((tokens, DT), F32),
        pltpu.VMEM((tokens, DL), F32),
        pltpu.VMEM((4, DT, DT), BF16),
        pltpu.SemaphoreType.DMA((32,)),
    ]
    return pl.pallas_call(
        functools.partial(forward_kernel, packs, rows),
        out_shape=outs,
        in_specs=[SMEM] + [ANY] * 9 + [VMEM] * 11,
        out_specs=out_specs,
        scratch_shapes=scratch,
        compiler_params=pltpu.CompilerParams(vmem_limit_bytes=56 * MIB),
        name="forward",
    )(place, *blocks, wt, wl, mt, et, st, ml, el, sl, cot_t, cot_l, bt, gt, ot, bl, gl, ol)


E_ROWS = 896
P_ROWS = 896


def middle_kernel(
    place,
    hid_t,
    unit_t,
    inv_t,
    sum_t,
    slope_t,
    hid_l,
    unit_l,
    inv_l,
    sum_l,
    slope_l,
    act_l,
    st_in,
    et_in,
    mt_in,
    sl,
    el,
    ml,
    gt,
    gl,
    g0,
    g1,
    g2,
    g3,
    mid_t,
    mid_l,
    ad_t,
    ad_l,
    dctx_t,
    dctx_l,
    sv_t,
    sv_l,
    so_t,
    so_l,
    st,
    et,
    mt,
    before_t,
    before_l,
    hidden_t,
    hidden_l,
    turned,
    grads,
    sems,
):
    w_copies = copies_of(((st_in, st), (et_in, et), (mt_in, mt)), sems, 0)
    base = 3

    def feed_back(branch_delta, shrink, expand, slope, before, so, hidden_delta, chunk):
        width = slope.shape[1]
        for at in range(width // chunk):
            part = pl.ds(at * chunk, chunk)
            active_delta = dot_nt(branch_delta, shrink[part, :])
            low = (active_delta * slope[:, part].astype(F32)).astype(BF16)
            before[:, part] = low
            so[:, part] = column_sum(low.astype(F32))
            product = dot_nt(low, expand[:, part])
            if at == 0:
                hidden_delta[...] = product
            else:
                hidden_delta[...] += product

    def front(hidden_delta, total, unit, inv, g, merge, mid, ad, dctx, sv):
        delta = total[...] + hidden_delta[...]
        sv[0:1, :] = column_sum(delta * unit[...])
        sv[1:2, :] = column_sum(delta)
        middle = norm_back(delta * g, unit[...], inv[...])
        mid[...] = middle
        low = middle.astype(BF16)
        rounded = low.astype(F32)
        sv[2:3, :] = column_sum(rounded)
        ad[...] = rounded.T.astype(BF16)
        back = dot_nt(low, merge[...]).astype(BF16)
        dctx[...] = back
        sv[3:4, :] = column_sum(back.astype(F32)[:, : sv.shape[1]])

    s = place[0]
    text_delta = sum_t[...].astype(BF16)
    layout_delta = sum_l[...].astype(BF16)
    feed_back(layout_delta, sl, el, slope_l, before_l, so_l, hidden_l, 256)
    turned_l = before_l[...].astype(F32).T.astype(BF16)
    grown_l = dot(turned_l, hid_l[...]).astype(BF16)
    shrunk_l = dot(layout_delta.astype(F32).T.astype(BF16), act_l[...]).astype(BF16)
    for shard in range(4):
        for at in range(3):
            grads[shard, pl.ds(DT + 0, 64), pl.ds(at * SLAB, DL)] = grown_l[
                shard * DL + at * 64 : shard * DL + at * 64 + 64, :
            ]
        grads[shard, pl.ds(DT + 64, 48), :] = shrunk_l[shard * 48 : shard * 48 + 48, :]
    front(hidden_l, sum_l, unit_l, inv_l, gl[0:1, :].astype(F32), ml, mid_l, ad_l, dctx_l, sv_l)
    turned[...] = hid_t[...].astype(F32).T.astype(BF16)
    wait_all(w_copies)
    feed_back(text_delta, st, et, slope_t, before_t, so_t, hidden_t, 512)
    for shard in range(4):
        grads[shard, pl.ds(0, DT), :] = dot(
            turned[...], before_t[:, shard * DT : (shard + 1) * DT]
        ).astype(BF16)
    out_copies = copies_of(
        tuple(
            (grads.at[jnp.bitwise_xor(s, at)], target)
            for at, target in ((3, g3), (1, g1), (2, g2), (0, g0))
        ),
        sems,
        base,
    )
    front(hidden_t, sum_t, unit_t, inv_t, gt[0:1, :].astype(F32), mt, mid_t, ad_t, dctx_t, sv_t)
    wait_all(out_copies)


def middle_call(place, hid_t, unit_t, inv_t, sum_t, slope_t, hid_l, unit_l, inv_l, sum_l, slope_l, act_l, st, et, mt, sl, el, ml, gt, gl):
    tokens = hid_t.shape[0]
    outs = (shape_of((E_ROWS, DT), BF16),) * 4 + (
        shape_of((tokens, DT), F32),
        shape_of((tokens, DL), F32),
        shape_of((DT, tokens), BF16),
        shape_of((DL, tokens), BF16),
        shape_of((tokens, DT), BF16),
        shape_of((tokens, SLAB), BF16),
        shape_of((8, DT), F32),
        shape_of((8, DL), F32),
        shape_of((1, FT), F32),
        shape_of((1, FL), F32),
    )
    scratch = [
        pltpu.VMEM(st.shape, BF16),
        pltpu.VMEM(et.shape, BF16),
        pltpu.VMEM(mt.shape, BF16),
        pltpu.VMEM((tokens, FT), BF16),
        pltpu.VMEM((tokens, FL), BF16),
        pltpu.VMEM((tokens, DT), F32),
        pltpu.VMEM((tokens, DL), F32),
        pltpu.VMEM((DT, tokens), BF16),
        pltpu.VMEM((4, E_ROWS, DT), BF16),
        pltpu.SemaphoreType.DMA((8,)),
    ]
    return pl.pallas_call(
        middle_kernel,
        out_shape=outs,
        in_specs=[SMEM] + [VMEM] * 11 + [ANY] * 3 + [VMEM] * 5,
        out_specs=[ANY] * 4 + [VMEM] * 10,
        scratch_shapes=scratch,
        compiler_params=pltpu.CompilerParams(vmem_limit_bytes=48 * MIB),
        name="middle",
    )(place, hid_t, unit_t, inv_t, sum_t, slope_t, hid_l, unit_l, inv_l, sum_l, slope_l, act_l, st, et, mt, sl, el, ml, gt, gl)


def attention_kernel(
    packs,
    rows,
    place,
    x0,
    x1,
    x2,
    x3,
    kt_in,
    kl_in,
    vt_in,
    vl_in,
    p_in,
    q_t,
    q_l,
    dctx_t,
    dctx_l,
    ctx_t,
    ctx_l,
    ad_t,
    ad_l,
    sf_t,
    sf_l,
    sm_t,
    sm_l,
    so_t,
    so_l,
    g0,
    g1,
    g2,
    g3,
    joined_t,
    joined_l,
    query_t,
    query_l,
    xs,
    k_t,
    k_l,
    v_t,
    v_l,
    prob,
    dq_t,
    dq_l,
    dk_l,
    dv_l,
    text_grads,
    merge_grads,
    layout_grads,
    layout_merge,
    smalls,
    sems,
):
    blocks = (x0, x1, x2, x3)
    keys = rows * len(blocks)
    kv_copies = copies_of(((kt_in, k_t), (kl_in, k_l), (vt_in, v_t), (vl_in, v_l), (p_in, prob)), sems, 0)
    x_copies = copies_of(gather_pairs(blocks, rows, packs, xs), sems, 5)
    base = 5 + len(x_copies)
    dq_l[...] = jnp.zeros_like(dq_l)
    dk_l[...] = jnp.zeros_like(dk_l)
    dv_l[...] = jnp.zeros_like(dv_l)
    merge_grads[...] = dot(ad_t[...], ctx_t[...]).astype(BF16)
    layout_merge[...] = dot(ad_l[...], ctx_l[...]).astype(BF16)
    wait_all(kv_copies)

    def head_pair(pair_at, unused):
        masks = lane_masks(pair_at)
        text_lanes = pl.ds(pl.multiple_of(pair_at * LANES, LANES), LANES)
        layout_lanes = pl.ds(pl.multiple_of(pair_at // 4 * LANES, LANES), LANES)
        for pack in range(packs):
            mine = pl.ds(pack * rows, rows)
            span = pl.ds(pack * keys, keys)
            queries = stacked_heads(q_t[mine, text_lanes], q_l[mine, layout_lanes], masks)
            deltas = stacked_heads(dctx_t[mine, text_lanes], dctx_l[mine, layout_lanes], masks)
            one = jnp.concatenate([ctx_t[mine, text_lanes], ctx_l[mine, layout_lanes]], axis=1)
            contexts = jnp.concatenate([one, one], axis=0).astype(F32)
            products = deltas.astype(F32) * contexts
            layout_mean = jnp.sum(products[:, LANES:], axis=1, keepdims=True)
            both_mean = jnp.sum(products, axis=1, keepdims=True)
            text_values = v_t[span, text_lanes]
            layout_values = v_l[span, layout_lanes]
            both_values = jnp.concatenate([text_values, layout_values], axis=1)
            low = prob[pair_at, pack]
            chance = low.astype(F32)
            both_change = (chance * (dot_nt(deltas, both_values) - both_mean)).astype(BF16)
            layout_change = (
                chance * (dot_nt(deltas[:, LANES:], layout_values) - layout_mean)
            ).astype(BF16)
            from_text = dot(both_change, k_t[span, text_lanes])
            dq_t[mine, text_lanes] = (
                jnp.where(masks[0], from_text[:rows], from_text[rows:]) * 0.125
            ).astype(BF16)
            from_layout = dot(layout_change, k_l[span, layout_lanes]) * 0.25
            kept = dq_l[mine, layout_lanes]
            kept = jnp.where(masks[1], from_layout[:rows], kept)
            dq_l[mine, layout_lanes] = jnp.where(masks[2], from_layout[rows:], kept)
            turned_queries = queries.T
            turned_deltas = deltas.T
            joined_t[text_lanes, span] = dot(turned_queries[:LANES], both_change).astype(BF16)
            dk_l[layout_lanes, span] += dot(turned_queries[LANES:], layout_change)
            value_change = dot(turned_deltas, low)
            text_at = pl.ds(pl.multiple_of(pair_at * LANES + DT, LANES), LANES)
            joined_t[text_at, span] = value_change[:LANES].astype(BF16)
            dv_l[layout_lanes, span] += value_change[LANES:]
        return unused

    lax.fori_loop(0, HEADS // 2, head_pair, 0)
    joined_l[:SLAB, :] = dk_l[...].astype(BF16)
    joined_l[SLAB:, :] = dv_l[...].astype(BF16)
    whole_t = dq_t[...].astype(F32)
    whole_l = dq_l[...]
    low_l = whole_l.astype(BF16)
    query_t[...] = whole_t.T.astype(BF16)
    query_l[...] = whole_l.T.astype(BF16)
    wait_all(x_copies)
    own = jnp.concatenate([xs[pl.ds(pack * keys, rows), :] for pack in range(packs)], axis=0)
    text_grads[:DT, :] = dot(query_t[...], own[:, :DT]).astype(BF16)
    step = 256
    for at in range(2 * DT // step):
        text_grads[pl.ds(DT + at * step, step), :] = dot(
            joined_t[pl.ds(at * step, step), :], xs[:, :DT]
        ).astype(BF16)
    layout_grads[:DL, :] = dot(query_l[:DL, :], own[:, DT:]).astype(BF16)
    layout_grads[DL : 2 * DL, :] = dot(joined_l[:DL, :], xs[:, DT:]).astype(BF16)
    layout_grads[2 * DL :, :] = dot(joined_l[SLAB : SLAB + DL, :], xs[:, DT:]).astype(BF16)

    smalls[...] = jnp.zeros_like(smalls)
    text_lines = jnp.concatenate(
        [
            column_sum(whole_t),
            sm_t[3:4, :],
            sm_t[2:3, :],
            sm_t[1:2, :],
            sf_t[0:2, :],
            sm_t[0:1, :],
            sf_t[2:3, :],
            so_t[:, :DT],
            so_t[:, DT : 2 * DT],
            so_t[:, 2 * DT : 3 * DT],
            so_t[:, 3 * DT :],
            so_l[...],
            jnp.zeros((3, DT), F32),
        ],
        axis=0,
    )
    smalls[:16, :] = text_lines.astype(BF16)
    layout_lines = jnp.concatenate(
        [
            column_sum(low_l.astype(F32))[:, :DL],
            sm_l[3:4, :],
            sm_l[2:3, :],
            sm_l[1:2, :],
            sf_l[0:2, :],
            sm_l[0:1, :],
            sf_l[2:3, :],
            jnp.zeros((8, DL), F32),
        ],
        axis=0,
    )
    smalls[16:32, :DL] = layout_lines.astype(BF16)

    s = place[0]
    out_copies = []
    for at, target in ((3, g3), (1, g1), (2, g2), (0, g0)):
        shard = jnp.bitwise_xor(s, at)

        pairs = [
            (text_grads.at[pl.ds(pl.multiple_of(shard * 576, 64), 576), :], target.at[pl.ds(0, 576), :]),
            (merge_grads.at[pl.ds(pl.multiple_of(shard * 192, 64), 192), :], target.at[pl.ds(576, 192), :]),
            (smalls, target.at[pl.ds(832, 32), :]),
        ]
        for piece in range(3):
            lanes = pl.ds(piece * SLAB, SLAB)
            pairs.append(
                (
                    layout_grads.at[pl.ds(pl.multiple_of(shard * 144 + piece * 48, 16), 48), :],
                    target.at[pl.ds(768, 48), lanes],
                )
            )
            pairs.append(
                (
                    layout_merge.at[pl.ds(pl.multiple_of(shard * 48 + piece * 16, 16), 16), :],
                    target.at[pl.ds(816, 16), lanes],
                )
            )
        pairs.append((smalls, target.at[pl.ds(864, 32), :]))
        out_copies += copies_of(pairs, sems, base)
        base += len(pairs)
    wait_all(out_copies)


def attention_call(place, blocks, kt, kl, vt, vl, p, q_t, q_l, dctx_t, dctx_l, ctx_t, ctx_l, ad_t, ad_l, sf_t, sf_l, sm_t, sm_l, so_t, so_l, packs, rows):
    tokens = packs * rows
    every = tokens * len(blocks)
    outs = (shape_of((P_ROWS, DT), BF16),) * 4 + (
        shape_of((2 * DT, every), BF16),
        shape_of((2 * SLAB, every), BF16),
        shape_of((DT, tokens), BF16),
        shape_of((SLAB, tokens), BF16),
    )
    scratch = [
        pltpu.VMEM((every, DT + SLAB), BF16),
        pltpu.VMEM(kt.shape, BF16),
        pltpu.VMEM(kl.shape, BF16),
        pltpu.VMEM(vt.shape, BF16),
        pltpu.VMEM(vl.shape, BF16),
        pltpu.VMEM(p.shape, BF16),
        pltpu.VMEM((tokens, DT), BF16),
        pltpu.VMEM((tokens, SLAB), F32),
        pltpu.VMEM((SLAB, every), F32),
        pltpu.VMEM((SLAB, every), F32),
        pltpu.VMEM((3 * DT, DT), BF16),
        pltpu.VMEM((DT, DT), BF16),
        pltpu.VMEM((3 * DL, SLAB), BF16),
        pltpu.VMEM((DL, SLAB), BF16),
        pltpu.VMEM((32, DT), BF16),
        pltpu.SemaphoreType.DMA((64,)),
    ]
    return pl.pallas_call(
        functools.partial(attention_kernel, packs, rows),
        out_shape=outs,
        in_specs=[SMEM] + [ANY] * 9 + [VMEM] * 14,
        out_specs=[ANY] * 4 + [VMEM] * 4,
        scratch_shapes=scratch,
        compiler_params=pltpu.CompilerParams(vmem_limit_bytes=48 * MIB),
        name="attention_back",
    )(place, *blocks, kt, kl, vt, vl, p, q_t, q_l, dctx_t, dctx_l, ctx_t, ctx_l, ad_t, ad_l, sf_t, sf_l, sm_t, sm_l, so_t, so_l)


def input_kernel(packs, rows, joined_t, joined_l, query_t, query_l, wt, wl, g0, g1, g2, g3):
    keys = joined_t.shape[1] // packs
    for at, target in ((3, g3), (1, g1), (2, g2), (0, g0)):
        spans = [slice(pack * keys + at * rows, pack * keys + (at + 1) * rows) for pack in range(packs)]
        text_part = jnp.concatenate([joined_t[:, span] for span in spans], axis=1)
        layout_part = jnp.concatenate([joined_l[:, span] for span in spans], axis=1)
        text_sum = dot(wt[:, DT:], text_part)
        layout_sum = dot(wl[:DL, SLAB:], layout_part)
        if at == 0:
            text_sum += dot(wt[:, :DT], query_t[...])
            layout_sum += dot(wl[:DL, :SLAB], query_l[...])
        target[:DT, :] = text_sum.astype(target.dtype)
        target[DT:, :] = layout_sum.astype(target.dtype)


def input_call(joined_t, joined_l, query_t, query_l, wt, wl, packs, rows):
    tokens = packs * rows
    return pl.pallas_call(
        functools.partial(input_kernel, packs, rows),
        out_shape=(shape_of((DT + DL, tokens), F32),) + (shape_of((DT + DL, tokens), BF16),) * 3,
        in_specs=[VMEM] * 6,
        out_specs=[VMEM] * 4,
        compiler_params=pltpu.CompilerParams(vmem_limit_bytes=32 * MIB),
        name="input_back",
    )(joined_t, joined_l, query_t, query_l, wt, wl)


def sensitivity_kernel(own, near, far, mid_t, mid_l, out_t, out_l):
    total = own[...] + near[...].astype(F32) + far[...].astype(F32)
    out_t[...] = mid_t[...] + total[:DT, :].T
    out_l[...] = mid_l[...] + total[DT:, :].T


def sensitivity_call(own, near, far, mid_t, mid_l):
    return pl.pallas_call(
        sensitivity_kernel,
        out_shape=(shape_of(mid_t.shape, F32), shape_of(mid_l.shape, F32)),
        in_specs=[VMEM] * 5,
        out_specs=[VMEM] * 2,
        compiler_params=pltpu.CompilerParams(vmem_limit_bytes=16 * MIB),
        name="sensitivity",
    )(own, near, far, mid_t, mid_l)


def pieces_in_order(index, total, whole, pieces):
    size = total.shape[0] // pieces
    for at in range(pieces):
        mark = pl.multiple_of(jnp.bitwise_xor(index, at) * size, 16)
        whole[at * size : (at + 1) * size, :] = total[pl.ds(mark, size), :].astype(F32)


def shrink_kernel(pieces, index, total, out, whole):
    pieces_in_order(index[0], total, whole, pieces)
    share = DT // 4
    for block in range(FT // DT):
        out[block * DT : (block + 1) * DT, :] = whole[block * share : (block + 1) * share, :].T


def expand_kernel(pieces, index, total, out, out_grow, out_shrink, whole):
    pieces_in_order(index[0], total, whole, pieces)
    out[...] = whole[:DT, :]
    grown = jnp.concatenate(
        [whole[DT : DT + 64, at * SLAB : at * SLAB + DL] for at in range(3)], axis=0
    )
    out_grow[...] = grown.T
    out_shrink[...] = whole[DT + 64 : DT + 112, :].T


def project_kernel(pieces, index, total, out, out_merge, out_layout, out_layout_merge, out_small, whole):
    pieces_in_order(index[0], total, whole, pieces)
    out[...] = whole[:576, :].T
    out_merge[...] = whole[576:768, :].T
    layout = jnp.concatenate([whole[768:816, at * SLAB : at * SLAB + DL] for at in range(3)], axis=0)
    out_layout[...] = layout.T
    merge = jnp.concatenate([whole[816:832, at * SLAB : at * SLAB + DL] for at in range(3)], axis=0)
    out_layout_merge[...] = merge.T
    out_small[...] = whole[832:864, :]


def final_call(kernel, name, index, total, pieces, outs):
    return pl.pallas_call(
        functools.partial(kernel, pieces),
        out_shape=tuple(shape_of(shape, F32) for shape in outs),
        in_specs=[SMEM, VMEM],
        out_specs=[VMEM] * len(outs),
        scratch_shapes=[pltpu.VMEM(total.shape, F32)],
        compiler_params=pltpu.CompilerParams(vmem_limit_bytes=24 * MIB),
        name=name,
    )(index, total)


def partners(size, bit):
    return [(at, at ^ bit) for at in range(size)]


def low_sum(parts):
    total = parts[0].astype(F32)
    for part in parts[1:]:
        total = total + part.astype(F32)
    return total


def over_seq(shards, size):
    own, near, far, corner = shards
    from_corner = lax.ppermute(corner, "seq", partners(size, 1))
    from_near = lax.ppermute(near, "seq", partners(size, 1))
    onward = low_sum([far, from_corner]).astype(BF16)
    from_far = lax.ppermute(onward, "seq", partners(size, 2))
    return [own, from_near, from_far]


def padded_rows(shards, multiple):
    short = -shards[0].shape[0] % multiple
    if short:
        return [jnp.pad(shard, ((0, short), (0, 0))) for shard in shards]
    return list(shards)


def summed(shards, seq_size, dp_size, order):
    shards = padded_rows(shards, 16 * dp_size)
    parts = over_seq(shards, seq_size)
    device = lax.axis_index("dp")
    rows = shards[0].shape[0]
    index = 0
    for bit in order:
        mine = jnp.bitwise_and(device // bit, 1)
        half = rows // 2
        send = low_sum([lax.dynamic_slice_in_dim(part, (1 - mine) * half, half) for part in parts])
        keep = low_sum([lax.dynamic_slice_in_dim(part, mine * half, half) for part in parts])
        parts = [keep, lax.ppermute(send.astype(BF16), "dp", partners(dp_size, bit))]
        index = 2 * index + mine
        rows = half
    total = low_sum(parts).astype(BF16)
    for bit in reversed(order):
        total = jnp.concatenate([total, lax.ppermute(total, "dp", partners(dp_size, bit))], axis=0)
    return total, index.reshape(1).astype(jnp.int32)


def local(
    dp_size,
    seq_size,
    text_input,
    layout_input,
    segments,
    text_cotangent,
    layout_cotangent,
    text_project,
    text_biases,
    text_gains,
    text_merge,
    text_expand,
    text_offsets,
    text_shrink,
    layout_project,
    layout_biases,
    layout_gains,
    layout_merge,
    layout_expand,
    layout_offsets,
    layout_shrink,
):
    packs, rows, unused = text_input.shape
    tokens = packs * rows
    shard = lax.axis_index("seq")
    place = shard.reshape(1).astype(jnp.int32)
    marks = jnp.broadcast_to(segments.astype(BF16)[:, :, None], (packs, rows, SLAB - DL))
    own = jnp.concatenate([text_input, layout_input, marks], axis=2).reshape(tokens, DT + SLAB)
    far = lax.ppermute(own, "seq", partners(seq_size, 2))
    near = lax.ppermute(own, "seq", partners(seq_size, 1))
    corner = lax.ppermute(far, "seq", partners(seq_size, 1))
    blocks = (own, near, far, corner)

    pad = SLAB - DL
    wl = jnp.pad(layout_project.reshape(DL, 3, DL), ((0, pad), (0, 0), (0, pad))).reshape(SLAB, 3 * SLAB)
    bl = jnp.pad(layout_biases, ((0, 0), (0, pad)))
    ml = jnp.pad(layout_merge, ((0, pad), (0, 0)))
    (
        res_t, res_l, q_t, q_l, kt, kl, vt, vl, p, ctx_t, ctx_l,
        hid_t, unit_t, inv_t, sum_t, slope_t,
        hid_l, unit_l, inv_l, sum_l, slope_l, act_l, sf_t, sf_l,
        *shrink_parts,
    ) = forward_call(
        place, blocks, text_project, wl, text_merge, text_expand, text_shrink,
        ml, layout_expand, layout_shrink,
        text_cotangent.reshape(tokens, DT), layout_cotangent.reshape(tokens, DL),
        text_biases, text_gains, text_offsets.reshape(1, FT), bl, layout_gains, layout_offsets.reshape(1, FL),
        packs, rows,
    )
    order = [1 << at for at in range((dp_size - 1).bit_length())]
    shrink_total, shrink_index = summed(shrink_parts, seq_size, dp_size, order)
    *expand_parts, mid_t, mid_l, ad_t, ad_l, dctx_t, dctx_l, sm_t, sm_l, so_t, so_l = middle_call(
        place, hid_t, unit_t, inv_t, sum_t, slope_t, hid_l, unit_l, inv_l, sum_l, slope_l, act_l,
        text_shrink, text_expand, text_merge, layout_shrink, layout_expand, ml, text_gains, layout_gains,
    )
    expand_total, expand_index = summed(expand_parts, seq_size, dp_size, order)
    *project_parts, joined_t, joined_l, query_t, query_l = attention_call(
        place, blocks, kt, kl, vt, vl, p, q_t, q_l, dctx_t, dctx_l, ctx_t, ctx_l, ad_t, ad_l,
        sf_t, sf_l, sm_t, sm_l, so_t, so_l, packs, rows,
    )
    project_total, project_index = summed(project_parts, seq_size, dp_size, order)
    input_parts = input_call(joined_t, joined_l, query_t, query_l, text_project, wl, packs, rows)
    sens_t, sens_l = sensitivity_call(*over_seq(input_parts, seq_size), mid_t, mid_l)

    (shrink_t,) = final_call(shrink_kernel, "shrink_out", shrink_index, shrink_total, dp_size, [(FT, DT // 4)])
    expand_t, expand_l, shrink_l = final_call(
        expand_kernel, "expand_out", expand_index, expand_total, dp_size, [(DT, DT), (DL, DL), (FL, DL // 4)]
    )
    project_t, merge_t, project_l, merge_l, small = final_call(
        project_kernel, "project_out", project_index, project_total, dp_size,
        [(DT, 576), (DT, 192), (DL, 144), (DL, 48), (32, DT)],
    )
    text_small = lax.dynamic_slice_in_dim(small[:8], shard * (DT // 4), DT // 4, 1)
    layout_small = lax.dynamic_slice_in_dim(small[16:24, :DL], shard * (DL // 4), DL // 4, 1)
    offsets_t = lax.dynamic_slice_in_dim(small[8:12], shard, 1, 0).reshape(DT)
    offsets_l = lax.dynamic_slice_in_dim(small[12:13].reshape(FL), shard * (FL // 4), FL // 4, 0)
    return (
        res_t.reshape(packs, rows, DT),
        res_l.reshape(packs, rows, DL),
        sens_t.reshape(packs, rows, DT),
        sens_l.reshape(packs, rows, DL),
        project_t,
        text_small[:6],
        text_small[6:8],
        merge_t,
        expand_t,
        offsets_t,
        shrink_t,
        project_l,
        layout_small[:6],
        layout_small[6:8],
        merge_l,
        expand_l,
        offsets_l,
        shrink_l,
    )


def solution(mesh):
    rows = P("dp", "seq", None)
    columns = P(None, "seq")
    in_specs = (rows, rows, P("dp", "seq"), rows, rows) + (P(),) * 14
    out_specs = (
        (rows,) * 4 + (columns,) * 5 + (P("seq"),) + (columns,) * 6 + (P("seq"),) + (columns,)
    )
    body = functools.partial(local, mesh.shape["dp"], mesh.shape["seq"])
    return jax.shard_map(body, mesh=mesh, in_specs=in_specs, out_specs=out_specs, check_vma=False)
```

```python
import functools

import jax
import jax.numpy as jnp
from jax import lax
from jax.experimental import pallas as pl
from jax.experimental.pallas import tpu as pltpu
from jax.sharding import PartitionSpec as P

HEADS = 12
EPSILON = 1e-05
MASKED = -1000000000.0
F32 = jnp.float32
BF16 = jnp.bfloat16
DT = 768
DL = 192
FT = 3072
FL = 768
LANES = 128
SLAB = 256
S_ROWS = 768
E_ROWS = 1152
P_ROWS = 640
MIB = 1024 * 1024

VMEM = pl.BlockSpec(memory_space=pltpu.VMEM)
ANY = pl.BlockSpec(memory_space=pl.ANY)


def dot(left, right):
    return jnp.dot(left, right, preferred_element_type=F32)


def dot_nt(left, right):
    return lax.dot_general(left, right, (((1,), (1,)), ((), ())), preferred_element_type=F32)


LIMIT = 60 * MIB
FIRST = 60 * MIB
SMALL = 16 * MIB


COST = pl.CostEstimate(flops=1, bytes_accessed=1, transcendentals=0)


def shape_of(shape, dtype):
    return jax.ShapeDtypeStruct(shape, dtype)


def copies_of(pairs, sems, base):
    made = []
    for at, (source, target) in enumerate(pairs):
        copy = pltpu.make_async_copy(source, target, sems.at[base + at])
        copy.start()
        made.append(copy)
    return made


def wait_all(made):
    for copy in made:
        copy.wait()


def gather_pairs(blocks, rows, packs, target):
    span = rows * len(blocks)
    return [
        (block.at[pack], target.at[pl.ds(pack * span + at * rows, rows), :])
        for at, block in enumerate(blocks)
        for pack in range(packs)
    ]


def in_lines(shards, subs, dp_size, targets):
    place = (lax.axis_index("seq"), lax.axis_index("dp"))
    pairs = []
    for core in (1, 0):
        for at, (first, rows, hops, growth) in enumerate(subs):
            size = rows // dp_size
            target = targets[2 * at + 1 - core]
            for across in range(2):
                shard = jnp.bitwise_xor(place[0], core + 2 * across)
                for other in range(dp_size):
                    piece = jnp.bitwise_xor(place[1], other)
                    mark = pl.multiple_of(first + piece * size, 16)
                    line = position(hops, across, other) * size
                    pairs.append(
                        (shards.at[shard, pl.ds(mark, size), :], target.at[pl.ds(line, size), :])
                    )
    return pairs


def position(hops, across, other):
    at = 0
    for group in hops:
        index = 0
        for n, (axis, bit) in enumerate(group):
            if across if axis == "seq" else other & bit:
                index += 1 << n
        at = (at << len(group)) + index
    return at


def sub_chunks(rows, split, dp_size):
    step = 16 * dp_size
    total = (rows + step - 1) // step * step
    subs = []
    first = 0
    for at, (share, hops, growth) in enumerate(split):
        size = total - first if at == len(split) - 1 else (share + step - 1) // step * step
        subs.append((first, size, hops, growth))
        first += size
    return tuple(subs)


def total_lines(subs):
    return sum(rows for first, rows, hops, growth in subs)


def pair_shapes(subs):
    return tuple(shape_of((2 * rows, DT), BF16) for first, rows, hops, growth in subs for unused in range(2))


def lane_masks(pair_at):
    lanes = lax.broadcasted_iota(jnp.int32, (1, LANES), 1)
    low_half = lanes < 64
    group_of_16 = lax.shift_right_logical(lanes, 4)
    first = group_of_16 == 2 * lax.rem(pair_at, 4)
    second = group_of_16 == 2 * lax.rem(pair_at, 4) + 1
    return (low_half, first, second)


def stacked_heads(text_rows, layout_rows, masks):
    low_half, first, second = masks
    zero_text = jnp.zeros_like(text_rows)
    zero_layout = jnp.zeros_like(layout_rows)
    top = jnp.concatenate(
        [jnp.where(low_half, text_rows, zero_text), jnp.where(first, layout_rows, zero_layout)],
        axis=1,
    )
    bottom = jnp.concatenate(
        [jnp.where(low_half, zero_text, text_rows), jnp.where(second, layout_rows, zero_layout)],
        axis=1,
    )
    return jnp.concatenate([top, bottom], axis=0)


def normalized(values):
    centre = values - jnp.mean(values, axis=-1, keepdims=True)
    spread = jnp.mean(centre * centre, axis=-1, keepdims=True)
    inverse = lax.rsqrt(spread + EPSILON)
    return (centre * inverse, inverse)


def norm_back(delta, unit, inverse):
    return inverse * (
        delta
        - jnp.mean(delta, axis=-1, keepdims=True)
        - unit * jnp.mean(delta * unit, axis=-1, keepdims=True)
    )


def column_sum(values):
    return jnp.sum(values, axis=0, keepdims=True)


def feed_forward(hidden_low, expand, offsets, shrink, turned, active, slope, chunk, branch_ref):
    width = expand.shape[1]
    for at in range(width // chunk):
        part = pl.ds(at * chunk, chunk)
        before = dot(hidden_low, expand[:, part]) + offsets[:, part].astype(F32)
        share = 0.5 + 0.5 * lax.erf(before * (0.5**0.5))
        density = jnp.exp(-0.5 * (before * before)) * 0.3989422804014327
        active_part = (before * share).astype(BF16)
        active[:, part] = active_part
        slope[:, part] = (share + before * density).astype(BF16)
        product = dot_nt(active_part, shrink[:, part]) if turned else dot(active_part, shrink[part, :])
        if at == 0:
            branch_ref[...] = product
        else:
            branch_ref[...] += product


def prepare_kernel(text_rows, layout_rows, segments, project, offsets_t, offsets_l, joined, padded, line_t, line_l):
    packs, width, rows = layout_rows.shape
    for pack in range(packs):
        marks = jnp.broadcast_to(segments[pack : pack + 1, :].astype(F32), (SLAB - width, rows))
        lines = jnp.concatenate([layout_rows[pack].astype(F32), marks], axis=0)
        joined[pack, :, :DT] = text_rows[pack]
        joined[pack, :, DT:] = lines.T.astype(BF16)
    line_t[...] = offsets_t[...].reshape(line_t.shape)
    line_l[...] = offsets_l[...].reshape(line_l.shape)
    padded[...] = jnp.zeros_like(padded)
    for third in range(3):
        padded[:, third * SLAB : third * SLAB + DL] = project[:, third * DL : (third + 1) * DL]


def prepare_call(text_rows, layout_rows, segments, project, offsets_t, offsets_l):
    packs, rows, unused = text_rows.shape
    return pl.pallas_call(
        prepare_kernel,
        out_shape=(
            shape_of((packs, rows, DT + SLAB), BF16),
            shape_of((DL, 3 * SLAB), BF16),
            shape_of((1, FT), BF16),
            shape_of((1, FL), BF16),
        ),
        in_specs=[VMEM] * 6,
        out_specs=[VMEM] * 4,
        compiler_params=pltpu.CompilerParams(vmem_limit_bytes=LIMIT),
        cost_estimate=COST,
        name="prepare",
    )(text_rows, layout_rows, segments, project, offsets_t, offsets_l)


def forward_kernel(
    packs,
    rows,
    dp_size,
    subs,
    x0,
    x1,
    x2,
    x3,
    wt_in,
    wl_in,
    mt_in,
    et_in,
    st_in,
    ml,
    el,
    sl,
    cot_t,
    cot_l,
    bt,
    gt,
    ot,
    bl,
    gl,
    ol,
    res_t,
    res_l,
    q_t,
    q_l,
    kt_out,
    kl_out,
    vt_out,
    vl_out,
    p_out,
    ctx_t,
    ctx_l,
    hid_t,
    unit_t,
    inv_t,
    sum_t,
    slope_t,
    hid_l,
    unit_l,
    inv_l,
    sum_l,
    slope_l,
    act_l,
    sv_t,
    sv_l,
    *rest,
):
    targets, rest = rest[: 2 * len(subs)], rest[2 * len(subs) :]
    (
        xs,
        layout_bias_ref,
        wt,
        wl,
        mt,
        et,
        st,
        k_t,
        k_l,
        v_t,
        v_l,
        prob,
        bias,
        act_t,
        turned,
        branch_t,
        branch_l,
        grads,
        sems,
    ) = rest
    blocks = (x0, x1, x2, x3)
    keys = rows * len(blocks)
    tokens = packs * rows
    x_copies = copies_of(
        gather_pairs(blocks, rows, packs, xs), sems, 0
    )
    base = len(x_copies)
    w_copies = copies_of(((wt_in, wt), (wl_in, wl), (mt_in, mt), (et_in, et), (st_in, st)), sems, base)
    base += 5
    text_bias = bt[...].astype(F32)
    layout_bias_ref[...] = jnp.zeros_like(layout_bias_ref)
    layout_bias_ref[:, :DL] = bl[...].astype(F32)
    layout_bias = layout_bias_ref[...]
    wait_all(x_copies)
    wait_all(w_copies[:2])

    for pack in range(packs):
        own = pl.ds(pack * keys, rows)
        mine = pl.ds(pack * rows, rows)
        q_t[mine, :] = (dot(xs[own, :DT], wt[:, :DT]) + text_bias[0:1, :]).astype(BF16) * 0.125
        q_l[mine, :] = (dot(xs[own, DT : DT + DL], wl[:, :SLAB]) + layout_bias[0:1, :]).astype(BF16) * 0.25

    step = 256

    def key_rows(at, unused):
        span = pl.ds(pl.multiple_of(at * step, step), step)
        k_t[span, :] = dot(xs[span, :DT], wt[:, DT : 2 * DT]).astype(BF16)
        v_t[span, :] = (dot(xs[span, :DT], wt[:, 2 * DT :]) + text_bias[1:2, :]).astype(BF16)
        k_l[span, :] = dot(xs[span, DT : DT + DL], wl[:, SLAB : 2 * SLAB]).astype(BF16)
        v_l[span, :] = (dot(xs[span, DT : DT + DL], wl[:, 2 * SLAB :]) + layout_bias[1:2, :]).astype(BF16)
        return unused

    lax.fori_loop(0, packs * keys // step, key_rows, 0)
    kv_copies = copies_of(((k_t, kt_out), (k_l, kl_out), (v_t, vt_out), (v_l, vl_out)), sems, base)
    base += 4

    marks = lax.broadcasted_iota(jnp.int32, (1, LANES), 1) - 64
    for pack in range(packs):
        slab = xs[pl.ds(pack * keys, keys), DT + LANES : DT + 2 * LANES].astype(F32)
        hot = jnp.where((slab == marks.astype(F32)) & (marks >= 0) & (marks < 16), 1.0, 0.0).astype(BF16)
        same = dot_nt(hot[:rows], hot)
        bias[pack] = jnp.where(same > 0.5, 0.0, MASKED)

    ctx_l[...] = jnp.zeros_like(ctx_l)

    def head_pair(pair_at, unused):
        masks = lane_masks(pair_at)
        text_lanes = pl.ds(pl.multiple_of(pair_at * LANES, LANES), LANES)
        layout_lanes = pl.ds(pl.multiple_of(pair_at // 4 * LANES, LANES), LANES)
        for pack in range(packs):
            mine = pl.ds(pack * rows, rows)
            span = pl.ds(pack * keys, keys)
            queries = stacked_heads(q_t[mine, text_lanes], q_l[mine, layout_lanes], masks)
            both_keys = jnp.concatenate([k_t[span, text_lanes], k_l[span, layout_lanes]], axis=1)
            both_values = jnp.concatenate([v_t[span, text_lanes], v_l[span, layout_lanes]], axis=1)
            allowed = bias[pack]
            logit = dot_nt(queries, both_keys) + jnp.concatenate([allowed, allowed], axis=0)
            raised = jnp.exp(logit - jnp.max(logit, axis=1, keepdims=True))
            low = (raised * (1.0 / jnp.sum(raised, axis=1, keepdims=True))).astype(BF16)
            prob[pair_at, pack] = low
            mixed = dot(low, both_values).astype(BF16)
            ctx_t[mine, text_lanes] = jnp.where(masks[0], mixed[:rows, :LANES], mixed[rows:, :LANES])
            kept = ctx_l[mine, layout_lanes]
            kept = jnp.where(masks[1], mixed[:rows, LANES:], kept)
            ctx_l[mine, layout_lanes] = jnp.where(masks[2], mixed[rows:, LANES:], kept)
        return unused

    lax.fori_loop(0, HEADS // 2, head_pair, 0)
    p_copies = copies_of(((prob, p_out),), sems, base)
    base += 1

    wait_all(w_copies[2:])

    def own_rows(lanes):
        return jnp.concatenate(
            [xs[pl.ds(pack * keys, rows), lanes].astype(F32) for pack in range(packs)], axis=0
        )

    def tail(x, attended, expand, offsets, shrink, turned, b, g, cotangent, active, slope, branch, chunk, hid, unit, inv, delta, sv):
        width = x.shape[1]
        middle = x + attended + b[2:3, :width]
        unit_first, inverse_first = normalized(middle)
        hidden = unit_first * g[0:1, :] + b[3:4, :width]
        hidden_low = hidden.astype(BF16)
        hid[...] = hidden_low
        unit[...] = unit_first
        inv[...] = inverse_first
        feed_forward(hidden_low, expand, offsets, shrink, turned, active, slope, chunk, branch)
        unit_second, inverse_second = normalized(hidden + branch[...] + b[4:5, :width])
        result = unit_second * g[1:2, :] + b[5:6, :width]
        sv[1:2, :] = column_sum(cotangent)
        sv[2:3, :] = column_sum(cotangent * unit_second)
        sum_delta = norm_back(cotangent * g[1:2, :], unit_second, inverse_second)
        delta[...] = sum_delta
        rounded = sum_delta.astype(BF16).astype(F32)
        sv[0:1, :] = column_sum(rounded)
        return result, rounded

    result, rounded = tail(
        own_rows(slice(0, DT)), dot(ctx_t[...], mt[...]), et, ot, st, False, text_bias, gt[...].astype(F32),
        jnp.concatenate([cot_t[pack] for pack in range(packs)], axis=0).astype(F32),
        act_t, slope_t, branch_t, 512, hid_t, unit_t, inv_t, sum_t, sv_t,
    )
    res_t[...] = result.astype(BF16)
    turned[...] = rounded.T.astype(BF16)
    share = DT // 4
    for shard in range(4):
        own = turned[shard * share : (shard + 1) * share, :]
        for block in range(FT // DT):
            grads[shard, pl.ds(block * share, share), :] = dot(
                own, act_t[:, block * DT : (block + 1) * DT]
            ).astype(BF16)
    if grads.shape[1] > S_ROWS:
        grads[:, S_ROWS:, :] = jnp.zeros((4, grads.shape[1] - S_ROWS, DT), BF16)
    out_copies = copies_of(
        in_lines(grads, subs, dp_size, targets), sems, base
    )
    result, unused = tail(
        own_rows(slice(DT, DT + DL)), dot(ctx_l[:, :DL], ml[...]), el, ol, sl, True, layout_bias,
        gl[...].astype(F32),
        jnp.concatenate([cot_l[pack].astype(F32).T for pack in range(packs)], axis=0),
        act_l, slope_l, branch_l, 256, hid_l, unit_l, inv_l, sum_l, sv_l,
    )
    for pack in range(packs):
        res_l[pack] = result[pack * rows : (pack + 1) * rows, :].T.astype(BF16)
    wait_all(kv_copies)
    wait_all(p_copies)
    wait_all(out_copies)


def forward_call(blocks, wt, wl, mt, et, st, ml, el, sl, cot_t, cot_l, bt, gt, ot, bl, gl, ol, packs, rows, dp_size, subs):
    tokens = packs * rows
    lines = total_lines(subs)
    every = tokens * len(blocks)
    keys = rows * len(blocks)
    pairs = HEADS // 2
    outs = (
        shape_of((tokens, DT), BF16),
        shape_of((packs, DL, rows), BF16),
        shape_of((tokens, DT), BF16),
        shape_of((tokens, SLAB), BF16),
        shape_of((every, DT), BF16),
        shape_of((every, SLAB), BF16),
        shape_of((every, DT), BF16),
        shape_of((every, SLAB), BF16),
        shape_of((pairs, packs, 2 * rows, keys), BF16),
        shape_of((tokens, DT), BF16),
        shape_of((tokens, SLAB), BF16),
        shape_of((tokens, DT), BF16),
        shape_of((tokens, DT), F32),
        shape_of((tokens, 1), F32),
        shape_of((tokens, DT), F32),
        shape_of((tokens, FT), BF16),
        shape_of((tokens, DL), BF16),
        shape_of((tokens, DL), F32),
        shape_of((tokens, 1), F32),
        shape_of((tokens, DL), F32),
        shape_of((tokens, FL), BF16),
        shape_of((tokens, FL), BF16),
        shape_of((8, DT), F32),
        shape_of((8, DL), F32),
    ) + pair_shapes(subs)
    out_specs = [VMEM] * 4 + [ANY] * 5 + [VMEM] * 15 + [ANY] * (2 * len(subs))
    scratch = [
        pltpu.VMEM((every, DT + SLAB), BF16),
        pltpu.VMEM((6, SLAB), F32),
        pltpu.VMEM(wt.shape, BF16),
        pltpu.VMEM(wl.shape, BF16),
        pltpu.VMEM(mt.shape, BF16),
        pltpu.VMEM(et.shape, BF16),
        pltpu.VMEM(st.shape, BF16),
        pltpu.VMEM((every, DT), BF16),
        pltpu.VMEM((every, SLAB), BF16),
        pltpu.VMEM((every, DT), BF16),
        pltpu.VMEM((every, SLAB), BF16),
        pltpu.VMEM((pairs, packs, 2 * rows, keys), BF16),
        pltpu.VMEM((packs, rows, keys), F32),
        pltpu.VMEM((tokens, FT), BF16),
        pltpu.VMEM((DT, tokens), BF16),
        pltpu.VMEM((tokens, DT), F32),
        pltpu.VMEM((tokens, DL), F32),
        pltpu.VMEM((4, lines, DT), BF16),
        pltpu.SemaphoreType.DMA((24 + 4 * dp_size * len(subs),)),
    ]
    return pl.pallas_call(
        functools.partial(forward_kernel, packs, rows, dp_size, subs),
        out_shape=outs,
        in_specs=[ANY] * 9 + [VMEM] * 11,
        out_specs=out_specs,
        scratch_shapes=scratch,
        compiler_params=pltpu.CompilerParams(vmem_limit_bytes=FIRST),
        cost_estimate=COST,
        name="forward",
    )(*blocks, wt, wl, mt, et, st, ml, el, sl, cot_t, cot_l, bt, gt, ot, bl, gl, ol)


def middle_kernel(
    dp_size,
    subs,
    hid_t,
    unit_t,
    inv_t,
    sum_t,
    slope_t,
    hid_l,
    unit_l,
    inv_l,
    sum_l,
    slope_l,
    act_l,
    ctx_t,
    ctx_l,
    st_in,
    et_in,
    mt_in,
    sl,
    el,
    ml,
    gt,
    gl,
    after,
    mid_t,
    mid_l,
    dctx_t,
    dctx_l,
    sv_t,
    sv_l,
    so_t,
    so_l,
    *rest,
):
    targets, rest = rest[: 2 * len(subs)], rest[2 * len(subs) :]
    (
        st,
        et,
        mt,
        before_t,
        before_l,
        hidden_t,
        hidden_l,
        turned,
        grads,
        sems,
    ) = rest
    w_copies = copies_of(((st_in, st), (et_in, et), (mt_in, mt)), sems, 0)
    base = 3

    def feed_back(branch_delta, shrink, turned, expand, slope, before, so, hidden_delta, chunk):
        width = slope.shape[1]
        for at in range(width // chunk):
            part = pl.ds(at * chunk, chunk)
            if turned:
                active_delta = dot(branch_delta, shrink[:, part])
            else:
                active_delta = dot_nt(branch_delta, shrink[part, :])
            low = (active_delta * slope[:, part].astype(F32)).astype(BF16)
            before[:, part] = low
            so[:, part] = column_sum(low.astype(F32))
            product = dot_nt(low, expand[:, part])
            if at == 0:
                hidden_delta[...] = product
            else:
                hidden_delta[...] += product

    def front(hidden_delta, total, unit, inv, g, merge, sv):
        delta = total[...] + hidden_delta[...]
        sv[0:1, :] = column_sum(delta * unit[...])
        sv[1:2, :] = column_sum(delta)
        middle = norm_back(delta * g, unit[...], inv[...])
        low = middle.astype(BF16)
        rounded = low.astype(F32)
        sv[2:3, :] = column_sum(rounded)
        back = dot_nt(low, merge).astype(BF16)
        sv[3:4, :] = column_sum(back.astype(F32))
        return middle, rounded.T.astype(BF16), back

    text_delta = sum_t[...].astype(BF16)
    layout_delta = sum_l[...].astype(BF16)
    feed_back(layout_delta, sl, True, el, slope_l, before_l, so_l, hidden_l, 256)
    turned_l = before_l[...].astype(F32).T.astype(BF16)
    grown_l = dot(turned_l, hid_l[...]).astype(BF16)
    shrunk_l = dot(layout_delta.astype(F32).T.astype(BF16), act_l[...]).astype(BF16)
    middle, low_turned, back = front(
        hidden_l, sum_l, unit_l, inv_l, gl[0:1, :].astype(F32), ml[...], sv_l
    )
    for pack in range(mid_l.shape[0]):
        size = mid_l.shape[2]
        mid_l[pack] = middle[pack * size : (pack + 1) * size, :].T
    dctx_l[...] = jnp.zeros_like(dctx_l)
    dctx_l[:, :DL] = back
    merged_l = dot(low_turned, ctx_l[...]).astype(BF16)
    turned[...] = hid_t[...].astype(F32).T.astype(BF16)
    wait_all(w_copies)
    feed_back(text_delta, st, False, et, slope_t, before_t, so_t, hidden_t, 512)
    middle, low_turned, back = front(
        hidden_t, sum_t, unit_t, inv_t, gt[0:1, :].astype(F32), mt[...], sv_t
    )
    mid_t[...] = middle
    dctx_t[...] = back
    for shard in range(4):
        grads[shard, pl.ds(0, DT), :] = dot(
            turned[...], before_t[:, shard * DT : (shard + 1) * DT]
        ).astype(BF16)
        grads[shard, pl.ds(DT, 192), :] = dot(
            low_turned[shard * 192 : (shard + 1) * 192, :], ctx_t[...]
        ).astype(BF16)
    for shard in range(4):
        grads[shard, 960:, :] = jnp.zeros((grads.shape[1] - 960, DT), BF16)
        for at in range(3):
            lanes = slice(at * SLAB, at * SLAB + DL)
            line = shard * DL + at * 64
            grads[shard, 960:1024, lanes] = grown_l[line : line + 64, :]
            line = shard * 48 + at * 16
            grads[shard, 1072:1088, at * SLAB : (at + 1) * SLAB] = merged_l[line : line + 16, :]
        grads[shard, 1024:1072, :] = shrunk_l[shard * 48 : shard * 48 + 48, :]
    wait_all(
        copies_of(in_lines(grads, subs, dp_size, targets), sems, base)
    )


def middle_call(operands, packs, rows, dp_size, subs):
    tokens = packs * rows
    lines = total_lines(subs)
    outs = (
        shape_of((tokens, DT), F32),
        shape_of((packs, DL, rows), F32),
        shape_of((tokens, DT), BF16),
        shape_of((tokens, SLAB), BF16),
        shape_of((8, DT), F32),
        shape_of((8, DL), F32),
        shape_of((1, FT), F32),
        shape_of((1, FL), F32),
    ) + pair_shapes(subs)
    scratch = [
        pltpu.VMEM((FT, DT), BF16),
        pltpu.VMEM((DT, FT), BF16),
        pltpu.VMEM((DT, DT), BF16),
        pltpu.VMEM((tokens, FT), BF16),
        pltpu.VMEM((tokens, FL), BF16),
        pltpu.VMEM((tokens, DT), F32),
        pltpu.VMEM((tokens, DL), F32),
        pltpu.VMEM((DT, tokens), BF16),
        pltpu.VMEM((4, lines, DT), BF16),
        pltpu.SemaphoreType.DMA((8 + 4 * dp_size * len(subs),)),
    ]
    return pl.pallas_call(
        functools.partial(middle_kernel, dp_size, subs),
        out_shape=outs,
        in_specs=[VMEM] * 13 + [ANY] * 3 + [VMEM] * 5 + [ANY],
        out_specs=[VMEM] * 8 + [ANY] * (2 * len(subs)),
        scratch_shapes=scratch,
        compiler_params=pltpu.CompilerParams(vmem_limit_bytes=LIMIT),
        cost_estimate=COST,
        name="middle",
    )(*operands)


def attention_kernel(
    packs,
    rows,
    dp_size,
    subs,
    x0,
    x1,
    x2,
    x3,
    kt_in,
    kl_in,
    vt_in,
    vl_in,
    p_in,
    q_t,
    q_l,
    dctx_t,
    dctx_l,
    ctx_t,
    ctx_l,
    sf_t,
    sf_l,
    sm_t,
    sm_l,
    so_t,
    so_l,
    after,
    joined_t,
    joined_l,
    query_t,
    query_l,
    *rest,
):
    targets, rest = rest[: 2 * len(subs)], rest[2 * len(subs) :]
    (
        xs,
        k_t,
        k_l,
        v_t,
        v_l,
        prob,
        dq_t,
        dq_l,
        dk_l,
        dv_l,
        layout_grads,
        grads,
        smalls,
        sems,
    ) = rest
    blocks = (x0, x1, x2, x3)
    keys = rows * len(blocks)
    kv_copies = copies_of(((kt_in, k_t), (kl_in, k_l), (vt_in, v_t), (vl_in, v_l), (p_in, prob)), sems, 0)
    x_copies = copies_of(
        gather_pairs(blocks, rows, packs, xs), sems, 5
    )
    base = 5 + len(x_copies)
    dq_l[...] = jnp.zeros_like(dq_l)
    dk_l[...] = jnp.zeros_like(dk_l)
    dv_l[...] = jnp.zeros_like(dv_l)
    wait_all(kv_copies)

    def head_pair(pair_at, unused):
        masks = lane_masks(pair_at)
        text_lanes = pl.ds(pl.multiple_of(pair_at * LANES, LANES), LANES)
        layout_lanes = pl.ds(pl.multiple_of(pair_at // 4 * LANES, LANES), LANES)
        for pack in range(packs):
            mine = pl.ds(pack * rows, rows)
            span = pl.ds(pack * keys, keys)
            queries = stacked_heads(q_t[mine, text_lanes], q_l[mine, layout_lanes], masks)
            deltas = stacked_heads(dctx_t[mine, text_lanes], dctx_l[mine, layout_lanes], masks)
            one = jnp.concatenate([ctx_t[mine, text_lanes], ctx_l[mine, layout_lanes]], axis=1)
            contexts = jnp.concatenate([one, one], axis=0).astype(F32)
            products = deltas.astype(F32) * contexts
            layout_mean = jnp.sum(products[:, LANES:], axis=1, keepdims=True)
            both_mean = jnp.sum(products, axis=1, keepdims=True)
            text_values = v_t[span, text_lanes]
            layout_values = v_l[span, layout_lanes]
            both_values = jnp.concatenate([text_values, layout_values], axis=1)
            low = prob[pair_at, pack]
            chance = low.astype(F32)
            both_change = (chance * (dot_nt(deltas, both_values) - both_mean)).astype(BF16)
            layout_change = (
                chance * (dot_nt(deltas[:, LANES:], layout_values) - layout_mean)
            ).astype(BF16)
            from_text = dot(both_change, k_t[span, text_lanes])
            dq_t[mine, text_lanes] = (
                jnp.where(masks[0], from_text[:rows], from_text[rows:]) * 0.125
            ).astype(BF16)
            from_layout = dot(layout_change, k_l[span, layout_lanes]) * 0.25
            kept = dq_l[mine, layout_lanes]
            kept = jnp.where(masks[1], from_layout[:rows], kept)
            dq_l[mine, layout_lanes] = jnp.where(masks[2], from_layout[rows:], kept)
            turned_queries = queries.T
            turned_deltas = deltas.T
            joined_t[text_lanes, span] = dot(turned_queries[:LANES], both_change).astype(BF16)
            dk_l[layout_lanes, span] += dot(turned_queries[LANES:], layout_change)
            value_change = dot(turned_deltas, low)
            text_at = pl.ds(pl.multiple_of(pair_at * LANES + DT, LANES), LANES)
            joined_t[text_at, span] = value_change[:LANES].astype(BF16)
            dv_l[layout_lanes, span] += value_change[LANES:]
        return unused

    lax.fori_loop(0, HEADS // 2, head_pair, 0)
    joined_l[:SLAB, :] = dk_l[...].astype(BF16)
    joined_l[SLAB:, :] = dv_l[...].astype(BF16)
    whole_t = dq_t[...].astype(F32)
    whole_l = dq_l[...]
    low_l = whole_l.astype(BF16)
    query_t[...] = whole_t.T.astype(BF16)
    query_l[...] = whole_l.T.astype(BF16)
    wait_all(x_copies)
    own = jnp.concatenate([xs[pl.ds(pack * keys, rows), :] for pack in range(packs)], axis=0)
    step = 192
    for at in range(3 * DT // step):
        shard, line = at // 3, at % 3 * step
        if at < DT // step:
            product = dot(query_t[at * step : (at + 1) * step, :], own[:, :DT])
        else:
            product = dot(joined_t[at * step - DT : (at + 1) * step - DT, :], xs[:, :DT])
        grads[shard, line : line + step, :] = product.astype(BF16)
    layout_grads[:DL, :] = dot(query_l[:DL, :], own[:, DT:]).astype(BF16)
    layout_grads[DL : 2 * DL, :] = dot(joined_l[:DL, :], xs[:, DT:]).astype(BF16)
    layout_grads[2 * DL :, :] = dot(joined_l[SLAB : SLAB + DL, :], xs[:, DT:]).astype(BF16)
    text_lines = jnp.concatenate(
        [column_sum(whole_t), sm_t[3:4, :], sm_t[2:3, :], sm_t[1:2, :], sf_t[0:2, :], sm_t[0:1, :], sf_t[2:3, :]],
        axis=0,
    )
    layout_lines = jnp.concatenate(
        [
            column_sum(low_l.astype(F32))[:, :DL],
            sm_l[3:4, :], sm_l[2:3, :], sm_l[1:2, :], sf_l[0:2, :], sm_l[0:1, :], sf_l[2:3, :],
        ],
        axis=0,
    )
    for shard in range(4):
        for at in range(3):
            line = shard * 144 + at * 48
            grads[shard, 576:624, at * SLAB : (at + 1) * SLAB] = layout_grads[line : line + 48, :]
        smalls[...] = jnp.zeros_like(smalls)
        share = DT // 4
        smalls[0:8, 0:share] = text_lines[:, shard * share : (shard + 1) * share]
        smalls[8:9, :] = so_t[:, shard * DT : (shard + 1) * DT]
        share = DL // 4
        smalls[0:8, SLAB : SLAB + share] = layout_lines[:, shard * share : (shard + 1) * share]
        share = FL // 4
        smalls[9:10, 0:share] = so_l[:, shard * share : (shard + 1) * share]
        grads[shard, 624:640, :] = smalls[...].astype(BF16)
        if grads.shape[1] > P_ROWS:
            grads[shard, P_ROWS:, :] = jnp.zeros((grads.shape[1] - P_ROWS, DT), BF16)
    wait_all(copies_of(in_lines(grads, subs, dp_size, targets), sems, base))


def attention_call(operands, packs, rows, dp_size, subs):
    tokens = packs * rows
    every = tokens * 4
    lines = total_lines(subs)
    pairs = HEADS // 2
    outs = (
        shape_of((2 * DT, every), BF16),
        shape_of((2 * SLAB, every), BF16),
        shape_of((DT, tokens), BF16),
        shape_of((SLAB, tokens), BF16),
    ) + pair_shapes(subs)
    scratch = [
        pltpu.VMEM((every, DT + SLAB), BF16),
        pltpu.VMEM((every, DT), BF16),
        pltpu.VMEM((every, SLAB), BF16),
        pltpu.VMEM((every, DT), BF16),
        pltpu.VMEM((every, SLAB), BF16),
        pltpu.VMEM((pairs, packs, 2 * rows, 4 * rows), BF16),
        pltpu.VMEM((tokens, DT), BF16),
        pltpu.VMEM((tokens, SLAB), F32),
        pltpu.VMEM((SLAB, every), F32),
        pltpu.VMEM((SLAB, every), F32),
        pltpu.VMEM((3 * DL, SLAB), BF16),
        pltpu.VMEM((4, lines, DT), BF16),
        pltpu.VMEM((16, DT), F32),
        pltpu.SemaphoreType.DMA((24 + 4 * dp_size * len(subs),)),
    ]
    return pl.pallas_call(
        functools.partial(attention_kernel, packs, rows, dp_size, subs),
        out_shape=outs,
        in_specs=[ANY] * 9 + [VMEM] * 12 + [ANY],
        out_specs=[VMEM] * 4 + [ANY] * (2 * len(subs)),
        scratch_shapes=scratch,
        compiler_params=pltpu.CompilerParams(vmem_limit_bytes=LIMIT),
        cost_estimate=COST,
        name="attention_back",
    )(*operands)


def input_kernel(packs, rows, joined_t, joined_l, query_t, query_l, wt, wl, after, give, hold):
    keys = joined_t.shape[1] // packs
    for at in (3, 1, 2, 0):
        target = (hold, give)[at % 2].at[at // 2]
        spans = [slice(pack * keys + at * rows, pack * keys + (at + 1) * rows) for pack in range(packs)]
        text_part = jnp.concatenate([joined_t[:, span] for span in spans], axis=1)
        layout_part = jnp.concatenate([joined_l[:, span] for span in spans], axis=1)
        text_sum = dot(wt[:, DT:], text_part)
        layout_sum = dot(wl[:, SLAB:], layout_part)
        if at == 0:
            text_sum += dot(wt[:, :DT], query_t[...])
            layout_sum += dot(wl[:, :SLAB], query_l[...])
        target[:DT, :] = text_sum.astype(target.dtype)
        target[DT:, :] = layout_sum.astype(target.dtype)


def input_call(joined_t, joined_l, query_t, query_l, wt, wl, after, packs, rows):
    tokens = packs * rows
    return pl.pallas_call(
        functools.partial(input_kernel, packs, rows),
        out_shape=(shape_of((2, DT + DL, tokens), BF16),) * 2,
        in_specs=[VMEM] * 6 + [ANY],
        out_specs=[VMEM] * 2,
        compiler_params=pltpu.CompilerParams(vmem_limit_bytes=LIMIT),
        cost_estimate=COST,
        name="input_back",
    )(joined_t, joined_l, query_t, query_l, wt, wl, after)


def sensitivity_kernel(own, far, mid_t, mid_l, after, out_t, out_l):
    total = own[...].astype(F32) + far[...].astype(F32)
    out_t[...] = mid_t[...] + total[:DT, :].T
    packs, unused, rows = mid_l.shape
    for pack in range(packs):
        out_l[pack] = mid_l[pack] + total[DT:, pack * rows : (pack + 1) * rows]


def sensitivity_call(own, far, mid_t, mid_l, after):
    return pl.pallas_call(
        sensitivity_kernel,
        out_shape=(shape_of(mid_t.shape, F32), shape_of(mid_l.shape, F32)),
        in_specs=[VMEM] * 4 + [ANY],
        out_specs=[VMEM] * 2,
        compiler_params=pltpu.CompilerParams(vmem_limit_bytes=SMALL),
        cost_estimate=COST,
        name="sensitivity",
    )(own, far, mid_t, mid_l, after)


def lines_in_order(dp_size, sources, subs, whole):
    device = lax.axis_index("dp")
    for at, (first, rows, hops, growth) in enumerate(subs):
        half, other = sources[2 * at : 2 * at + 2]
        size = rows // dp_size
        for index in range(dp_size):
            line = position(growth[::-1], 0, index) * size
            source = half if line < rows // 2 else other
            line = line % (rows // 2)
            mark = pl.multiple_of(first + jnp.bitwise_xor(device, index) * size, 16)
            whole[pl.ds(mark, size), :] = source[line : line + size, :].astype(F32)


def shrink_store(whole, out):
    share = DT // 4
    for block in range(FT // DT):
        out[:, block * DT : (block + 1) * DT] = whole[block * share : (block + 1) * share, :]


def expand_store(whole, out, out_merge, out_grow, out_shrink, out_layout_merge):
    out[...] = whole[:DT, :]
    out_merge[...] = whole[DT:960, :]
    grown = jnp.concatenate(
        [whole[960:1024, at * SLAB : at * SLAB + DL] for at in range(3)], axis=0
    )
    out_grow[...] = grown.T
    out_shrink[...] = whole[1024:1072, :]
    out_layout_merge[...] = jnp.concatenate(
        [whole[1072:1088, at * SLAB : at * SLAB + DL] for at in range(3)], axis=0
    )


def project_store(whole, out, out_layout, biases_t, gains_t, offsets_t, biases_l, gains_l, offsets_l):
    out[...] = whole[:576, :]
    out_layout[...] = jnp.concatenate(
        [whole[576:624, at * SLAB : at * SLAB + DL] for at in range(3)], axis=0
    )
    biases_t[...] = whole[624:630, : DT // 4]
    gains_t[...] = whole[630:632, : DT // 4]
    offsets_t[...] = whole[632:633, :].reshape(DT)
    biases_l[...] = whole[624:630, SLAB : SLAB + DL // 4]
    gains_l[...] = whole[630:632, SLAB : SLAB + DL // 4]
    offsets_l[...] = whole[633:634, : FL // 4].reshape(FL // 4)


def final_kernel(store, dp_size, subs, *refs):
    sources, outs, whole = refs[: 2 * len(subs)], refs[2 * len(subs) + 1 : -1], refs[-1]
    lines_in_order(dp_size, sources, subs, whole)
    store(whole, *outs)


def final_call(store, name, sources, after, dp_size, subs, outs):
    return pl.pallas_call(
        functools.partial(final_kernel, store, dp_size, subs),
        out_shape=tuple(shape_of(shape, F32) for shape in outs),
        in_specs=[VMEM] * len(sources) + [ANY],
        out_specs=[VMEM] * len(outs),
        scratch_shapes=[pltpu.VMEM((total_lines(subs), DT), F32)],
        compiler_params=pltpu.CompilerParams(vmem_limit_bytes=SMALL),
        cost_estimate=COST,
        name=name,
    )(*sources, after)


def add_kernel(count, parts, *refs):
    sources, targets = refs[: count * parts], refs[count * parts + 1 :]
    for at, target in enumerate(targets):
        total = sources[at][...].astype(F32)
        for n in range(1, count):
            total += sources[n * parts + at][...].astype(F32)
        target[...] = total.astype(BF16)


def add_call(sources, parts, after):
    lines, width = sources[0].shape
    size = lines // parts
    steps = max(n for n in (1, 2, 3, 4) if size % (16 * n) == 0 and (n == 1 or lines // n >= 256))
    block = size // steps
    specs = [
        pl.BlockSpec((block, width), functools.partial(lambda at, i: (at * steps + i, 0), at))
        for unused in sources
        for at in range(parts)
    ]
    return pl.pallas_call(
        functools.partial(add_kernel, len(sources), parts),
        grid=(steps,),
        out_shape=(shape_of((size, width), BF16),) * parts,
        in_specs=specs + [ANY],
        out_specs=[pl.BlockSpec((block, width), lambda i: (i, 0))] * parts,
        compiler_params=pltpu.CompilerParams(vmem_limit_bytes=SMALL),
        cost_estimate=COST,
        name="add",
    )(*[source for source in sources for unused in range(parts)], after)


def gate_call(arrays, after):
    count = len(arrays)
    return pl.pallas_call(
        lambda *refs: None,
        out_shape=tuple(shape_of(array.shape, array.dtype) for array in arrays),
        in_specs=[ANY] * (count + 1),
        out_specs=[ANY] * count,
        input_output_aliases={at: at for at in range(count)},
        compiler_params=pltpu.CompilerParams(vmem_limit_bytes=SMALL),
        cost_estimate=COST,
        name="gate",
    )(*arrays, after)


def join_kernel(count, *refs):
    sources, target = refs[:count], refs[-1]
    size = sources[0].shape[0]
    for at, source in enumerate(sources):
        target[at * size : (at + 1) * size, :] = source[...]


def join_call(sources, after):
    lines, width = sources[0].shape
    return pl.pallas_call(
        functools.partial(join_kernel, len(sources)),
        out_shape=shape_of((len(sources) * lines, width), BF16),
        in_specs=[VMEM] * len(sources) + [ANY],
        out_specs=VMEM,
        compiler_params=pltpu.CompilerParams(vmem_limit_bytes=SMALL),
        cost_estimate=COST,
        name="join",
    )(*sources, after)


def sent(array, group, index, seq_size, dp_size):
    across = other = 0
    for n, (axis, bit) in enumerate(group):
        if index & (1 << n):
            if axis == "seq":
                across |= bit
            else:
                other |= bit
    if not other:
        return lax.ppermute(array, "seq", [(at, at ^ across) for at in range(seq_size)])
    if not across:
        return lax.ppermute(array, "dp", [(at, at ^ other) for at in range(dp_size)])
    pairs = [
        (d * seq_size + s, (d ^ other) * seq_size + (s ^ across))
        for d in range(dp_size)
        for s in range(seq_size)
    ]
    return lax.ppermute(array, ("dp", "seq"), pairs)


def steps_of(give, hold, hops, growth, send):
    parts = [hold, send(give, (("seq", 1),), 1)]
    for group in hops:
        keep, *sends = yield functools.partial(add_call, parts, 1 << len(group))
        parts = [keep] + [send(array, group, at + 1) for at, array in enumerate(sends)]
    (piece,) = yield functools.partial(add_call, parts, 1)
    gathered = [piece]
    for group in growth:
        if len(gathered) > 1:
            piece = yield functools.partial(join_call, gathered)
        gathered = [piece] + [send(piece, group, at) for at in range(1, 1 << len(group))]
    return gathered


X = ("dp", 1)
Y = ("seq", 2)
Z1 = ("dp", 2)
Z2 = ("dp", 4)


def hops_of(text, extra):
    groups = {"x": (X,), "y": (Y,), "1": (Z1,), "2": (Z2,), "d": (Y, X), "z": (Z1, Z2)}
    return tuple(groups[letter] for letter in text) + extra


SPLIT_S = ((768, "y1x2B"), )
SPLIT_E = ((640, "1xy2B"), (512, "xyzB"), )
SPLIT_P = ((256, "xy12B"), (384, "yxzB"), )
ORDER = "B S0 GE E1 E0 C E1 S0 E0 GP D E1 P0 S0 E0 P1 GX E1 X0 E0 E1 S0 P0 E0 FX E1 S0 P0 E0 P0 P1 S0 P0 E0 P1 P0 S0 P0 P1 FE P1 P1 FS FP"


def local(
    dp_size,
    seq_size,
    text_input,
    layout_input,
    segments,
    text_cotangent,
    layout_cotangent,
    text_project,
    text_biases,
    text_gains,
    text_merge,
    text_expand,
    text_offsets,
    text_shrink,
    layout_project,
    layout_biases,
    layout_gains,
    layout_merge,
    layout_expand,
    layout_offsets,
    layout_shrink,
):
    packs, rows, unused = text_input.shape

    def send(array, group, index):
        return sent(array, group, index, seq_size, dp_size)

    core = (("seq", 1),)
    own, wl, line_t, line_l = prepare_call(
        text_input, layout_input.transpose(0, 2, 1), segments, layout_project, text_offsets, layout_offsets
    )
    far, near = send(own, (Y,), 1), send(own, core, 1)
    blocks = (own, near, far, send(far, core, 1))
    turned_shrink = layout_shrink.T

    bits = [1 << at for at in range((dp_size - 1).bit_length())]
    extra = tuple((("dp", bit),) for bit in bits[3:])
    growths = {
        "B": tuple(reversed(extra)) + ((Z2,), (Z1,), (X,)),
        "D": tuple(reversed(extra)) + ((Z1, Z2), (X,)),
    }
    subs = {
        name: sub_chunks(count, [(share, hops_of(text[:-1], extra), growths[text[-1]]) for share, text in split], dp_size)
        for name, count, split in (
            ("S", S_ROWS, SPLIT_S),
            ("E", E_ROWS, SPLIT_E),
            ("P", P_ROWS, SPLIT_P),
        )
    }
    reductions = {}
    calls = {}
    halves = {}
    values = {}
    token = None

    def begin(name, pairs):
        for at, (first, count, hops, growth) in enumerate(subs[name]):
            steps = steps_of(pairs[2 * at], pairs[2 * at + 1], hops, growth, send)
            reductions[name + str(at)] = steps
            calls[name + str(at)] = next(steps)

    def forward(after):
        (
            res_t, res_l, q_t, q_l, kt, kl, vt, vl, p, ctx_t, ctx_l,
            hid_t, unit_t, inv_t, sum_t, slope_t,
            hid_l, unit_l, inv_l, sum_l, slope_l, act_l, sf_t, sf_l,
            *pairs,
        ) = forward_call(
            blocks, text_project, wl, text_merge, text_expand, text_shrink,
            layout_merge, layout_expand, turned_shrink,
            text_cotangent, layout_cotangent.transpose(0, 2, 1),
            text_biases, text_gains, line_t, layout_biases, layout_gains,
            line_l, packs, rows, dp_size, subs["S"],
        )
        begin("S", pairs)
        values.update(
            results=(res_t, res_l),
            tail=(
                hid_t, unit_t, inv_t, sum_t, slope_t, hid_l, unit_l, inv_l, sum_l, slope_l, act_l,
                ctx_t, ctx_l,
            ),
            attended=(kt, kl, vt, vl, p, q_t, q_l),
            contexts=(ctx_t, ctx_l),
            first_sums=(sf_t, sf_l),
        )
        return sf_t

    def middle(after):
        mid_t, mid_l, dctx_t, dctx_l, sm_t, sm_l, so_t, so_l, *pairs = middle_call(
            (
                *values["tail"], text_shrink, text_expand, text_merge, turned_shrink,
                layout_expand, layout_merge, text_gains, layout_gains, after,
            ),
            packs, rows, dp_size, subs["E"],
        )
        values["E pairs"] = pairs
        values.update(
            middles=(mid_t, mid_l), deltas=(dctx_t, dctx_l), second_sums=(sm_t, sm_l, so_t, so_l)
        )
        return sm_t

    def attention(after):
        joined_t, joined_l, query_t, query_l, *pairs = attention_call(
            (
                *blocks, *values["attended"], *values["deltas"],
                *values["contexts"], *values["first_sums"], *values["second_sums"], after,
            ),
            packs, rows, dp_size, subs["P"],
        )
        values["P pairs"] = pairs
        values.update(joined=(joined_t, joined_l, query_t, query_l))
        return query_l

    def inputs(after):
        give, hold = input_call(*values["joined"], text_project, wl, after, packs, rows)
        values["X pairs"] = [give, hold]
        return hold

    def inputs_gate(after):
        give, hold = gate_call(values["X pairs"], after)
        lines = 2 * (DT + DL)
        values.update(inputs=[hold.reshape(lines, -1), send(give, core, 1).reshape(lines, -1)])
        return hold

    def gate(name):
        def call(after):
            pairs = gate_call(values[name + " pairs"], after)
            begin(name, pairs)
            return pairs[1]

        return call

    def inputs_add(after):
        own, onward = add_call(values["inputs"], 2, after)
        values.update(onward=(own, send(onward, (Y,), 1)))
        return own

    def inputs_end(after):
        values.update(sens=sensitivity_call(*values["onward"], *values["middles"], after))
        return values["sens"][1]

    def end(name, store, label, outs):
        def call(after):
            sources = [array for at in range(len(subs[name])) for array in halves[name + str(at)]]
            values[name] = final_call(
                store, label, sources, after, dp_size, subs[name], outs
            )
            return values[name][-1]

        return call

    kernels = {
        "A": forward,
        "B": middle,
        "C": attention,
        "D": inputs,
        "GE": gate("E"),
        "GP": gate("P"),
        "GX": inputs_gate,
        "X0": inputs_add,
        "FX": inputs_end,
        "FS": end("S", shrink_store, "shrink_out", [(DT // 4, FT)]),
        "FE": end(
            "E", expand_store, "expand_out",
            [(DT, DT), (DT // 4, DT), (DL, DL), (DL // 4, FL), (DL // 4, DL)],
        ),
        "FP": end(
            "P", project_store, "project_out",
            [
                (576, DT), (144, DL), (6, DT // 4), (2, DT // 4), (DT,),
                (6, DL // 4), (2, DL // 4), (FL // 4,),
            ],
        ),
    }

    def advance(name, after):
        outs = calls[name](after)
        try:
            calls[name] = reductions[name].send(outs)
        except StopIteration as stop:
            halves[name] = stop.value
            del calls[name]
        return outs[0] if isinstance(outs, (tuple, list)) else outs

    def finish(name, after):
        for at in range(len(subs[name])):
            while name + str(at) in calls:
                after = advance(name + str(at), after)
        return after

    token = forward(None)
    for label in ORDER.split():
        if label in kernels:
            if label[0] == "F" and label[1] in subs:
                token = finish(label[1], token)
            token = kernels[label](token)
        elif label in calls:
            token = advance(label, token)

    res_t, res_l = values["results"]
    sens_t, sens_l = values["sens"]
    (shrink_t,) = values["S"]
    expand_t, merge_t, expand_l, shrink_l, merge_l = values["E"]
    project_t, project_l, biases_t, gains_t, offsets_t, biases_l, gains_l, offsets_l = values["P"]
    return (
        res_t.reshape(packs, rows, DT),
        res_l.transpose(0, 2, 1),
        sens_t.reshape(packs, rows, DT),
        sens_l.transpose(0, 2, 1),
        project_t.T,
        biases_t,
        gains_t,
        merge_t.T,
        expand_t,
        offsets_t,
        shrink_t.T,
        project_l.T,
        biases_l,
        gains_l,
        merge_l.T,
        expand_l,
        offsets_l,
        shrink_l.T,
    )


def solution(mesh):
    rows = P("dp", "seq", None)
    columns = P(None, "seq")
    in_specs = (rows, rows, P("dp", "seq"), rows, rows) + (P(),) * 14
    out_specs = (
        (rows,) * 4 + (columns,) * 5 + (P("seq"),) + (columns,) * 6 + (P("seq"),) + (columns,)
    )
    body = functools.partial(local, mesh.shape["dp"], mesh.shape["seq"])
    return jax.shard_map(body, mesh=mesh, in_specs=in_specs, out_specs=out_specs, check_vma=False)
```

```python
import functools

import jax
import jax.numpy as jnp
from jax import lax
from jax.experimental import pallas as pl
from jax.experimental.pallas import tpu as pltpu
from jax.sharding import PartitionSpec as P

HEADS = 12
EPSILON = 1e-05
MASKED = -1000000000.0
F32 = jnp.float32
BF16 = jnp.bfloat16
DT = 768
DL = 192
FT = 3072
FL = 768
LANES = 128
SLAB = 256
S_ROWS = 768
E_ROWS = 1152
P_ROWS = 640
MIB = 1024 * 1024

VMEM = pl.BlockSpec(memory_space=pltpu.VMEM)
ANY = pl.BlockSpec(memory_space=pl.ANY)
HBM = pl.BlockSpec(memory_space=pltpu.HBM)


def dot(left, right):
    return jnp.dot(left, right, preferred_element_type=F32)


def dot_nt(left, right):
    return lax.dot_general(left, right, (((1,), (1,)), ((), ())), preferred_element_type=F32)


LIMIT = 60 * MIB
FIRST = 60 * MIB
SECOND = 60 * MIB
LAST = 30 * MIB
SMALL = 16 * MIB
UNROLL = 6
UNROLL_BACK = 1


COST = pl.CostEstimate(flops=1, bytes_accessed=1, transcendentals=0)


def shape_of(shape, dtype):
    return jax.ShapeDtypeStruct(shape, dtype)


def copies_of(pairs, sems, base):
    made = []
    for at, (source, target) in enumerate(pairs):
        copy = pltpu.make_async_copy(source, target, sems.at[base + at])
        copy.start()
        made.append(copy)
    return made


def wait_all(made):
    for copy in made:
        copy.wait()


def gather_pairs(blocks, rows, packs, target):
    span = rows * len(blocks)
    return [
        (block.at[pack], target.at[pl.ds(pack * span + at * rows, rows), :])
        for at, block in enumerate(blocks)
        for pack in range(packs)
    ]


def in_lines(shards, subs, dp_size, targets, low=0, high=1 << 30):
    place = (lax.axis_index("seq"), lax.axis_index("dp"))
    pairs = []
    for core in (1, 0):
        for at, (first, rows, hops, growth) in enumerate(subs):
            if not low < first + rows <= high:
                continue
            size = rows // dp_size
            target = targets[2 * at + 1 - core]
            for across in range(2):
                shard = jnp.bitwise_xor(place[0], core + 2 * across)
                for other in range(dp_size):
                    piece = jnp.bitwise_xor(place[1], other)
                    mark = pl.multiple_of(first + piece * size, 16)
                    line = position(hops, across, other) * size
                    pairs.append(
                        (shards.at[shard, pl.ds(mark, size), :], target.at[pl.ds(line, size), :])
                    )
    return pairs


def position(hops, across, other):
    at = 0
    for group in hops:
        index = 0
        for n, (axis, bit) in enumerate(group):
            if across if axis == "seq" else other & bit:
                index += 1 << n
        at = (at << len(group)) + index
    return at


def sub_chunks(rows, split, dp_size):
    step = 16 * dp_size
    total = (rows + step - 1) // step * step
    subs = []
    first = 0
    for at, (share, hops, growth) in enumerate(split):
        size = total - first if at == len(split) - 1 else (share + step - 1) // step * step
        subs.append((first, size, hops, growth))
        first += size
    return tuple(subs)


def total_lines(subs):
    return sum(rows for first, rows, hops, growth in subs)


def pair_shapes(subs):
    return tuple(shape_of((2 * rows, DT), BF16) for first, rows, hops, growth in subs for unused in range(2))


def lane_masks(pair_at):
    lanes = lax.broadcasted_iota(jnp.int32, (1, LANES), 1)
    low_half = lanes < 64
    group_of_16 = lax.shift_right_logical(lanes, 4)
    first = group_of_16 == 2 * lax.rem(pair_at, 4)
    second = group_of_16 == 2 * lax.rem(pair_at, 4) + 1
    return (low_half, first, second)


def stacked_heads(text_rows, layout_rows, masks):
    low_half, first, second = masks
    zero_text = jnp.zeros_like(text_rows)
    zero_layout = jnp.zeros_like(layout_rows)
    top = jnp.concatenate(
        [jnp.where(low_half, text_rows, zero_text), jnp.where(first, layout_rows, zero_layout)],
        axis=1,
    )
    bottom = jnp.concatenate(
        [jnp.where(low_half, zero_text, text_rows), jnp.where(second, layout_rows, zero_layout)],
        axis=1,
    )
    return jnp.concatenate([top, bottom], axis=0)


def normalized(values):
    centre = values - jnp.mean(values, axis=-1, keepdims=True)
    spread = jnp.mean(centre * centre, axis=-1, keepdims=True)
    inverse = lax.rsqrt(spread + EPSILON)
    return (centre * inverse, inverse)


def norm_back(delta, unit, inverse):
    return inverse * (
        delta
        - jnp.mean(delta, axis=-1, keepdims=True)
        - unit * jnp.mean(delta * unit, axis=-1, keepdims=True)
    )


def column_sum(values):
    return jnp.sum(values, axis=0, keepdims=True)


def feed_forward(hidden_low, expand, offsets, shrink, turned, active, slope, chunk, branch_ref):
    width = expand.shape[1]
    for at in range(width // chunk):
        part = pl.ds(at * chunk, chunk)
        before = dot(hidden_low, expand[:, part]) + offsets[:, part].astype(F32)
        share = 0.5 + 0.5 * lax.erf(before * (0.5**0.5))
        density = jnp.exp(-0.5 * (before * before)) * 0.3989422804014327
        active_part = (before * share).astype(BF16)
        active[:, part] = active_part
        slope[:, part] = (share + before * density).astype(BF16)
        product = dot_nt(active_part, shrink[:, part]) if turned else dot(active_part, shrink[part, :])
        if at == 0:
            branch_ref[...] = product
        else:
            branch_ref[...] += product


def prepare_kernel(text_rows, layout_rows, segments, project, offsets_t, offsets_l, joined, padded, line_t, line_l):
    packs, width, rows = layout_rows.shape
    for pack in range(packs):
        marks = jnp.broadcast_to(segments[pack : pack + 1, :].astype(F32), (SLAB - width, rows))
        lines = jnp.concatenate([layout_rows[pack].astype(F32), marks], axis=0)
        joined[pack, :, :DT] = text_rows[pack]
        joined[pack, :, DT:] = lines.T.astype(BF16)
    line_t[...] = offsets_t[...].reshape(line_t.shape)
    line_l[...] = offsets_l[...].reshape(line_l.shape)
    padded[...] = jnp.zeros_like(padded)
    for third in range(3):
        padded[:, third * SLAB : third * SLAB + DL] = project[:, third * DL : (third + 1) * DL]


def prepare_call(text_rows, layout_rows, segments, project, offsets_t, offsets_l):
    packs, rows, unused = text_rows.shape
    return pl.pallas_call(
        prepare_kernel,
        out_shape=(
            shape_of((packs, rows, DT + SLAB), BF16),
            shape_of((DL, 3 * SLAB), BF16),
            shape_of((1, FT), BF16),
            shape_of((1, FL), BF16),
        ),
        in_specs=[VMEM] * 6,
        out_specs=[VMEM] * 4,
        compiler_params=pltpu.CompilerParams(vmem_limit_bytes=LIMIT),
        cost_estimate=COST,
        name="prepare",
    )(text_rows, layout_rows, segments, project, offsets_t, offsets_l)


def forward_kernel(
    packs,
    rows,
    dp_size,
    subs,
    x0,
    x1,
    x2,
    x3,
    wt_in,
    wl_in,
    mt_in,
    et_in,
    st_in,
    ml,
    el,
    sl,
    cot_t,
    cot_l,
    bt,
    gt,
    ot,
    bl,
    gl,
    ol,
    res_t_out,
    res_l_out,
    q_t_out,
    q_l_out,
    kt_out,
    kl_out,
    vt_out,
    vl_out,
    p_out,
    ctx_t_out,
    ctx_l_out,
    hid_t_out,
    unit_t_out,
    inv_t_out,
    sum_t_out,
    slope_t_out,
    hid_l_out,
    unit_l_out,
    inv_l_out,
    sum_l_out,
    slope_l_out,
    act_l_out,
    sv_t_out,
    sv_l_out,
    *rest,
):
    targets, rest = rest[: 2 * len(subs)], rest[2 * len(subs) :]
    (
        xs,
        res_t,
        res_l,
        q_t,
        q_l,
        ctx_t,
        ctx_l,
        hid_t,
        unit_t,
        inv_t,
        sum_t,
        slope_t,
        hid_l,
        unit_l,
        inv_l,
        sum_l,
        slope_l,
        act_l,
        sv_t,
        sv_l,
        layout_bias_ref,
        wt,
        wl,
        mt,
        et,
        st,
        k_t,
        k_l,
        v_t,
        v_l,
        prob,
        bias,
        act_t,
        turned,
        branch_t,
        branch_l,
        grads,
        sems,
    ) = rest
    blocks = (x0, x1, x2, x3)
    keys = rows * len(blocks)
    tokens = packs * rows
    x_copies = copies_of(
        gather_pairs(blocks, rows, packs, xs), sems, 0
    )
    base = len(x_copies)
    w_copies = copies_of(((wt_in, wt), (wl_in, wl)), sems, base)
    base += 2
    pending = []

    def emit(*pairs):
        pending.extend(copies_of(pairs, sems, base + len(pending)))

    text_bias = bt[...].astype(F32)
    layout_bias_ref[...] = jnp.zeros_like(layout_bias_ref)
    layout_bias_ref[:, :DL] = bl[...].astype(F32)
    layout_bias = layout_bias_ref[...]
    wait_all(x_copies)
    wait_all(w_copies)
    w_copies = copies_of(((mt_in, mt), (et_in, et), (st_in, st)), sems, base)
    base += 3

    for pack in range(packs):
        own = pl.ds(pack * keys, rows)
        mine = pl.ds(pack * rows, rows)
        q_t[mine, :] = (dot(xs[own, :DT], wt[:, :DT]) + text_bias[0:1, :]).astype(BF16) * 0.125
        q_l[mine, :] = (dot(xs[own, DT : DT + DL], wl[:, :SLAB]) + layout_bias[0:1, :]).astype(BF16) * 0.25

    step = 256

    def key_rows(at, unused):
        span = pl.ds(pl.multiple_of(at * step, step), step)
        k_t[span, :] = dot(xs[span, :DT], wt[:, DT : 2 * DT]).astype(BF16)
        v_t[span, :] = (dot(xs[span, :DT], wt[:, 2 * DT :]) + text_bias[1:2, :]).astype(BF16)
        k_l[span, :] = dot(xs[span, DT : DT + DL], wl[:, SLAB : 2 * SLAB]).astype(BF16)
        v_l[span, :] = (dot(xs[span, DT : DT + DL], wl[:, 2 * SLAB :]) + layout_bias[1:2, :]).astype(BF16)
        return unused

    lax.fori_loop(0, packs * keys // step, key_rows, 0)
    emit((k_t, kt_out), (k_l, kl_out), (v_t, vt_out), (v_l, vl_out), (q_t, q_t_out), (q_l, q_l_out))

    marks = lax.broadcasted_iota(jnp.int32, (1, LANES), 1) - 64
    for pack in range(packs):
        slab = xs[pl.ds(pack * keys, keys), DT + LANES : DT + 2 * LANES].astype(F32)
        hot = jnp.where((slab == marks.astype(F32)) & (marks >= 0) & (marks < 16), 1.0, 0.0).astype(BF16)
        same = dot_nt(hot[:rows], hot)
        bias[pack] = jnp.where(same > 0.5, 0.0, MASKED)

    ctx_l[...] = jnp.zeros_like(ctx_l)

    def head_pair(pair_at, unused):
        masks = lane_masks(pair_at)
        text_lanes = pl.ds(pl.multiple_of(pair_at * LANES, LANES), LANES)
        layout_lanes = pl.ds(pl.multiple_of(pair_at // 4 * LANES, LANES), LANES)
        for pack in range(packs):
            mine = pl.ds(pack * rows, rows)
            span = pl.ds(pack * keys, keys)
            queries = stacked_heads(q_t[mine, text_lanes], q_l[mine, layout_lanes], masks)
            both_keys = jnp.concatenate([k_t[span, text_lanes], k_l[span, layout_lanes]], axis=1)
            both_values = jnp.concatenate([v_t[span, text_lanes], v_l[span, layout_lanes]], axis=1)
            allowed = bias[pack]
            logit = dot_nt(queries, both_keys) + jnp.concatenate([allowed, allowed], axis=0)
            raised = jnp.exp(logit - jnp.max(logit, axis=1, keepdims=True))
            low = (raised * (1.0 / jnp.sum(raised, axis=1, keepdims=True))).astype(BF16)
            prob[pair_at, pack] = low
            mixed = dot(low, both_values).astype(BF16)
            ctx_t[mine, text_lanes] = jnp.where(masks[0], mixed[:rows, :LANES], mixed[rows:, :LANES])
            kept = ctx_l[mine, layout_lanes]
            kept = jnp.where(masks[1], mixed[:rows, LANES:], kept)
            ctx_l[mine, layout_lanes] = jnp.where(masks[2], mixed[rows:, LANES:], kept)
        return unused

    lax.fori_loop(0, HEADS // 2, head_pair, 0, unroll=UNROLL)
    emit((prob, p_out), (ctx_t, ctx_t_out), (ctx_l, ctx_l_out))
    wait_all(w_copies)

    def own_rows(lanes):
        return jnp.concatenate(
            [xs[pl.ds(pack * keys, rows), lanes].astype(F32) for pack in range(packs)], axis=0
        )

    def tail(x, attended, expand, offsets, shrink, turned, b, g, cotangent, active, slope, branch, chunk, hid, unit, inv, delta, sv, outs):
        width = x.shape[1]
        middle = x + attended + b[2:3, :width]
        unit_first, inverse_first = normalized(middle)
        hidden = unit_first * g[0:1, :] + b[3:4, :width]
        hidden_low = hidden.astype(BF16)
        hid[...] = hidden_low
        unit[...] = unit_first
        inv[...] = inverse_first
        emit((hid, outs[0]), (unit, outs[1]), (inv, outs[2]))
        feed_forward(hidden_low, expand, offsets, shrink, turned, active, slope, chunk, branch)
        emit((slope, outs[3]))
        unit_second, inverse_second = normalized(hidden + branch[...] + b[4:5, :width])
        result = unit_second * g[1:2, :] + b[5:6, :width]
        sv[1:2, :] = column_sum(cotangent)
        sv[2:3, :] = column_sum(cotangent * unit_second)
        sum_delta = norm_back(cotangent * g[1:2, :], unit_second, inverse_second)
        delta[...] = sum_delta
        emit((delta, outs[4]))
        rounded = sum_delta.astype(BF16).astype(F32)
        sv[0:1, :] = column_sum(rounded)
        emit((sv, outs[5]))
        return result, rounded

    result, rounded = tail(
        own_rows(slice(0, DT)), dot(ctx_t[...], mt[...]), et, ot, st, False, text_bias, gt[...].astype(F32),
        jnp.concatenate([cot_t[pack] for pack in range(packs)], axis=0).astype(F32),
        act_t, slope_t, branch_t, 512, hid_t, unit_t, inv_t, sum_t, sv_t,
        (hid_t_out, unit_t_out, inv_t_out, slope_t_out, sum_t_out, sv_t_out),
    )
    res_t[...] = result.astype(BF16)
    emit((res_t, res_t_out))
    turned[...] = rounded.T.astype(BF16)
    share = DT // 4
    for shard in range(4):
        own = turned[shard * share : (shard + 1) * share, :]
        for block in range(FT // DT):
            grads[shard, pl.ds(block * share, share), :] = dot(
                own, act_t[:, block * DT : (block + 1) * DT]
            ).astype(BF16)
    if grads.shape[1] > S_ROWS:
        grads[:, S_ROWS:, :] = jnp.zeros((4, grads.shape[1] - S_ROWS, DT), BF16)
    emit(*in_lines(grads, subs, dp_size, targets))
    result, unused = tail(
        own_rows(slice(DT, DT + DL)), dot(ctx_l[:, :DL], ml[...]), el, ol, sl, True, layout_bias,
        gl[...].astype(F32),
        jnp.concatenate([cot_l[pack].astype(F32).T for pack in range(packs)], axis=0),
        act_l, slope_l, branch_l, 256, hid_l, unit_l, inv_l, sum_l, sv_l,
        (hid_l_out, unit_l_out, inv_l_out, slope_l_out, sum_l_out, sv_l_out),
    )
    for pack in range(packs):
        res_l[pack] = result[pack * rows : (pack + 1) * rows, :].T.astype(BF16)
    emit((res_l, res_l_out), (act_l, act_l_out))
    wait_all(pending)


def forward_call(blocks, wt, wl, mt, et, st, ml, el, sl, cot_t, cot_l, bt, gt, ot, bl, gl, ol, packs, rows, dp_size, subs):
    tokens = packs * rows
    lines = total_lines(subs)
    every = tokens * len(blocks)
    keys = rows * len(blocks)
    pairs = HEADS // 2
    outs = (
        shape_of((tokens, DT), BF16),
        shape_of((packs, DL, rows), BF16),
        shape_of((tokens, DT), BF16),
        shape_of((tokens, SLAB), BF16),
        shape_of((every, DT), BF16),
        shape_of((every, SLAB), BF16),
        shape_of((every, DT), BF16),
        shape_of((every, SLAB), BF16),
        shape_of((pairs, packs, 2 * rows, keys), BF16),
        shape_of((tokens, DT), BF16),
        shape_of((tokens, SLAB), BF16),
        shape_of((tokens, DT), BF16),
        shape_of((tokens, DT), F32),
        shape_of((tokens, 1), F32),
        shape_of((tokens, DT), F32),
        shape_of((tokens, FT), BF16),
        shape_of((tokens, DL), BF16),
        shape_of((tokens, DL), F32),
        shape_of((tokens, 1), F32),
        shape_of((tokens, DL), F32),
        shape_of((tokens, FL), BF16),
        shape_of((tokens, FL), BF16),
        shape_of((8, DT), F32),
        shape_of((8, DL), F32),
    ) + pair_shapes(subs)
    out_specs = [ANY] * len(outs)
    kept = (0, 1, 2, 3, 9, 10) + tuple(range(11, 24))
    scratch = [
        pltpu.VMEM((every, DT + SLAB), BF16),
        *(pltpu.VMEM(outs[at].shape, outs[at].dtype) for at in kept),
        pltpu.VMEM((6, SLAB), F32),
        pltpu.VMEM(wt.shape, BF16),
        pltpu.VMEM(wl.shape, BF16),
        pltpu.VMEM(mt.shape, BF16),
        pltpu.VMEM(et.shape, BF16),
        pltpu.VMEM(st.shape, BF16),
        pltpu.VMEM((every, DT), BF16),
        pltpu.VMEM((every, SLAB), BF16),
        pltpu.VMEM((every, DT), BF16),
        pltpu.VMEM((every, SLAB), BF16),
        pltpu.VMEM((pairs, packs, 2 * rows, keys), BF16),
        pltpu.VMEM((packs, rows, keys), F32),
        pltpu.VMEM((tokens, FT), BF16),
        pltpu.VMEM((DT, tokens), BF16),
        pltpu.VMEM((tokens, DT), F32),
        pltpu.VMEM((tokens, DL), F32),
        pltpu.VMEM((4, lines, DT), BF16),
        pltpu.SemaphoreType.DMA((48 + 4 * dp_size * len(subs),)),
    ]
    return pl.pallas_call(
        functools.partial(forward_kernel, packs, rows, dp_size, subs),
        out_shape=outs,
        in_specs=[ANY] * 9 + [VMEM] * 11,
        out_specs=out_specs,
        scratch_shapes=scratch,
        compiler_params=pltpu.CompilerParams(vmem_limit_bytes=FIRST),
        cost_estimate=COST,
        name="forward",
    )(*blocks, wt, wl, mt, et, st, ml, el, sl, cot_t, cot_l, bt, gt, ot, bl, gl, ol)


def middle_kernel(
    dp_size,
    subs,
    hid_t_in,
    unit_t_in,
    inv_t_in,
    sum_t_in,
    slope_t_in,
    hid_l,
    unit_l,
    inv_l,
    sum_l,
    slope_l,
    act_l,
    ctx_t_in,
    ctx_l,
    st_in,
    et_in,
    mt_in,
    sl,
    el,
    ml,
    gt,
    gl,
    after,
    mid_t,
    mid_l,
    dctx_t,
    dctx_l,
    sv_t,
    sv_l,
    so_t,
    so_l,
    *rest,
):
    targets, rest = rest[: 2 * len(subs)], rest[2 * len(subs) :]
    (
        hid_t,
        unit_t,
        inv_t,
        sum_t,
        slope_t,
        ctx_t,
        st,
        et,
        mt,
        before_t,
        before_l,
        turned,
        grads,
        sems,
    ) = rest
    w_copies = copies_of(
        (
            (sum_t_in, sum_t), (st_in, st), (slope_t_in, slope_t), (hid_t_in, hid_t), (et_in, et),
            (unit_t_in, unit_t), (inv_t_in, inv_t), (ctx_t_in, ctx_t), (mt_in, mt),
        ),
        sems,
        0,
    )
    base = len(w_copies)

    def feed_back(branch_delta, shrink, turned, slope, before, so, chunk):
        for at in range(slope.shape[1] // chunk):
            part = pl.ds(at * chunk, chunk)
            if turned:
                active_delta = dot(branch_delta, shrink[:, part])
            else:
                active_delta = dot_nt(branch_delta, shrink[part, :])
            low = (active_delta * slope[:, part].astype(F32)).astype(BF16)
            before[:, part] = low
            so[:, part] = column_sum(low.astype(F32))

    def front(hidden_delta, total, unit, inv, g, merge, sv):
        delta = total[...] + hidden_delta
        sv[0:1, :] = column_sum(delta * unit[...])
        sv[1:2, :] = column_sum(delta)
        middle = norm_back(delta * g, unit[...], inv[...])
        low = middle.astype(BF16)
        rounded = low.astype(F32)
        sv[2:3, :] = column_sum(rounded)
        back = dot_nt(low, merge).astype(BF16)
        sv[3:4, :] = column_sum(back.astype(F32))
        return middle, rounded.T.astype(BF16), back

    layout_delta = sum_l[...].astype(BF16)
    feed_back(layout_delta, sl, True, slope_l, before_l, so_l, 256)
    turned_l = before_l[...].astype(F32).T.astype(BF16)
    grown_l = dot(turned_l, hid_l[...]).astype(BF16)
    shrunk_l = dot(layout_delta.astype(F32).T.astype(BF16), act_l[...]).astype(BF16)
    middle, low_turned, back = front(
        dot_nt(before_l[...], el[...]), sum_l, unit_l, inv_l, gl[0:1, :].astype(F32), ml[...], sv_l
    )
    for pack in range(mid_l.shape[0]):
        size = mid_l.shape[2]
        mid_l[pack] = middle[pack * size : (pack + 1) * size, :].T
    dctx_l[...] = jnp.zeros_like(dctx_l)
    dctx_l[:, :DL] = back
    merged_l = dot(low_turned, ctx_l[...]).astype(BF16)
    wait_all(w_copies[:3])
    feed_back(sum_t[...].astype(BF16), st, False, slope_t, before_t, so_t, 512)
    wait_all(w_copies[3:4])
    turned[...] = hid_t[...].astype(F32).T.astype(BF16)
    for shard in range(4):
        grads[shard, pl.ds(0, DT), :] = dot(
            turned[...], before_t[:, shard * DT : (shard + 1) * DT]
        ).astype(BF16)
    early = copies_of(in_lines(grads, subs, dp_size, targets, 0, DT), sems, base)
    base += len(early)
    wait_all(w_copies[4:])
    middle, low_turned, back = front(
        dot_nt(before_t[...], et[...]), sum_t, unit_t, inv_t, gt[0:1, :].astype(F32), mt[...], sv_t
    )
    mid_t[...] = middle
    dctx_t[...] = back
    for shard in range(4):
        grads[shard, pl.ds(DT, 192), :] = dot(
            low_turned[shard * 192 : (shard + 1) * 192, :], ctx_t[...]
        ).astype(BF16)
    for shard in range(4):
        grads[shard, 960:, :] = jnp.zeros((grads.shape[1] - 960, DT), BF16)
        for at in range(3):
            lanes = slice(at * SLAB, at * SLAB + DL)
            line = shard * DL + at * 64
            grads[shard, 960:1024, lanes] = grown_l[line : line + 64, :]
            line = shard * 48 + at * 16
            grads[shard, 1072:1088, at * SLAB : (at + 1) * SLAB] = merged_l[line : line + 16, :]
        grads[shard, 1024:1072, :] = shrunk_l[shard * 48 : shard * 48 + 48, :]
    wait_all(copies_of(in_lines(grads, subs, dp_size, targets, DT), sems, base))
    wait_all(early)


def middle_call(operands, packs, rows, dp_size, subs):
    tokens = packs * rows
    lines = total_lines(subs)
    outs = (
        shape_of((tokens, DT), F32),
        shape_of((packs, DL, rows), F32),
        shape_of((tokens, DT), BF16),
        shape_of((tokens, SLAB), BF16),
        shape_of((8, DT), F32),
        shape_of((8, DL), F32),
        shape_of((1, FT), F32),
        shape_of((1, FL), F32),
    ) + pair_shapes(subs)
    scratch = [
        *(pltpu.VMEM(operands[at].shape, operands[at].dtype) for at in (0, 1, 2, 3, 4, 11)),
        pltpu.VMEM((FT, DT), BF16),
        pltpu.VMEM((DT, FT), BF16),
        pltpu.VMEM((DT, DT), BF16),
        pltpu.VMEM((tokens, FT), BF16),
        pltpu.VMEM((tokens, FL), BF16),
        pltpu.VMEM((DT, tokens), BF16),
        pltpu.VMEM((4, lines, DT), BF16),
        pltpu.SemaphoreType.DMA((16 + 4 * dp_size * len(subs),)),
    ]
    return pl.pallas_call(
        functools.partial(middle_kernel, dp_size, subs),
        out_shape=outs,
        in_specs=[ANY] * 5 + [VMEM] * 6 + [ANY, VMEM] + [ANY] * 3 + [VMEM] * 5 + [ANY],
        out_specs=[VMEM] * 8 + [ANY] * (2 * len(subs)),
        scratch_shapes=scratch,
        compiler_params=pltpu.CompilerParams(vmem_limit_bytes=SECOND),
        cost_estimate=COST,
        name="middle",
    )(*operands)


def attention_kernel(
    packs,
    rows,
    dp_size,
    subs,
    x0,
    x1,
    x2,
    x3,
    kt_in,
    kl_in,
    vt_in,
    vl_in,
    p_in,
    q_t,
    q_l,
    dctx_t,
    dctx_l,
    ctx_t,
    ctx_l,
    sf_t,
    sf_l,
    sm_t,
    sm_l,
    so_t,
    so_l,
    after,
    joined_t_out,
    joined_l_out,
    query_t_out,
    query_l_out,
    *rest,
):
    targets, rest = rest[: 2 * len(subs)], rest[2 * len(subs) :]
    (
        xs,
        joined_t,
        joined_l,
        query_t,
        query_l,
        k_t,
        k_l,
        v_t,
        v_l,
        prob,
        dq_t,
        dq_l,
        dk_l,
        dv_l,
        layout_grads,
        grads,
        smalls,
        sems,
    ) = rest
    blocks = (x0, x1, x2, x3)
    keys = rows * len(blocks)
    kv_copies = copies_of(((kt_in, k_t), (vt_in, v_t), (kl_in, k_l), (vl_in, v_l)), sems, 0)

    def chances(at):
        return pltpu.make_async_copy(p_in.at[at], prob.at[at], sems.at[4 + at])

    for at in range(HEADS // 2):
        chances(at).start()
    base = 4 + HEADS // 2
    dq_l[...] = jnp.zeros_like(dq_l)
    dk_l[...] = jnp.zeros_like(dk_l)
    dv_l[...] = jnp.zeros_like(dv_l)
    wait_all(kv_copies)
    x_copies = copies_of(gather_pairs(blocks, rows, packs, xs), sems, base)
    base += len(x_copies)

    def head_pair(pair_at, unused):
        chances(pair_at).wait()
        masks = lane_masks(pair_at)
        text_lanes = pl.ds(pl.multiple_of(pair_at * LANES, LANES), LANES)
        layout_lanes = pl.ds(pl.multiple_of(pair_at // 4 * LANES, LANES), LANES)
        for pack in range(packs):
            mine = pl.ds(pack * rows, rows)
            span = pl.ds(pack * keys, keys)
            queries = stacked_heads(q_t[mine, text_lanes], q_l[mine, layout_lanes], masks)
            deltas = stacked_heads(dctx_t[mine, text_lanes], dctx_l[mine, layout_lanes], masks)
            one = jnp.concatenate([ctx_t[mine, text_lanes], ctx_l[mine, layout_lanes]], axis=1)
            contexts = jnp.concatenate([one, one], axis=0).astype(F32)
            products = deltas.astype(F32) * contexts
            layout_mean = jnp.sum(products[:, LANES:], axis=1, keepdims=True)
            both_mean = jnp.sum(products, axis=1, keepdims=True)
            text_values = v_t[span, text_lanes]
            layout_values = v_l[span, layout_lanes]
            both_values = jnp.concatenate([text_values, layout_values], axis=1)
            low = prob[pair_at, pack]
            chance = low.astype(F32)
            both_change = (chance * (dot_nt(deltas, both_values) - both_mean)).astype(BF16)
            layout_change = (
                chance * (dot_nt(deltas[:, LANES:], layout_values) - layout_mean)
            ).astype(BF16)
            from_text = dot(both_change, k_t[span, text_lanes])
            dq_t[mine, text_lanes] = (
                jnp.where(masks[0], from_text[:rows], from_text[rows:]) * 0.125
            ).astype(BF16)
            from_layout = dot(layout_change, k_l[span, layout_lanes]) * 0.25
            kept = dq_l[mine, layout_lanes]
            kept = jnp.where(masks[1], from_layout[:rows], kept)
            dq_l[mine, layout_lanes] = jnp.where(masks[2], from_layout[rows:], kept)
            turned_queries = queries.T
            turned_deltas = deltas.T
            joined_t[text_lanes, span] = dot(turned_queries[:LANES], both_change).astype(BF16)
            dk_l[layout_lanes, span] += dot(turned_queries[LANES:], layout_change)
            value_change = dot(turned_deltas, low)
            text_at = pl.ds(pl.multiple_of(pair_at * LANES + DT, LANES), LANES)
            joined_t[text_at, span] = value_change[:LANES].astype(BF16)
            dv_l[layout_lanes, span] += value_change[LANES:]
        return unused

    lax.fori_loop(0, HEADS // 2, head_pair, 0, unroll=UNROLL_BACK)
    joined_l[:SLAB, :] = dk_l[...].astype(BF16)
    joined_l[SLAB:, :] = dv_l[...].astype(BF16)
    whole_t = dq_t[...].astype(F32)
    whole_l = dq_l[...]
    low_l = whole_l.astype(BF16)
    query_t[...] = whole_t.T.astype(BF16)
    query_l[...] = whole_l.T.astype(BF16)
    out_copies = copies_of(
        ((joined_t, joined_t_out), (joined_l, joined_l_out), (query_t, query_t_out), (query_l, query_l_out)),
        sems,
        base,
    )
    base += 4
    wait_all(x_copies)
    own = jnp.concatenate([xs[pl.ds(pack * keys, rows), :] for pack in range(packs)], axis=0)
    step = 192
    for at in range(3 * DT // step):
        shard, line = at // 3, at % 3 * step
        if at < DT // step:
            product = dot(query_t[at * step : (at + 1) * step, :], own[:, :DT])
        else:
            product = dot(joined_t[at * step - DT : (at + 1) * step - DT, :], xs[:, :DT])
        grads[shard, line : line + step, :] = product.astype(BF16)
    layout_grads[:DL, :] = dot(query_l[:DL, :], own[:, DT:]).astype(BF16)
    layout_grads[DL : 2 * DL, :] = dot(joined_l[:DL, :], xs[:, DT:]).astype(BF16)
    layout_grads[2 * DL :, :] = dot(joined_l[SLAB : SLAB + DL, :], xs[:, DT:]).astype(BF16)
    text_lines = jnp.concatenate(
        [column_sum(whole_t), sm_t[3:4, :], sm_t[2:3, :], sm_t[1:2, :], sf_t[0:2, :], sm_t[0:1, :], sf_t[2:3, :]],
        axis=0,
    )
    layout_lines = jnp.concatenate(
        [
            column_sum(low_l.astype(F32))[:, :DL],
            sm_l[3:4, :], sm_l[2:3, :], sm_l[1:2, :], sf_l[0:2, :], sm_l[0:1, :], sf_l[2:3, :],
        ],
        axis=0,
    )
    for shard in range(4):
        for at in range(3):
            line = shard * 144 + at * 48
            grads[shard, 576:624, at * SLAB : (at + 1) * SLAB] = layout_grads[line : line + 48, :]
        smalls[...] = jnp.zeros_like(smalls)
        share = DT // 4
        smalls[0:8, 0:share] = text_lines[:, shard * share : (shard + 1) * share]
        smalls[8:9, :] = so_t[:, shard * DT : (shard + 1) * DT]
        share = DL // 4
        smalls[0:8, SLAB : SLAB + share] = layout_lines[:, shard * share : (shard + 1) * share]
        share = FL // 4
        smalls[9:10, 0:share] = so_l[:, shard * share : (shard + 1) * share]
        grads[shard, 624:640, :] = smalls[...].astype(BF16)
        if grads.shape[1] > P_ROWS:
            grads[shard, P_ROWS:, :] = jnp.zeros((grads.shape[1] - P_ROWS, DT), BF16)
    wait_all(copies_of(in_lines(grads, subs, dp_size, targets), sems, base))
    wait_all(out_copies)


def attention_call(operands, packs, rows, dp_size, subs):
    tokens = packs * rows
    every = tokens * 4
    lines = total_lines(subs)
    pairs = HEADS // 2
    outs = (
        shape_of((2 * DT, every), BF16),
        shape_of((2 * SLAB, every), BF16),
        shape_of((DT, tokens), BF16),
        shape_of((SLAB, tokens), BF16),
    ) + pair_shapes(subs)
    scratch = [
        pltpu.VMEM((every, DT + SLAB), BF16),
        *(pltpu.VMEM(outs[at].shape, outs[at].dtype) for at in range(4)),
        pltpu.VMEM((every, DT), BF16),
        pltpu.VMEM((every, SLAB), BF16),
        pltpu.VMEM((every, DT), BF16),
        pltpu.VMEM((every, SLAB), BF16),
        pltpu.VMEM((pairs, packs, 2 * rows, 4 * rows), BF16),
        pltpu.VMEM((tokens, DT), BF16),
        pltpu.VMEM((tokens, SLAB), F32),
        pltpu.VMEM((SLAB, every), F32),
        pltpu.VMEM((SLAB, every), F32),
        pltpu.VMEM((3 * DL, SLAB), BF16),
        pltpu.VMEM((4, lines, DT), BF16),
        pltpu.VMEM((16, DT), F32),
        pltpu.SemaphoreType.DMA((32 + 4 * dp_size * len(subs),)),
    ]
    return pl.pallas_call(
        functools.partial(attention_kernel, packs, rows, dp_size, subs),
        out_shape=outs,
        in_specs=[ANY] * 9 + [VMEM] * 12 + [ANY],
        out_specs=[ANY] * len(outs),
        scratch_shapes=scratch,
        compiler_params=pltpu.CompilerParams(vmem_limit_bytes=LAST),
        cost_estimate=COST,
        name="attention_back",
    )(*operands)


def input_kernel(
    packs, rows, joined_in, joined_l, query_t, query_l, wt_in, wl, after, give, hold, joined_t, wt, totals, sums, sems
):
    keys = joined_t.shape[1] // packs
    pairs = []
    for third in (1, 2):
        lanes = pl.ds(third * DT, DT)
        lines = pl.ds((third - 1) * DT, DT)
        pairs += [(wt_in.at[:, lanes], wt.at[:, lanes]), (joined_in.at[lines, :], joined_t.at[lines, :])]
    pairs.append((wt_in.at[:, pl.ds(0, DT)], wt.at[:, pl.ds(0, DT)]))
    copies = copies_of(pairs, sems, 0)

    def tokens_of(ref, lines, at):
        spans = [slice(pack * keys + at * rows, pack * keys + (at + 1) * rows) for pack in range(packs)]
        return jnp.concatenate([ref[lines, span] for span in spans], axis=1)

    everything = slice(None)
    for at in range(4):
        sums[at, DT:, :] = dot(wl[:, SLAB:], tokens_of(joined_l, everything, at)).astype(BF16)
    layout_own = dot(wl[:, :SLAB], query_l[...])
    sums[0, DT:, :] = (sums[0, DT:, :].astype(F32) + layout_own).astype(BF16)
    wait_all(copies[:2])
    for at in range(4):
        totals[at] = dot(wt[:, DT : 2 * DT], tokens_of(joined_t, slice(0, DT), at))
    wait_all(copies[2:])
    out = []
    for at in (3, 1, 2, 0):
        total = totals[at] + dot(wt[:, 2 * DT :], tokens_of(joined_t, slice(DT, 2 * DT), at))
        if at == 0:
            total += dot(wt[:, :DT], query_t[...])
        sums[at, :DT, :] = total.astype(BF16)
        target = (hold, give)[at % 2].at[at // 2]
        out += copies_of(((sums.at[at], target),), sems, 5 + at)
    wait_all(out)


def input_call(joined_t, joined_l, query_t, query_l, wt, wl, after, packs, rows):
    tokens = packs * rows
    return pl.pallas_call(
        functools.partial(input_kernel, packs, rows),
        out_shape=(shape_of((2, DT + DL, tokens), BF16),) * 2,
        in_specs=[ANY] + [VMEM] * 3 + [ANY, VMEM, after[1]],
        out_specs=[ANY] * 2,
        scratch_shapes=[
            pltpu.VMEM(joined_t.shape, BF16),
            pltpu.VMEM(wt.shape, BF16),
            pltpu.VMEM((4, DT, tokens), F32),
            pltpu.VMEM((4, DT + DL, tokens), BF16),
            pltpu.SemaphoreType.DMA((9,)),
        ],
        compiler_params=pltpu.CompilerParams(vmem_limit_bytes=LIMIT),
        cost_estimate=COST,
        name="input_back",
    )(joined_t, joined_l, query_t, query_l, wt, wl, after[0])


def sensitivity_kernel(own, far, mid_t, mid_l, after, out_t, out_l):
    total = own[...].astype(F32) + far[...].astype(F32)
    out_t[...] = mid_t[...] + total[:DT, :].T
    packs, unused, rows = mid_l.shape
    for pack in range(packs):
        out_l[pack] = mid_l[pack] + total[DT:, pack * rows : (pack + 1) * rows]


def sensitivity_call(own, far, mid_t, mid_l, after):
    return pl.pallas_call(
        sensitivity_kernel,
        out_shape=(shape_of(mid_t.shape, F32), shape_of(mid_l.shape, F32)),
        in_specs=[VMEM] * 4 + [after[1]],
        out_specs=[VMEM] * 2,
        compiler_params=pltpu.CompilerParams(vmem_limit_bytes=SMALL),
        cost_estimate=COST,
        name="sensitivity",
    )(own, far, mid_t, mid_l, after[0])


def lines_in_order(dp_size, sources, subs, whole):
    device = lax.axis_index("dp")
    for at, (first, rows, hops, growth) in enumerate(subs):
        half, other = sources[2 * at : 2 * at + 2]
        size = rows // dp_size
        for index in range(dp_size):
            line = position(growth[::-1], 0, index) * size
            source = half if line < rows // 2 else other
            line = line % (rows // 2)
            mark = pl.multiple_of(first + jnp.bitwise_xor(device, index) * size, 16)
            whole[pl.ds(mark, size), :] = source[line : line + size, :].astype(F32)


def shrink_store(whole, out):
    share = DT // 4
    for block in range(FT // DT):
        out[:, block * DT : (block + 1) * DT] = whole[block * share : (block + 1) * share, :]


def expand_store(whole, out, out_merge, out_grow, out_shrink, out_layout_merge):
    out[...] = whole[:DT, :]
    out_merge[...] = whole[DT:960, :]
    grown = jnp.concatenate(
        [whole[960:1024, at * SLAB : at * SLAB + DL] for at in range(3)], axis=0
    )
    out_grow[...] = grown.T
    out_shrink[...] = whole[1024:1072, :]
    out_layout_merge[...] = jnp.concatenate(
        [whole[1072:1088, at * SLAB : at * SLAB + DL] for at in range(3)], axis=0
    )


def project_store(whole, out, out_layout, biases_t, gains_t, offsets_t, biases_l, gains_l, offsets_l):
    out[...] = whole[:576, :]
    out_layout[...] = jnp.concatenate(
        [whole[576:624, at * SLAB : at * SLAB + DL] for at in range(3)], axis=0
    )
    biases_t[...] = whole[624:630, : DT // 4]
    gains_t[...] = whole[630:632, : DT // 4]
    offsets_t[...] = whole[632:633, :].reshape(DT)
    biases_l[...] = whole[624:630, SLAB : SLAB + DL // 4]
    gains_l[...] = whole[630:632, SLAB : SLAB + DL // 4]
    offsets_l[...] = whole[633:634, : FL // 4].reshape(FL // 4)


def final_kernel(store, dp_size, subs, *refs):
    sources, outs, whole = refs[: 2 * len(subs)], refs[2 * len(subs) + 1 : -1], refs[-1]
    lines_in_order(dp_size, sources, subs, whole)
    store(whole, *outs)


def final_call(store, name, sources, after, dp_size, subs, outs):
    return pl.pallas_call(
        functools.partial(final_kernel, store, dp_size, subs),
        out_shape=tuple(shape_of(shape, F32) for shape in outs),
        in_specs=[VMEM] * len(sources) + [after[1]],
        out_specs=[VMEM] * len(outs),
        scratch_shapes=[pltpu.VMEM((total_lines(subs), DT), F32)],
        compiler_params=pltpu.CompilerParams(vmem_limit_bytes=SMALL),
        cost_estimate=COST,
        name=name,
    )(*sources, after[0])


def add_kernel(count, parts, *refs):
    sources, targets = refs[: count * parts], refs[count * parts + 1 :]
    for at, target in enumerate(targets):
        total = sources[at][...].astype(F32)
        for n in range(1, count):
            total += sources[n * parts + at][...].astype(F32)
        target[...] = total.astype(BF16)


def add_call(sources, parts, after):
    lines, width = sources[0].shape
    size = lines // parts
    steps = max(n for n in (1, 2, 3, 4) if size % (16 * n) == 0 and (n == 1 or lines // n >= 256))
    block = size // steps
    specs = [
        pl.BlockSpec((block, width), functools.partial(lambda at, i: (at * steps + i, 0), at))
        for unused in sources
        for at in range(parts)
    ]
    return pl.pallas_call(
        functools.partial(add_kernel, len(sources), parts),
        grid=(steps,),
        out_shape=(shape_of((size, width), BF16),) * parts,
        in_specs=specs + [after[1]],
        out_specs=[pl.BlockSpec((block, width), lambda i: (i, 0))] * parts,
        compiler_params=pltpu.CompilerParams(vmem_limit_bytes=SMALL),
        cost_estimate=COST,
        name="add",
    )(*[source for source in sources for unused in range(parts)], after[0])


def gate_call(arrays, after):
    count = len(arrays)
    return pl.pallas_call(
        lambda *refs: None,
        out_shape=tuple(shape_of(array.shape, array.dtype) for array in arrays),
        in_specs=[ANY] * count + [after[1]],
        out_specs=[ANY] * count,
        input_output_aliases={at: at for at in range(count)},
        compiler_params=pltpu.CompilerParams(vmem_limit_bytes=SMALL),
        cost_estimate=COST,
        name="gate",
    )(*arrays, after[0])


def join_kernel(count, *refs):
    sources, target = refs[:count], refs[-1]
    size = sources[0].shape[0]
    for at, source in enumerate(sources):
        target[at * size : (at + 1) * size, :] = source[...]


def join_call(sources, after):
    lines, width = sources[0].shape
    return pl.pallas_call(
        functools.partial(join_kernel, len(sources)),
        out_shape=shape_of((len(sources) * lines, width), BF16),
        in_specs=[VMEM] * len(sources) + [after[1]],
        out_specs=VMEM,
        compiler_params=pltpu.CompilerParams(vmem_limit_bytes=SMALL),
        cost_estimate=COST,
        name="join",
    )(*sources, after[0])


def sent(array, group, index, seq_size, dp_size):
    across = other = 0
    for n, (axis, bit) in enumerate(group):
        if index & (1 << n):
            if axis == "seq":
                across |= bit
            else:
                other |= bit
    if not other:
        return lax.ppermute(array, "seq", [(at, at ^ across) for at in range(seq_size)])
    if not across:
        return lax.ppermute(array, "dp", [(at, at ^ other) for at in range(dp_size)])
    pairs = [
        (d * seq_size + s, (d ^ other) * seq_size + (s ^ across))
        for d in range(dp_size)
        for s in range(seq_size)
    ]
    return lax.ppermute(array, ("dp", "seq"), pairs)


def steps_of(give, hold, hops, growth, send):
    parts = [hold, send(give, (("seq", 1),), 1)]
    for group in hops:
        keep, *sends = yield functools.partial(add_call, parts, 1 << len(group))
        parts = [keep] + [send(array, group, at + 1) for at, array in enumerate(sends)]
    (piece,) = yield functools.partial(add_call, parts, 1)
    gathered = [piece]
    for group in growth:
        if len(gathered) > 1:
            piece = yield functools.partial(join_call, gathered)
        gathered = [piece] + [send(piece, group, at) for at in range(1, 1 << len(group))]
    return gathered


X = ("dp", 1)
Y = ("seq", 2)
Z1 = ("dp", 2)
Z2 = ("dp", 4)


def hops_of(text, extra):
    groups = {"x": (X,), "y": (Y,), "1": (Z1,), "2": (Z2,), "d": (Y, X), "z": (Z1, Z2)}
    return tuple(groups[letter] for letter in text) + extra


SPLIT_S = ((768, "y1x2B"), )
SPLIT_E = ((640, "1xy2B"), (512, "xyzB"), )
SPLIT_P = ((256, "xy12B"), (384, "yxzB"), )
ORDER = ('B', 'S0', 'GE', 'E1', 'E0', 'C', 'E1', 'S0', 'E0', 'GP', 'D', 'E1', 'P0', 'S0', 'E0', 'P1', 'GX', 'E1', 'X0', 'E0', 'E1', 'S0', 'P0', 'E0', 'FX', 'E1', 'S0', 'P0', 'E0', 'P0', 'P1', 'S0', 'P0', 'E0', 'P1', 'P0', 'S0', 'P0', 'P1', 'FE', 'P1', 'P1', 'FS', 'FP')


def local(
    dp_size,
    seq_size,
    text_input,
    layout_input,
    segments,
    text_cotangent,
    layout_cotangent,
    text_project,
    text_biases,
    text_gains,
    text_merge,
    text_expand,
    text_offsets,
    text_shrink,
    layout_project,
    layout_biases,
    layout_gains,
    layout_merge,
    layout_expand,
    layout_offsets,
    layout_shrink,
):
    packs, rows, unused = text_input.shape

    def send(array, group, index):
        return sent(array, group, index, seq_size, dp_size)

    core = (("seq", 1),)
    own, wl, line_t, line_l = prepare_call(
        text_input, layout_input.transpose(0, 2, 1), segments, layout_project, text_offsets, layout_offsets
    )
    far, near = send(own, (Y,), 1), send(own, core, 1)
    blocks = (own, near, far, send(far, core, 1))
    turned_shrink = layout_shrink.T

    bits = [1 << at for at in range((dp_size - 1).bit_length())]
    extra = tuple((("dp", bit),) for bit in bits[3:])
    growths = {
        "B": tuple(reversed(extra)) + ((Z2,), (Z1,), (X,)),
        "D": tuple(reversed(extra)) + ((Z1, Z2), (X,)),
    }
    subs = {
        name: sub_chunks(count, [(share, hops_of(text[:-1], extra), growths[text[-1]]) for share, text in split], dp_size)
        for name, count, split in (
            ("S", S_ROWS, SPLIT_S),
            ("E", E_ROWS, SPLIT_E),
            ("P", P_ROWS, SPLIT_P),
        )
    }
    reductions = {}
    calls = {}
    halves = {}
    values = {}
    token = None

    def begin(name, pairs):
        for at, (first, count, hops, growth) in enumerate(subs[name]):
            steps = steps_of(pairs[2 * at], pairs[2 * at + 1], hops, growth, send)
            reductions[name + str(at)] = steps
            calls[name + str(at)] = next(steps)

    def forward(after):
        (
            res_t, res_l, q_t, q_l, kt, kl, vt, vl, p, ctx_t, ctx_l,
            hid_t, unit_t, inv_t, sum_t, slope_t,
            hid_l, unit_l, inv_l, sum_l, slope_l, act_l, sf_t, sf_l,
            *pairs,
        ) = forward_call(
            blocks, text_project, wl, text_merge, text_expand, text_shrink,
            layout_merge, layout_expand, turned_shrink,
            text_cotangent, layout_cotangent.transpose(0, 2, 1),
            text_biases, text_gains, line_t, layout_biases, layout_gains,
            line_l, packs, rows, dp_size, subs["S"],
        )
        begin("S", pairs)
        values.update(
            results=(res_t, res_l),
            tail=(
                hid_t, unit_t, inv_t, sum_t, slope_t, hid_l, unit_l, inv_l, sum_l, slope_l, act_l,
                ctx_t, ctx_l,
            ),
            attended=(kt, kl, vt, vl, p, q_t, q_l),
            contexts=(ctx_t, ctx_l),
            first_sums=(sf_t, sf_l),
        )
        return sf_t, HBM

    def middle(after):
        mid_t, mid_l, dctx_t, dctx_l, sm_t, sm_l, so_t, so_l, *pairs = middle_call(
            (
                *values["tail"], text_shrink, text_expand, text_merge, turned_shrink,
                layout_expand, layout_merge, text_gains, layout_gains, after[0],
            ),
            packs, rows, dp_size, subs["E"],
        )
        values["E pairs"] = pairs
        values.update(
            middles=(mid_t, mid_l), deltas=(dctx_t, dctx_l), second_sums=(sm_t, sm_l, so_t, so_l)
        )
        return sm_t, HBM

    def attention(after):
        joined_t, joined_l, query_t, query_l, *pairs = attention_call(
            (
                *blocks, *values["attended"], *values["deltas"],
                *values["contexts"], *values["first_sums"], *values["second_sums"], after[0],
            ),
            packs, rows, dp_size, subs["P"],
        )
        values["P pairs"] = pairs
        values.update(joined=(joined_t, joined_l, query_t, query_l))
        return query_l, HBM

    def inputs(after):
        give, hold = input_call(*values["joined"], text_project, wl, after, packs, rows)
        values["X pairs"] = [give, hold]
        return hold, HBM

    def inputs_gate(after):
        give, hold = gate_call(values["X pairs"], after)
        lines = 2 * (DT + DL)
        values.update(inputs=[hold.reshape(lines, -1), send(give, core, 1).reshape(lines, -1)])
        return hold, ANY

    def gate(name):
        def call(after):
            pairs = gate_call(values[name + " pairs"], after)
            begin(name, pairs)
            return pairs[1], ANY

        return call

    def inputs_add(after):
        own, onward = add_call(values["inputs"], 2, after)
        values.update(onward=(own, send(onward, (Y,), 1)))
        return own, ANY

    def inputs_end(after):
        values.update(sens=sensitivity_call(*values["onward"], *values["middles"], after))
        return values["sens"][1], HBM

    def end(name, store, label, outs):
        def call(after):
            sources = [array for at in range(len(subs[name])) for array in halves[name + str(at)]]
            values[name] = final_call(
                store, label, sources, after, dp_size, subs[name], outs
            )
            return values[name][-1], HBM

        return call

    kernels = {
        "A": forward,
        "B": middle,
        "C": attention,
        "D": inputs,
        "GE": gate("E"),
        "GP": gate("P"),
        "GX": inputs_gate,
        "X0": inputs_add,
        "FX": inputs_end,
        "FS": end("S", shrink_store, "shrink_out", [(DT // 4, FT)]),
        "FE": end(
            "E", expand_store, "expand_out",
            [(DT, DT), (DT // 4, DT), (DL, DL), (DL // 4, FL), (DL // 4, DL)],
        ),
        "FP": end(
            "P", project_store, "project_out",
            [
                (576, DT), (144, DL), (6, DT // 4), (2, DT // 4), (DT,),
                (6, DL // 4), (2, DL // 4), (FL // 4,),
            ],
        ),
    }

    def advance(name, after):
        outs = calls[name](after)
        try:
            calls[name] = reductions[name].send(outs)
        except StopIteration as stop:
            halves[name] = stop.value
            del calls[name]
        return (outs[0] if isinstance(outs, (tuple, list)) else outs), ANY

    def finish(name, after):
        for at in range(len(subs[name])):
            while name + str(at) in calls:
                after = advance(name + str(at), after)
        return after

    token = forward(None)
    for label in ORDER:
        if label in kernels:
            if label[0] == "F" and label[1] in subs:
                token = finish(label[1], token)
            token = kernels[label](token)
        elif label in calls:
            token = advance(label, token)

    res_t, res_l = values["results"]
    sens_t, sens_l = values["sens"]
    (shrink_t,) = values["S"]
    expand_t, merge_t, expand_l, shrink_l, merge_l = values["E"]
    project_t, project_l, biases_t, gains_t, offsets_t, biases_l, gains_l, offsets_l = values["P"]
    return (
        res_t.reshape(packs, rows, DT),
        res_l.transpose(0, 2, 1),
        sens_t.reshape(packs, rows, DT),
        sens_l.transpose(0, 2, 1),
        project_t.T,
        biases_t,
        gains_t,
        merge_t.T,
        expand_t,
        offsets_t,
        shrink_t.T,
        project_l.T,
        biases_l,
        gains_l,
        merge_l.T,
        expand_l,
        offsets_l,
        shrink_l.T,
    )


def solution(mesh):
    rows = P("dp", "seq", None)
    columns = P(None, "seq")
    in_specs = (rows, rows, P("dp", "seq"), rows, rows) + (P(),) * 14
    out_specs = (
        (rows,) * 4 + (columns,) * 5 + (P("seq"),) + (columns,) * 6 + (P("seq"),) + (columns,)
    )
    body = functools.partial(local, mesh.shape["dp"], mesh.shape["seq"])
    return jax.shard_map(body, mesh=mesh, in_specs=in_specs, out_specs=out_specs, check_vma=False)
```

```python
import functools

import jax
import jax.numpy as jnp
from jax import lax
from jax.experimental import pallas as pl
from jax.experimental.pallas import tpu as pltpu
from jax.sharding import PartitionSpec as P

HEADS = 12
EPSILON = 1e-05
MASKED = -1000000000.0
F32 = jnp.float32
BF16 = jnp.bfloat16
DT = 768
DL = 192
FT = 3072
FL = 768
LANES = 128
SLAB = 256
S_ROWS = 768
E_ROWS = 1152
P_ROWS = 640
MIB = 1024 * 1024

VMEM = pl.BlockSpec(memory_space=pltpu.VMEM)
ANY = pl.BlockSpec(memory_space=pl.ANY)
HBM = pl.BlockSpec(memory_space=pltpu.HBM)


def dot(left, right):
    return jnp.dot(left, right, preferred_element_type=F32)


def dot_nt(left, right):
    return lax.dot_general(left, right, (((1,), (1,)), ((), ())), preferred_element_type=F32)


LIMIT = 60 * MIB
FIRST = 60 * MIB
SECOND = 60 * MIB
LAST = 30 * MIB
SMALL = 16 * MIB
UNROLL = 6
UNROLL_BACK = 1


COST = pl.CostEstimate(flops=1, bytes_accessed=1, transcendentals=0)


def shape_of(shape, dtype):
    return jax.ShapeDtypeStruct(shape, dtype)


def copies_of(pairs, sems, base):
    made = []
    for at, (source, target) in enumerate(pairs):
        copy = pltpu.make_async_copy(source, target, sems.at[base + at])
        copy.start()
        made.append(copy)
    return made


def wait_all(made):
    for copy in made:
        copy.wait()


def gather_pairs(blocks, rows, packs, target):
    span = rows * len(blocks)
    return [
        (block.at[pack], target.at[pl.ds(pack * span + at * rows, rows), :])
        for at, block in enumerate(blocks)
        for pack in range(packs)
    ]


def in_lines(shards, subs, dp_size, targets, low=0, high=1 << 30):
    place = (lax.axis_index("seq"), lax.axis_index("dp"))
    pairs = []
    for core in (1, 0):
        for at, (first, rows, hops, growth) in enumerate(subs):
            if not low < first + rows <= high:
                continue
            size = rows // dp_size
            target = targets[2 * at + 1 - core]
            for across in range(2):
                shard = jnp.bitwise_xor(place[0], core + 2 * across)
                for other in range(dp_size):
                    piece = jnp.bitwise_xor(place[1], other)
                    mark = pl.multiple_of(first + piece * size, 16)
                    line = position(hops, across, other) * size
                    pairs.append(
                        (shards.at[shard, pl.ds(mark, size), :], target.at[pl.ds(line, size), :])
                    )
    return pairs


def position(hops, across, other):
    at = 0
    for group in hops:
        index = 0
        for n, (axis, bit) in enumerate(group):
            if across if axis == "seq" else other & bit:
                index += 1 << n
        at = (at << len(group)) + index
    return at


def sub_chunks(rows, split, dp_size):
    step = 16 * dp_size
    total = (rows + step - 1) // step * step
    subs = []
    first = 0
    for at, (share, hops, growth) in enumerate(split):
        size = total - first if at == len(split) - 1 else (share + step - 1) // step * step
        subs.append((first, size, hops, growth))
        first += size
    return tuple(subs)


def total_lines(subs):
    return sum(rows for first, rows, hops, growth in subs)


def pair_shapes(subs):
    return tuple(shape_of((2 * rows, DT), BF16) for first, rows, hops, growth in subs for unused in range(2))


def lane_masks(pair_at):
    lanes = lax.broadcasted_iota(jnp.int32, (1, LANES), 1)
    low_half = lanes < 64
    group_of_16 = lax.shift_right_logical(lanes, 4)
    first = group_of_16 == 2 * lax.rem(pair_at, 4)
    second = group_of_16 == 2 * lax.rem(pair_at, 4) + 1
    return (low_half, first, second)


def stacked_heads(text_rows, layout_rows, masks):
    low_half, first, second = masks
    zero_text = jnp.zeros_like(text_rows)
    zero_layout = jnp.zeros_like(layout_rows)
    top = jnp.concatenate(
        [jnp.where(low_half, text_rows, zero_text), jnp.where(first, layout_rows, zero_layout)],
        axis=1,
    )
    bottom = jnp.concatenate(
        [jnp.where(low_half, zero_text, text_rows), jnp.where(second, layout_rows, zero_layout)],
        axis=1,
    )
    return jnp.concatenate([top, bottom], axis=0)


def normalized(values):
    centre = values - jnp.mean(values, axis=-1, keepdims=True)
    spread = jnp.mean(centre * centre, axis=-1, keepdims=True)
    inverse = lax.rsqrt(spread + EPSILON)
    return (centre * inverse, inverse)


def norm_back(delta, unit, inverse):
    return inverse * (
        delta
        - jnp.mean(delta, axis=-1, keepdims=True)
        - unit * jnp.mean(delta * unit, axis=-1, keepdims=True)
    )


def column_sum(values):
    return jnp.sum(values, axis=0, keepdims=True)


def feed_forward(hidden_low, expand, offsets, shrink, turned, active, slope, chunk, branch_ref):
    width = expand.shape[1]
    for at in range(width // chunk):
        part = pl.ds(at * chunk, chunk)
        before = dot(hidden_low, expand[:, part]) + offsets[:, part].astype(F32)
        share = 0.5 + 0.5 * lax.erf(before * (0.5**0.5))
        density = jnp.exp(-0.5 * (before * before)) * 0.3989422804014327
        active_part = (before * share).astype(BF16)
        active[:, part] = active_part
        slope[:, part] = (share + before * density).astype(BF16)
        product = dot_nt(active_part, shrink[:, part]) if turned else dot(active_part, shrink[part, :])
        if at == 0:
            branch_ref[...] = product
        else:
            branch_ref[...] += product


def prepare_kernel(text_rows, layout_rows, segments, project, offsets_t, offsets_l, joined, padded, line_t, line_l):
    packs, width, rows = layout_rows.shape
    for pack in range(packs):
        marks = jnp.broadcast_to(segments[pack : pack + 1, :].astype(F32), (SLAB - width, rows))
        lines = jnp.concatenate([layout_rows[pack].astype(F32), marks], axis=0)
        joined[pack, :, :DT] = text_rows[pack]
        joined[pack, :, DT:] = lines.T.astype(BF16)
    line_t[...] = offsets_t[...].reshape(line_t.shape)
    line_l[...] = offsets_l[...].reshape(line_l.shape)
    padded[...] = jnp.zeros_like(padded)
    for third in range(3):
        padded[:, third * SLAB : third * SLAB + DL] = project[:, third * DL : (third + 1) * DL]


def prepare_call(text_rows, layout_rows, segments, project, offsets_t, offsets_l):
    packs, rows, unused = text_rows.shape
    return pl.pallas_call(
        prepare_kernel,
        out_shape=(
            shape_of((packs, rows, DT + SLAB), BF16),
            shape_of((DL, 3 * SLAB), BF16),
            shape_of((1, FT), BF16),
            shape_of((1, FL), BF16),
        ),
        in_specs=[VMEM] * 6,
        out_specs=[VMEM] * 4,
        compiler_params=pltpu.CompilerParams(vmem_limit_bytes=LIMIT),
        cost_estimate=COST,
        name="prepare",
    )(text_rows, layout_rows, segments, project, offsets_t, offsets_l)


def forward_kernel(
    packs,
    rows,
    dp_size,
    subs,
    x0,
    x1,
    x2,
    x3,
    wt_in,
    wl_in,
    mt_in,
    et_in,
    st_in,
    ml,
    el,
    sl,
    cot_t,
    cot_l,
    bt,
    gt,
    ot,
    bl,
    gl,
    ol,
    res_t_out,
    res_l_out,
    q_t_out,
    q_l_out,
    kt_out,
    kl_out,
    vt_out,
    vl_out,
    p_out,
    ctx_t_out,
    ctx_l_out,
    hid_t_out,
    unit_t_out,
    inv_t_out,
    sum_t_out,
    slope_t_out,
    hid_l_out,
    unit_l_out,
    inv_l_out,
    sum_l_out,
    slope_l_out,
    act_l_out,
    sv_t_out,
    sv_l_out,
    *rest,
):
    targets, rest = rest[: 2 * len(subs)], rest[2 * len(subs) :]
    (
        xs,
        res_t,
        res_l,
        q_t,
        q_l,
        ctx_t,
        ctx_l,
        hid_t,
        unit_t,
        inv_t,
        sum_t,
        slope_t,
        hid_l,
        unit_l,
        inv_l,
        sum_l,
        slope_l,
        act_l,
        sv_t,
        sv_l,
        layout_bias_ref,
        wt,
        wl,
        mt,
        et,
        st,
        k_t,
        k_l,
        v_t,
        v_l,
        prob,
        bias,
        act_t,
        turned,
        branch_t,
        branch_l,
        grads,
        sems,
    ) = rest
    blocks = (x0, x1, x2, x3)
    keys = rows * len(blocks)
    tokens = packs * rows
    x_copies = copies_of(
        gather_pairs(blocks, rows, packs, xs), sems, 0
    )
    base = len(x_copies)
    w_copies = copies_of(((wt_in, wt), (wl_in, wl)), sems, base)
    base += 2
    pending = []

    def emit(*pairs):
        pending.extend(copies_of(pairs, sems, base + len(pending)))

    text_bias = bt[...].astype(F32)
    layout_bias_ref[...] = jnp.zeros_like(layout_bias_ref)
    layout_bias_ref[:, :DL] = bl[...].astype(F32)
    layout_bias = layout_bias_ref[...]
    wait_all(x_copies)
    wait_all(w_copies)
    w_copies = copies_of(((mt_in, mt), (et_in, et), (st_in, st)), sems, base)
    base += 3

    for pack in range(packs):
        own = pl.ds(pack * keys, rows)
        mine = pl.ds(pack * rows, rows)
        q_t[mine, :] = (dot(xs[own, :DT], wt[:, :DT]) + text_bias[0:1, :]).astype(BF16) * 0.125
        q_l[mine, :] = (dot(xs[own, DT : DT + DL], wl[:, :SLAB]) + layout_bias[0:1, :]).astype(BF16) * 0.25

    step = 256

    def key_rows(at, unused):
        span = pl.ds(pl.multiple_of(at * step, step), step)
        k_t[span, :] = dot(xs[span, :DT], wt[:, DT : 2 * DT]).astype(BF16)
        v_t[span, :] = (dot(xs[span, :DT], wt[:, 2 * DT :]) + text_bias[1:2, :]).astype(BF16)
        k_l[span, :] = dot(xs[span, DT : DT + DL], wl[:, SLAB : 2 * SLAB]).astype(BF16)
        v_l[span, :] = (dot(xs[span, DT : DT + DL], wl[:, 2 * SLAB :]) + layout_bias[1:2, :]).astype(BF16)
        return unused

    lax.fori_loop(0, packs * keys // step, key_rows, 0)
    emit((k_t, kt_out), (k_l, kl_out), (v_t, vt_out), (v_l, vl_out), (q_t, q_t_out), (q_l, q_l_out))

    marks = lax.broadcasted_iota(jnp.int32, (1, LANES), 1) - 64
    for pack in range(packs):
        slab = xs[pl.ds(pack * keys, keys), DT + LANES : DT + 2 * LANES].astype(F32)
        hot = jnp.where((slab == marks.astype(F32)) & (marks >= 0) & (marks < 16), 1.0, 0.0).astype(BF16)
        same = dot_nt(hot[:rows], hot)
        bias[pack] = jnp.where(same > 0.5, 0.0, MASKED)

    ctx_l[...] = jnp.zeros_like(ctx_l)

    def head_pair(pair_at, unused):
        masks = lane_masks(pair_at)
        text_lanes = pl.ds(pl.multiple_of(pair_at * LANES, LANES), LANES)
        layout_lanes = pl.ds(pl.multiple_of(pair_at // 4 * LANES, LANES), LANES)
        for pack in range(packs):
            mine = pl.ds(pack * rows, rows)
            span = pl.ds(pack * keys, keys)
            queries = stacked_heads(q_t[mine, text_lanes], q_l[mine, layout_lanes], masks)
            both_keys = jnp.concatenate([k_t[span, text_lanes], k_l[span, layout_lanes]], axis=1)
            both_values = jnp.concatenate([v_t[span, text_lanes], v_l[span, layout_lanes]], axis=1)
            allowed = bias[pack]
            logit = dot_nt(queries, both_keys) + jnp.concatenate([allowed, allowed], axis=0)
            raised = jnp.exp(logit - jnp.max(logit, axis=1, keepdims=True))
            low = (raised * (1.0 / jnp.sum(raised, axis=1, keepdims=True))).astype(BF16)
            prob[pair_at, pack] = low
            mixed = dot(low, both_values).astype(BF16)
            ctx_t[mine, text_lanes] = jnp.where(masks[0], mixed[:rows, :LANES], mixed[rows:, :LANES])
            kept = ctx_l[mine, layout_lanes]
            kept = jnp.where(masks[1], mixed[:rows, LANES:], kept)
            ctx_l[mine, layout_lanes] = jnp.where(masks[2], mixed[rows:, LANES:], kept)
        return unused

    lax.fori_loop(0, HEADS // 2, head_pair, 0, unroll=UNROLL)
    emit((prob, p_out), (ctx_t, ctx_t_out), (ctx_l, ctx_l_out))
    wait_all(w_copies)

    def own_rows(lanes):
        return jnp.concatenate(
            [xs[pl.ds(pack * keys, rows), lanes].astype(F32) for pack in range(packs)], axis=0
        )

    def tail(x, attended, expand, offsets, shrink, turned, b, g, cotangent, active, slope, branch, chunk, hid, unit, inv, delta, sv, outs):
        width = x.shape[1]
        middle = x + attended + b[2:3, :width]
        unit_first, inverse_first = normalized(middle)
        hidden = unit_first * g[0:1, :] + b[3:4, :width]
        hidden_low = hidden.astype(BF16)
        hid[...] = hidden_low
        unit[...] = unit_first
        inv[...] = inverse_first
        emit((hid, outs[0]), (unit, outs[1]), (inv, outs[2]))
        feed_forward(hidden_low, expand, offsets, shrink, turned, active, slope, chunk, branch)
        emit((slope, outs[3]))
        unit_second, inverse_second = normalized(hidden + branch[...] + b[4:5, :width])
        result = unit_second * g[1:2, :] + b[5:6, :width]
        sv[1:2, :] = column_sum(cotangent)
        sv[2:3, :] = column_sum(cotangent * unit_second)
        sum_delta = norm_back(cotangent * g[1:2, :], unit_second, inverse_second)
        delta[...] = sum_delta
        emit((delta, outs[4]))
        rounded = sum_delta.astype(BF16).astype(F32)
        sv[0:1, :] = column_sum(rounded)
        emit((sv, outs[5]))
        return result, rounded

    result, rounded = tail(
        own_rows(slice(0, DT)), dot(ctx_t[...], mt[...]), et, ot, st, False, text_bias, gt[...].astype(F32),
        jnp.concatenate([cot_t[pack] for pack in range(packs)], axis=0).astype(F32),
        act_t, slope_t, branch_t, 512, hid_t, unit_t, inv_t, sum_t, sv_t,
        (hid_t_out, unit_t_out, inv_t_out, slope_t_out, sum_t_out, sv_t_out),
    )
    res_t[...] = result.astype(BF16)
    emit((res_t, res_t_out))
    turned[...] = rounded.T.astype(BF16)
    share = DT // 4
    for shard in range(4):
        own = turned[shard * share : (shard + 1) * share, :]
        for block in range(FT // DT):
            grads[shard, pl.ds(block * share, share), :] = dot(
                own, act_t[:, block * DT : (block + 1) * DT]
            ).astype(BF16)
    if grads.shape[1] > S_ROWS:
        grads[:, S_ROWS:, :] = jnp.zeros((4, grads.shape[1] - S_ROWS, DT), BF16)
    emit(*in_lines(grads, subs, dp_size, targets))
    result, unused = tail(
        own_rows(slice(DT, DT + DL)), dot(ctx_l[:, :DL], ml[...]), el, ol, sl, True, layout_bias,
        gl[...].astype(F32),
        jnp.concatenate([cot_l[pack].astype(F32).T for pack in range(packs)], axis=0),
        act_l, slope_l, branch_l, 256, hid_l, unit_l, inv_l, sum_l, sv_l,
        (hid_l_out, unit_l_out, inv_l_out, slope_l_out, sum_l_out, sv_l_out),
    )
    for pack in range(packs):
        res_l[pack] = result[pack * rows : (pack + 1) * rows, :].T.astype(BF16)
    emit((res_l, res_l_out), (act_l, act_l_out))
    wait_all(pending)


def forward_call(blocks, wt, wl, mt, et, st, ml, el, sl, cot_t, cot_l, bt, gt, ot, bl, gl, ol, packs, rows, dp_size, subs):
    tokens = packs * rows
    lines = total_lines(subs)
    every = tokens * len(blocks)
    keys = rows * len(blocks)
    pairs = HEADS // 2
    outs = (
        shape_of((tokens, DT), BF16),
        shape_of((packs, DL, rows), BF16),
        shape_of((tokens, DT), BF16),
        shape_of((tokens, SLAB), BF16),
        shape_of((every, DT), BF16),
        shape_of((every, SLAB), BF16),
        shape_of((every, DT), BF16),
        shape_of((every, SLAB), BF16),
        shape_of((pairs, packs, 2 * rows, keys), BF16),
        shape_of((tokens, DT), BF16),
        shape_of((tokens, SLAB), BF16),
        shape_of((tokens, DT), BF16),
        shape_of((tokens, DT), F32),
        shape_of((tokens, 1), F32),
        shape_of((tokens, DT), F32),
        shape_of((tokens, FT), BF16),
        shape_of((tokens, DL), BF16),
        shape_of((tokens, DL), F32),
        shape_of((tokens, 1), F32),
        shape_of((tokens, DL), F32),
        shape_of((tokens, FL), BF16),
        shape_of((tokens, FL), BF16),
        shape_of((8, DT), F32),
        shape_of((8, DL), F32),
    ) + pair_shapes(subs)
    out_specs = [ANY] * len(outs)
    kept = (0, 1, 2, 3, 9, 10) + tuple(range(11, 24))
    scratch = [
        pltpu.VMEM((every, DT + SLAB), BF16),
        *(pltpu.VMEM(outs[at].shape, outs[at].dtype) for at in kept),
        pltpu.VMEM((6, SLAB), F32),
        pltpu.VMEM(wt.shape, BF16),
        pltpu.VMEM(wl.shape, BF16),
        pltpu.VMEM(mt.shape, BF16),
        pltpu.VMEM(et.shape, BF16),
        pltpu.VMEM(st.shape, BF16),
        pltpu.VMEM((every, DT), BF16),
        pltpu.VMEM((every, SLAB), BF16),
        pltpu.VMEM((every, DT), BF16),
        pltpu.VMEM((every, SLAB), BF16),
        pltpu.VMEM((pairs, packs, 2 * rows, keys), BF16),
        pltpu.VMEM((packs, rows, keys), F32),
        pltpu.VMEM((tokens, FT), BF16),
        pltpu.VMEM((DT, tokens), BF16),
        pltpu.VMEM((tokens, DT), F32),
        pltpu.VMEM((tokens, DL), F32),
        pltpu.VMEM((4, lines, DT), BF16),
        pltpu.SemaphoreType.DMA((48 + 4 * dp_size * len(subs),)),
    ]
    return pl.pallas_call(
        functools.partial(forward_kernel, packs, rows, dp_size, subs),
        out_shape=outs,
        in_specs=[ANY] * 9 + [VMEM] * 11,
        out_specs=out_specs,
        scratch_shapes=scratch,
        compiler_params=pltpu.CompilerParams(vmem_limit_bytes=FIRST),
        cost_estimate=COST,
        name="forward",
    )(*blocks, wt, wl, mt, et, st, ml, el, sl, cot_t, cot_l, bt, gt, ot, bl, gl, ol)


def middle_kernel(
    dp_size,
    subs,
    hid_t_in,
    unit_t_in,
    inv_t_in,
    sum_t_in,
    slope_t_in,
    hid_l,
    unit_l,
    inv_l,
    sum_l,
    slope_l,
    act_l,
    ctx_t_in,
    ctx_l,
    st_in,
    et_in,
    mt_in,
    sl,
    el,
    ml,
    gt,
    gl,
    after,
    mid_t,
    mid_l,
    dctx_t,
    dctx_l,
    sv_t,
    sv_l,
    so_t,
    so_l,
    *rest,
):
    targets, rest = rest[: 2 * len(subs)], rest[2 * len(subs) :]
    (
        hid_t,
        unit_t,
        inv_t,
        sum_t,
        slope_t,
        ctx_t,
        st,
        et,
        mt,
        before_t,
        before_l,
        turned,
        grads,
        sems,
    ) = rest
    w_copies = copies_of(
        (
            (sum_t_in, sum_t), (st_in, st), (slope_t_in, slope_t), (hid_t_in, hid_t), (et_in, et),
            (unit_t_in, unit_t), (inv_t_in, inv_t), (ctx_t_in, ctx_t), (mt_in, mt),
        ),
        sems,
        0,
    )
    base = len(w_copies)

    def feed_back(branch_delta, shrink, turned, slope, before, so, chunk):
        for at in range(slope.shape[1] // chunk):
            part = pl.ds(at * chunk, chunk)
            if turned:
                active_delta = dot(branch_delta, shrink[:, part])
            else:
                active_delta = dot_nt(branch_delta, shrink[part, :])
            low = (active_delta * slope[:, part].astype(F32)).astype(BF16)
            before[:, part] = low
            so[:, part] = column_sum(low.astype(F32))

    def front(hidden_delta, total, unit, inv, g, merge, sv):
        delta = total[...] + hidden_delta
        sv[0:1, :] = column_sum(delta * unit[...])
        sv[1:2, :] = column_sum(delta)
        middle = norm_back(delta * g, unit[...], inv[...])
        low = middle.astype(BF16)
        rounded = low.astype(F32)
        sv[2:3, :] = column_sum(rounded)
        back = dot_nt(low, merge).astype(BF16)
        sv[3:4, :] = column_sum(back.astype(F32))
        return middle, rounded.T.astype(BF16), back

    layout_delta = sum_l[...].astype(BF16)
    feed_back(layout_delta, sl, True, slope_l, before_l, so_l, 256)
    turned_l = before_l[...].astype(F32).T.astype(BF16)
    grown_l = dot(turned_l, hid_l[...]).astype(BF16)
    shrunk_l = dot(layout_delta.astype(F32).T.astype(BF16), act_l[...]).astype(BF16)
    middle, low_turned, back = front(
        dot_nt(before_l[...], el[...]), sum_l, unit_l, inv_l, gl[0:1, :].astype(F32), ml[...], sv_l
    )
    for pack in range(mid_l.shape[0]):
        size = mid_l.shape[2]
        mid_l[pack] = middle[pack * size : (pack + 1) * size, :].T
    dctx_l[...] = jnp.zeros_like(dctx_l)
    dctx_l[:, :DL] = back
    merged_l = dot(low_turned, ctx_l[...]).astype(BF16)
    wait_all(w_copies[:3])
    feed_back(sum_t[...].astype(BF16), st, False, slope_t, before_t, so_t, 512)
    wait_all(w_copies[3:4])
    turned[...] = hid_t[...].astype(F32).T.astype(BF16)
    for shard in range(4):
        grads[shard, pl.ds(0, DT), :] = dot(
            turned[...], before_t[:, shard * DT : (shard + 1) * DT]
        ).astype(BF16)
    early = copies_of(in_lines(grads, subs, dp_size, targets, 0, DT), sems, base)
    base += len(early)
    wait_all(w_copies[4:])
    middle, low_turned, back = front(
        dot_nt(before_t[...], et[...]), sum_t, unit_t, inv_t, gt[0:1, :].astype(F32), mt[...], sv_t
    )
    mid_t[...] = middle
    dctx_t[...] = back
    for shard in range(4):
        grads[shard, pl.ds(DT, 192), :] = dot(
            low_turned[shard * 192 : (shard + 1) * 192, :], ctx_t[...]
        ).astype(BF16)
    for shard in range(4):
        grads[shard, 960:, :] = jnp.zeros((grads.shape[1] - 960, DT), BF16)
        for at in range(3):
            lanes = slice(at * SLAB, at * SLAB + DL)
            line = shard * DL + at * 64
            grads[shard, 960:1024, lanes] = grown_l[line : line + 64, :]
            line = shard * 48 + at * 16
            grads[shard, 1072:1088, at * SLAB : (at + 1) * SLAB] = merged_l[line : line + 16, :]
        grads[shard, 1024:1072, :] = shrunk_l[shard * 48 : shard * 48 + 48, :]
    wait_all(copies_of(in_lines(grads, subs, dp_size, targets, DT), sems, base))
    wait_all(early)


def middle_call(operands, packs, rows, dp_size, subs):
    tokens = packs * rows
    lines = total_lines(subs)
    outs = (
        shape_of((tokens, DT), F32),
        shape_of((packs, DL, rows), F32),
        shape_of((tokens, DT), BF16),
        shape_of((tokens, SLAB), BF16),
        shape_of((8, DT), F32),
        shape_of((8, DL), F32),
        shape_of((1, FT), F32),
        shape_of((1, FL), F32),
    ) + pair_shapes(subs)
    scratch = [
        *(pltpu.VMEM(operands[at].shape, operands[at].dtype) for at in (0, 1, 2, 3, 4, 11)),
        pltpu.VMEM((FT, DT), BF16),
        pltpu.VMEM((DT, FT), BF16),
        pltpu.VMEM((DT, DT), BF16),
        pltpu.VMEM((tokens, FT), BF16),
        pltpu.VMEM((tokens, FL), BF16),
        pltpu.VMEM((DT, tokens), BF16),
        pltpu.VMEM((4, lines, DT), BF16),
        pltpu.SemaphoreType.DMA((16 + 4 * dp_size * len(subs),)),
    ]
    return pl.pallas_call(
        functools.partial(middle_kernel, dp_size, subs),
        out_shape=outs,
        in_specs=[ANY] * 5 + [VMEM] * 6 + [ANY, VMEM] + [ANY] * 3 + [VMEM] * 5 + [ANY],
        out_specs=[VMEM] * 8 + [ANY] * (2 * len(subs)),
        scratch_shapes=scratch,
        compiler_params=pltpu.CompilerParams(vmem_limit_bytes=SECOND),
        cost_estimate=COST,
        name="middle",
    )(*operands)


def attention_kernel(
    packs,
    rows,
    dp_size,
    subs,
    x0,
    x1,
    x2,
    x3,
    kt_in,
    kl_in,
    vt_in,
    vl_in,
    p_in,
    q_t,
    q_l,
    dctx_t,
    dctx_l,
    ctx_t,
    ctx_l,
    sf_t,
    sf_l,
    sm_t,
    sm_l,
    so_t,
    so_l,
    after,
    joined_t_out,
    joined_l_out,
    query_t_out,
    query_l_out,
    *rest,
):
    targets, rest = rest[: 2 * len(subs)], rest[2 * len(subs) :]
    (
        xs,
        joined_t,
        joined_l,
        query_t,
        query_l,
        k_t,
        k_l,
        v_t,
        v_l,
        prob,
        dq_t,
        dq_l,
        dk_l,
        dv_l,
        layout_grads,
        grads,
        smalls,
        sems,
    ) = rest
    blocks = (x0, x1, x2, x3)
    keys = rows * len(blocks)
    kv_copies = copies_of(((kt_in, k_t), (vt_in, v_t), (kl_in, k_l), (vl_in, v_l)), sems, 0)

    def chances(at):
        return pltpu.make_async_copy(p_in.at[at], prob.at[at], sems.at[4 + at])

    for at in range(HEADS // 2):
        chances(at).start()
    base = 4 + HEADS // 2
    dq_l[...] = jnp.zeros_like(dq_l)
    dk_l[...] = jnp.zeros_like(dk_l)
    dv_l[...] = jnp.zeros_like(dv_l)
    wait_all(kv_copies)
    x_copies = copies_of(gather_pairs(blocks, rows, packs, xs), sems, base)
    base += len(x_copies)

    def head_pair(pair_at, unused):
        chances(pair_at).wait()
        masks = lane_masks(pair_at)
        text_lanes = pl.ds(pl.multiple_of(pair_at * LANES, LANES), LANES)
        layout_lanes = pl.ds(pl.multiple_of(pair_at // 4 * LANES, LANES), LANES)
        for pack in range(packs):
            mine = pl.ds(pack * rows, rows)
            span = pl.ds(pack * keys, keys)
            queries = stacked_heads(q_t[mine, text_lanes], q_l[mine, layout_lanes], masks)
            deltas = stacked_heads(dctx_t[mine, text_lanes], dctx_l[mine, layout_lanes], masks)
            one = jnp.concatenate([ctx_t[mine, text_lanes], ctx_l[mine, layout_lanes]], axis=1)
            contexts = jnp.concatenate([one, one], axis=0).astype(F32)
            products = deltas.astype(F32) * contexts
            layout_mean = jnp.sum(products[:, LANES:], axis=1, keepdims=True)
            both_mean = jnp.sum(products, axis=1, keepdims=True)
            text_values = v_t[span, text_lanes]
            layout_values = v_l[span, layout_lanes]
            both_values = jnp.concatenate([text_values, layout_values], axis=1)
            low = prob[pair_at, pack]
            chance = low.astype(F32)
            both_change = (chance * (dot_nt(deltas, both_values) - both_mean)).astype(BF16)
            layout_change = (
                chance * (dot_nt(deltas[:, LANES:], layout_values) - layout_mean)
            ).astype(BF16)
            from_text = dot(both_change, k_t[span, text_lanes])
            dq_t[mine, text_lanes] = (
                jnp.where(masks[0], from_text[:rows], from_text[rows:]) * 0.125
            ).astype(BF16)
            from_layout = dot(layout_change, k_l[span, layout_lanes]) * 0.25
            kept = dq_l[mine, layout_lanes]
            kept = jnp.where(masks[1], from_layout[:rows], kept)
            dq_l[mine, layout_lanes] = jnp.where(masks[2], from_layout[rows:], kept)
            turned_queries = queries.T
            turned_deltas = deltas.T
            joined_t[text_lanes, span] = dot(turned_queries[:LANES], both_change).astype(BF16)
            dk_l[layout_lanes, span] += dot(turned_queries[LANES:], layout_change)
            value_change = dot(turned_deltas, low)
            text_at = pl.ds(pl.multiple_of(pair_at * LANES + DT, LANES), LANES)
            joined_t[text_at, span] = value_change[:LANES].astype(BF16)
            dv_l[layout_lanes, span] += value_change[LANES:]
        return unused

    lax.fori_loop(0, HEADS // 2, head_pair, 0, unroll=UNROLL_BACK)
    joined_l[:SLAB, :] = dk_l[...].astype(BF16)
    joined_l[SLAB:, :] = dv_l[...].astype(BF16)
    whole_t = dq_t[...].astype(F32)
    whole_l = dq_l[...]
    low_l = whole_l.astype(BF16)
    query_t[...] = whole_t.T.astype(BF16)
    query_l[...] = whole_l.T.astype(BF16)
    out_copies = copies_of(
        ((joined_t, joined_t_out), (joined_l, joined_l_out), (query_t, query_t_out), (query_l, query_l_out)),
        sems,
        base,
    )
    base += 4
    wait_all(x_copies)
    own = jnp.concatenate([xs[pl.ds(pack * keys, rows), :] for pack in range(packs)], axis=0)
    step = 192
    for at in range(3 * DT // step):
        shard, line = at // 3, at % 3 * step
        if at < DT // step:
            product = dot(query_t[at * step : (at + 1) * step, :], own[:, :DT])
        else:
            product = dot(joined_t[at * step - DT : (at + 1) * step - DT, :], xs[:, :DT])
        grads[shard, line : line + step, :] = product.astype(BF16)
    layout_grads[:DL, :] = dot(query_l[:DL, :], own[:, DT:]).astype(BF16)
    layout_grads[DL : 2 * DL, :] = dot(joined_l[:DL, :], xs[:, DT:]).astype(BF16)
    layout_grads[2 * DL :, :] = dot(joined_l[SLAB : SLAB + DL, :], xs[:, DT:]).astype(BF16)
    text_lines = jnp.concatenate(
        [column_sum(whole_t), sm_t[3:4, :], sm_t[2:3, :], sm_t[1:2, :], sf_t[0:2, :], sm_t[0:1, :], sf_t[2:3, :]],
        axis=0,
    )
    layout_lines = jnp.concatenate(
        [
            column_sum(low_l.astype(F32))[:, :DL],
            sm_l[3:4, :], sm_l[2:3, :], sm_l[1:2, :], sf_l[0:2, :], sm_l[0:1, :], sf_l[2:3, :],
        ],
        axis=0,
    )
    for shard in range(4):
        for at in range(3):
            line = shard * 144 + at * 48
            grads[shard, 576:624, at * SLAB : (at + 1) * SLAB] = layout_grads[line : line + 48, :]
        smalls[...] = jnp.zeros_like(smalls)
        share = DT // 4
        smalls[0:8, 0:share] = text_lines[:, shard * share : (shard + 1) * share]
        smalls[8:9, :] = so_t[:, shard * DT : (shard + 1) * DT]
        share = DL // 4
        smalls[0:8, SLAB : SLAB + share] = layout_lines[:, shard * share : (shard + 1) * share]
        share = FL // 4
        smalls[9:10, 0:share] = so_l[:, shard * share : (shard + 1) * share]
        grads[shard, 624:640, :] = smalls[...].astype(BF16)
        if grads.shape[1] > P_ROWS:
            grads[shard, P_ROWS:, :] = jnp.zeros((grads.shape[1] - P_ROWS, DT), BF16)
    wait_all(copies_of(in_lines(grads, subs, dp_size, targets), sems, base))
    wait_all(out_copies)


def attention_call(operands, packs, rows, dp_size, subs):
    tokens = packs * rows
    every = tokens * 4
    lines = total_lines(subs)
    pairs = HEADS // 2
    outs = (
        shape_of((2 * DT, every), BF16),
        shape_of((2 * SLAB, every), BF16),
        shape_of((DT, tokens), BF16),
        shape_of((SLAB, tokens), BF16),
    ) + pair_shapes(subs)
    scratch = [
        pltpu.VMEM((every, DT + SLAB), BF16),
        *(pltpu.VMEM(outs[at].shape, outs[at].dtype) for at in range(4)),
        pltpu.VMEM((every, DT), BF16),
        pltpu.VMEM((every, SLAB), BF16),
        pltpu.VMEM((every, DT), BF16),
        pltpu.VMEM((every, SLAB), BF16),
        pltpu.VMEM((pairs, packs, 2 * rows, 4 * rows), BF16),
        pltpu.VMEM((tokens, DT), BF16),
        pltpu.VMEM((tokens, SLAB), F32),
        pltpu.VMEM((SLAB, every), F32),
        pltpu.VMEM((SLAB, every), F32),
        pltpu.VMEM((3 * DL, SLAB), BF16),
        pltpu.VMEM((4, lines, DT), BF16),
        pltpu.VMEM((16, DT), F32),
        pltpu.SemaphoreType.DMA((32 + 4 * dp_size * len(subs),)),
    ]
    return pl.pallas_call(
        functools.partial(attention_kernel, packs, rows, dp_size, subs),
        out_shape=outs,
        in_specs=[ANY] * 9 + [VMEM] * 12 + [ANY],
        out_specs=[ANY] * len(outs),
        scratch_shapes=scratch,
        compiler_params=pltpu.CompilerParams(vmem_limit_bytes=LAST),
        cost_estimate=COST,
        name="attention_back",
    )(*operands)


def input_kernel(
    packs, rows, joined_in, joined_l, query_t, query_l, wt_in, wl, after, give, hold, mark, joined_t, wt, totals, sums, sems
):
    keys = joined_t.shape[1] // packs
    pairs = []
    for third in (1, 2):
        lanes = pl.ds(third * DT, DT)
        lines = pl.ds((third - 1) * DT, DT)
        pairs += [(wt_in.at[:, lanes], wt.at[:, lanes]), (joined_in.at[lines, :], joined_t.at[lines, :])]
    pairs.append((wt_in.at[:, pl.ds(0, DT)], wt.at[:, pl.ds(0, DT)]))
    copies = copies_of(pairs, sems, 0)

    def tokens_of(ref, lines, at):
        spans = [slice(pack * keys + at * rows, pack * keys + (at + 1) * rows) for pack in range(packs)]
        return jnp.concatenate([ref[lines, span] for span in spans], axis=1)

    everything = slice(None)
    for at in range(4):
        sums[at, DT:, :] = dot(wl[:, SLAB:], tokens_of(joined_l, everything, at)).astype(BF16)
    layout_own = dot(wl[:, :SLAB], query_l[...])
    sums[0, DT:, :] = (sums[0, DT:, :].astype(F32) + layout_own).astype(BF16)
    mark[...] = layout_own[:8, :LANES]
    wait_all(copies[:2])
    for at in range(4):
        totals[at] = dot(wt[:, DT : 2 * DT], tokens_of(joined_t, slice(0, DT), at))
    wait_all(copies[2:])
    out = []
    for at in (3, 1, 2, 0):
        total = totals[at] + dot(wt[:, 2 * DT :], tokens_of(joined_t, slice(DT, 2 * DT), at))
        if at == 0:
            total += dot(wt[:, :DT], query_t[...])
        sums[at, :DT, :] = total.astype(BF16)
        target = (hold, give)[at % 2].at[at // 2]
        out += copies_of(((sums.at[at], target),), sems, 5 + at)
    wait_all(out)


def input_call(joined_t, joined_l, query_t, query_l, wt, wl, after, packs, rows):
    tokens = packs * rows
    return pl.pallas_call(
        functools.partial(input_kernel, packs, rows),
        out_shape=(shape_of((2, DT + DL, tokens), BF16),) * 2 + (shape_of((8, LANES), F32),),
        in_specs=[ANY] + [VMEM] * 3 + [ANY, VMEM, after[1]],
        out_specs=[ANY] * 2 + [VMEM],
        scratch_shapes=[
            pltpu.VMEM(joined_t.shape, BF16),
            pltpu.VMEM(wt.shape, BF16),
            pltpu.VMEM((4, DT, tokens), F32),
            pltpu.VMEM((4, DT + DL, tokens), BF16),
            pltpu.SemaphoreType.DMA((9,)),
        ],
        compiler_params=pltpu.CompilerParams(vmem_limit_bytes=LIMIT),
        cost_estimate=COST,
        name="input_back",
    )(joined_t, joined_l, query_t, query_l, wt, wl, after[0])


def sensitivity_kernel(own, far, mid_t, mid_l, after, out_t, out_l, mark):
    mark[...] = mid_t[:8, :LANES]
    total = own[...].astype(F32) + far[...].astype(F32)
    out_t[...] = mid_t[...] + total[:DT, :].T
    packs, unused, rows = mid_l.shape
    for pack in range(packs):
        out_l[pack] = mid_l[pack] + total[DT:, pack * rows : (pack + 1) * rows]


def sensitivity_call(own, far, mid_t, mid_l, after):
    return pl.pallas_call(
        sensitivity_kernel,
        out_shape=(shape_of(mid_t.shape, F32), shape_of(mid_l.shape, F32), shape_of((8, LANES), F32)),
        in_specs=[VMEM] * 4 + [after[1]],
        out_specs=[VMEM] * 3,
        compiler_params=pltpu.CompilerParams(vmem_limit_bytes=SMALL),
        cost_estimate=COST,
        name="sensitivity",
    )(own, far, mid_t, mid_l, after[0])


def lines_in_order(dp_size, sources, subs, whole):
    device = lax.axis_index("dp")
    for at, (first, rows, hops, growth) in enumerate(subs):
        half, other = sources[2 * at : 2 * at + 2]
        size = rows // dp_size
        for index in range(dp_size):
            line = position(growth[::-1], 0, index) * size
            source = half if line < rows // 2 else other
            line = line % (rows // 2)
            mark = pl.multiple_of(first + jnp.bitwise_xor(device, index) * size, 16)
            whole[pl.ds(mark, size), :] = source[line : line + size, :].astype(F32)


def shrink_store(whole, out):
    share = DT // 4
    for block in range(FT // DT):
        out[:, block * DT : (block + 1) * DT] = whole[block * share : (block + 1) * share, :]


def expand_store(whole, out, out_merge, out_grow, out_shrink, out_layout_merge):
    out[...] = whole[:DT, :]
    out_merge[...] = whole[DT:960, :]
    grown = jnp.concatenate(
        [whole[960:1024, at * SLAB : at * SLAB + DL] for at in range(3)], axis=0
    )
    out_grow[...] = grown.T
    out_shrink[...] = whole[1024:1072, :]
    out_layout_merge[...] = jnp.concatenate(
        [whole[1072:1088, at * SLAB : at * SLAB + DL] for at in range(3)], axis=0
    )


def project_store(whole, out, out_layout, biases_t, gains_t, offsets_t, biases_l, gains_l, offsets_l):
    out[...] = whole[:576, :]
    out_layout[...] = jnp.concatenate(
        [whole[576:624, at * SLAB : at * SLAB + DL] for at in range(3)], axis=0
    )
    biases_t[...] = whole[624:630, : DT // 4]
    gains_t[...] = whole[630:632, : DT // 4]
    offsets_t[...] = whole[632:633, :].reshape(DT)
    biases_l[...] = whole[624:630, SLAB : SLAB + DL // 4]
    gains_l[...] = whole[630:632, SLAB : SLAB + DL // 4]
    offsets_l[...] = whole[633:634, : FL // 4].reshape(FL // 4)


def final_kernel(store, dp_size, subs, *refs):
    sources, outs, whole = refs[: 2 * len(subs)], refs[2 * len(subs) + 1 : -1], refs[-1]
    lines_in_order(dp_size, sources, subs, whole)
    store(whole, *outs[:-1])
    outs[-1][...] = whole[:8, :LANES]


def final_call(store, name, sources, after, dp_size, subs, outs):
    return pl.pallas_call(
        functools.partial(final_kernel, store, dp_size, subs),
        out_shape=tuple(shape_of(shape, F32) for shape in outs) + (shape_of((8, LANES), F32),),
        in_specs=[VMEM] * len(sources) + [after[1]],
        out_specs=[VMEM] * (len(outs) + 1),
        scratch_shapes=[pltpu.VMEM((total_lines(subs), DT), F32)],
        compiler_params=pltpu.CompilerParams(vmem_limit_bytes=SMALL),
        cost_estimate=COST,
        name=name,
    )(*sources, after[0])


def add_kernel(count, parts, *refs):
    sources, targets = refs[: count * parts], refs[count * parts + 1 :]
    for at, target in enumerate(targets):
        total = sources[at][...].astype(F32)
        for n in range(1, count):
            total += sources[n * parts + at][...].astype(F32)
        target[...] = total.astype(BF16)


def add_call(sources, parts, after):
    lines, width = sources[0].shape
    size = lines // parts
    steps = max(n for n in (1, 2, 3, 4) if size % (16 * n) == 0 and (n == 1 or lines // n >= 256))
    block = size // steps
    specs = [
        pl.BlockSpec((block, width), functools.partial(lambda at, i: (at * steps + i, 0), at))
        for unused in sources
        for at in range(parts)
    ]
    return pl.pallas_call(
        functools.partial(add_kernel, len(sources), parts),
        grid=(steps,),
        out_shape=(shape_of((size, width), BF16),) * parts,
        in_specs=specs + [after[1]],
        out_specs=[pl.BlockSpec((block, width), lambda i: (i, 0))] * parts,
        compiler_params=pltpu.CompilerParams(vmem_limit_bytes=SMALL),
        cost_estimate=COST,
        name="add",
    )(*[source for source in sources for unused in range(parts)], after[0])


def gate_call(arrays, after):
    count = len(arrays)
    return pl.pallas_call(
        lambda *refs: None,
        out_shape=tuple(shape_of(array.shape, array.dtype) for array in arrays),
        in_specs=[ANY] * count + [after[1]],
        out_specs=[ANY] * count,
        input_output_aliases={at: at for at in range(count)},
        compiler_params=pltpu.CompilerParams(vmem_limit_bytes=SMALL),
        cost_estimate=COST,
        name="gate",
    )(*arrays, after[0])


def join_kernel(count, *refs):
    sources, target = refs[:count], refs[-1]
    size = sources[0].shape[0]
    for at, source in enumerate(sources):
        target[at * size : (at + 1) * size, :] = source[...]


def join_call(sources, after):
    lines, width = sources[0].shape
    return pl.pallas_call(
        functools.partial(join_kernel, len(sources)),
        out_shape=shape_of((len(sources) * lines, width), BF16),
        in_specs=[VMEM] * len(sources) + [after[1]],
        out_specs=VMEM,
        compiler_params=pltpu.CompilerParams(vmem_limit_bytes=SMALL),
        cost_estimate=COST,
        name="join",
    )(*sources, after[0])


def sent(array, group, index, seq_size, dp_size):
    across = other = 0
    for n, (axis, bit) in enumerate(group):
        if index & (1 << n):
            if axis == "seq":
                across |= bit
            else:
                other |= bit
    if not other:
        return lax.ppermute(array, "seq", [(at, at ^ across) for at in range(seq_size)])
    if not across:
        return lax.ppermute(array, "dp", [(at, at ^ other) for at in range(dp_size)])
    pairs = [
        (d * seq_size + s, (d ^ other) * seq_size + (s ^ across))
        for d in range(dp_size)
        for s in range(seq_size)
    ]
    return lax.ppermute(array, ("dp", "seq"), pairs)


def steps_of(give, hold, hops, growth, send):
    parts = [hold, send(give, (("seq", 1),), 1)]
    for group in hops:
        keep, *sends = yield functools.partial(add_call, parts, 1 << len(group))
        parts = [keep] + [send(array, group, at + 1) for at, array in enumerate(sends)]
    (piece,) = yield functools.partial(add_call, parts, 1)
    gathered = [piece]
    for group in growth:
        if len(gathered) > 1:
            piece = yield functools.partial(join_call, gathered)
        gathered = [piece] + [send(piece, group, at) for at in range(1, 1 << len(group))]
    return gathered


X = ("dp", 1)
Y = ("seq", 2)
Z1 = ("dp", 2)
Z2 = ("dp", 4)


def hops_of(text, extra):
    groups = {"x": (X,), "y": (Y,), "1": (Z1,), "2": (Z2,), "d": (Y, X), "z": (Z1, Z2)}
    return tuple(groups[letter] for letter in text) + extra


SPLIT_S = ((768, "y1x2B"), )
SPLIT_E = ((576, "1xy2B"), (576, "xyzB"), )
SPLIT_P = ((256, "xy12B"), (384, "yxzB"), )
ORDER = ('B', 'NE', 'S0', 'E1', 'E0', 'C', 'GP', 'E1', 'S0', 'E0', 'P0', 'P1', 'D', 'E1', 'S0', 'E0', 'GX', 'E1', 'X0', 'E0', 'E1', 'S0', 'P0', 'E0', 'FX', 'E1', 'S0', 'P0', 'E0', 'P0', 'P1', 'S0', 'P0', 'E0', 'P1', 'P0', 'S0', 'P0', 'P1', 'FE', 'P1', 'P1', 'FS', 'FP')


def local(
    dp_size,
    seq_size,
    text_input,
    layout_input,
    segments,
    text_cotangent,
    layout_cotangent,
    text_project,
    text_biases,
    text_gains,
    text_merge,
    text_expand,
    text_offsets,
    text_shrink,
    layout_project,
    layout_biases,
    layout_gains,
    layout_merge,
    layout_expand,
    layout_offsets,
    layout_shrink,
):
    packs, rows, unused = text_input.shape

    def send(array, group, index):
        return sent(array, group, index, seq_size, dp_size)

    core = (("seq", 1),)
    own, wl, line_t, line_l = prepare_call(
        text_input, layout_input.transpose(0, 2, 1), segments, layout_project, text_offsets, layout_offsets
    )
    far, near = send(own, (Y,), 1), send(own, core, 1)
    blocks = (own, near, far, send(far, core, 1))
    turned_shrink = layout_shrink.T

    bits = [1 << at for at in range((dp_size - 1).bit_length())]
    extra = tuple((("dp", bit),) for bit in bits[3:])
    growths = {
        "B": tuple(reversed(extra)) + ((Z2,), (Z1,), (X,)),
        "D": tuple(reversed(extra)) + ((Z1, Z2), (X,)),
    }
    subs = {
        name: sub_chunks(count, [(share, hops_of(text[:-1], extra), growths[text[-1]]) for share, text in split], dp_size)
        for name, count, split in (
            ("S", S_ROWS, SPLIT_S),
            ("E", E_ROWS, SPLIT_E),
            ("P", P_ROWS, SPLIT_P),
        )
    }
    reductions = {}
    calls = {}
    halves = {}
    values = {}
    token = None

    def begin(name, pairs):
        for at, (first, count, hops, growth) in enumerate(subs[name]):
            steps = steps_of(pairs[2 * at], pairs[2 * at + 1], hops, growth, send)
            reductions[name + str(at)] = steps
            calls[name + str(at)] = next(steps)

    def forward(after):
        (
            res_t, res_l, q_t, q_l, kt, kl, vt, vl, p, ctx_t, ctx_l,
            hid_t, unit_t, inv_t, sum_t, slope_t,
            hid_l, unit_l, inv_l, sum_l, slope_l, act_l, sf_t, sf_l,
            *pairs,
        ) = forward_call(
            blocks, text_project, wl, text_merge, text_expand, text_shrink,
            layout_merge, layout_expand, turned_shrink,
            text_cotangent, layout_cotangent.transpose(0, 2, 1),
            text_biases, text_gains, line_t, layout_biases, layout_gains,
            line_l, packs, rows, dp_size, subs["S"],
        )
        begin("S", pairs)
        values.update(
            results=(res_t, res_l),
            tail=(
                hid_t, unit_t, inv_t, sum_t, slope_t, hid_l, unit_l, inv_l, sum_l, slope_l, act_l,
                ctx_t, ctx_l,
            ),
            attended=(kt, kl, vt, vl, p, q_t, q_l),
            contexts=(ctx_t, ctx_l),
            first_sums=(sf_t, sf_l),
        )
        return sf_t, HBM

    def middle(after):
        mid_t, mid_l, dctx_t, dctx_l, sm_t, sm_l, so_t, so_l, *pairs = middle_call(
            (
                *values["tail"], text_shrink, text_expand, text_merge, turned_shrink,
                layout_expand, layout_merge, text_gains, layout_gains, after[0],
            ),
            packs, rows, dp_size, subs["E"],
        )
        values["E pairs"] = pairs
        values.update(
            middles=(mid_t, mid_l), deltas=(dctx_t, dctx_l), second_sums=(sm_t, sm_l, so_t, so_l)
        )
        return sm_t, HBM

    def attention(after):
        joined_t, joined_l, query_t, query_l, *pairs = attention_call(
            (
                *blocks, *values["attended"], *values["deltas"],
                *values["contexts"], *values["first_sums"], *values["second_sums"], after[0],
            ),
            packs, rows, dp_size, subs["P"],
        )
        values["P pairs"] = pairs
        values.update(joined=(joined_t, joined_l, query_t, query_l))
        return query_l, HBM

    def inputs(after):
        give, hold, mark = input_call(*values["joined"], text_project, wl, after, packs, rows)
        values["X pairs"] = [give, hold]
        return mark, ANY

    def inputs_gate(after, gated=True):
        give, hold = gate_call(values["X pairs"], after) if gated else values["X pairs"]
        lines = 2 * (DT + DL)
        values.update(inputs=[hold.reshape(lines, -1), send(give, core, 1).reshape(lines, -1)])
        return (hold, ANY) if gated else after

    def gate(name, gated=True):
        def call(after):
            pairs = gate_call(values[name + " pairs"], after) if gated else values[name + " pairs"]
            begin(name, pairs)
            return (pairs[1], ANY) if gated else after

        return call

    def inputs_add(after):
        own, onward = add_call(values["inputs"], 2, after)
        values.update(onward=(own, send(onward, (Y,), 1)))
        return own, ANY

    def inputs_end(after):
        values.update(sens=sensitivity_call(*values["onward"], *values["middles"], after))
        return values["sens"][2], ANY

    def end(name, store, label, outs):
        def call(after):
            sources = [array for at in range(len(subs[name])) for array in halves[name + str(at)]]
            values[name] = final_call(
                store, label, sources, after, dp_size, subs[name], outs
            )
            return values[name][-1], ANY

        return call

    kernels = {
        "A": forward,
        "B": middle,
        "C": attention,
        "D": inputs,
        "GE": gate("E"),
        "GP": gate("P"),
        "GX": inputs_gate,
        "NE": gate("E", False),
        "NP": gate("P", False),
        "NX": functools.partial(inputs_gate, gated=False),
        "X0": inputs_add,
        "FX": inputs_end,
        "FS": end("S", shrink_store, "shrink_out", [(DT // 4, FT)]),
        "FE": end(
            "E", expand_store, "expand_out",
            [(DT, DT), (DT // 4, DT), (DL, DL), (DL // 4, FL), (DL // 4, DL)],
        ),
        "FP": end(
            "P", project_store, "project_out",
            [
                (576, DT), (144, DL), (6, DT // 4), (2, DT // 4), (DT,),
                (6, DL // 4), (2, DL // 4), (FL // 4,),
            ],
        ),
    }

    def advance(name, after):
        outs = calls[name](after)
        try:
            calls[name] = reductions[name].send(outs)
        except StopIteration as stop:
            halves[name] = stop.value
            del calls[name]
        return (outs[0] if isinstance(outs, (tuple, list)) else outs), ANY

    def finish(name, after):
        for at in range(len(subs[name])):
            while name + str(at) in calls:
                after = advance(name + str(at), after)
        return after

    token = forward(None)
    for label in ORDER:
        if label in kernels:
            if label[0] == "F" and label[1] in subs:
                token = finish(label[1], token)
            token = kernels[label](token)
        elif label in calls:
            token = advance(label, token)

    res_t, res_l = values["results"]
    sens_t, sens_l, unused = values["sens"]
    shrink_t, unused = values["S"]
    expand_t, merge_t, expand_l, shrink_l, merge_l, unused = values["E"]
    project_t, project_l, biases_t, gains_t, offsets_t, biases_l, gains_l, offsets_l, unused = values["P"]
    return (
        res_t.reshape(packs, rows, DT),
        res_l.transpose(0, 2, 1),
        sens_t.reshape(packs, rows, DT),
        sens_l.transpose(0, 2, 1),
        project_t.T,
        biases_t,
        gains_t,
        merge_t.T,
        expand_t,
        offsets_t,
        shrink_t.T,
        project_l.T,
        biases_l,
        gains_l,
        merge_l.T,
        expand_l,
        offsets_l,
        shrink_l.T,
    )


def solution(mesh):
    rows = P("dp", "seq", None)
    columns = P(None, "seq")
    in_specs = (rows, rows, P("dp", "seq"), rows, rows) + (P(),) * 14
    out_specs = (
        (rows,) * 4 + (columns,) * 5 + (P("seq"),) + (columns,) * 6 + (P("seq"),) + (columns,)
    )
    body = functools.partial(local, mesh.shape["dp"], mesh.shape["seq"])
    return jax.shard_map(body, mesh=mesh, in_specs=in_specs, out_specs=out_specs, check_vma=False)
```

```python
import functools

import jax
import jax.numpy as jnp
from jax import lax
from jax.experimental import pallas as pl
from jax.experimental.pallas import tpu as pltpu
from jax.sharding import PartitionSpec as P

HEADS = 12
EPSILON = 1e-05
MASKED = -1000000000.0
F32 = jnp.float32
BF16 = jnp.bfloat16
DT = 768
DL = 192
FT = 3072
FL = 768
LANES = 128
SLAB = 256
S_ROWS = 768
E_ROWS = 1152
P_ROWS = 640
MIB = 1024 * 1024

VMEM = pl.BlockSpec(memory_space=pltpu.VMEM)
ANY = pl.BlockSpec(memory_space=pl.ANY)
HBM = pl.BlockSpec(memory_space=pltpu.HBM)


def dot(left, right):
    return jnp.dot(left, right, preferred_element_type=F32)


def dot_nt(left, right):
    return lax.dot_general(left, right, (((1,), (1,)), ((), ())), preferred_element_type=F32)


LIMIT = 60 * MIB
FIRST = 60 * MIB
SECOND = 60 * MIB
LAST = 30 * MIB
SMALL = 16 * MIB
UNROLL = 6
UNROLL_BACK = 1


COST = pl.CostEstimate(flops=1, bytes_accessed=1, transcendentals=0)


def shape_of(shape, dtype):
    return jax.ShapeDtypeStruct(shape, dtype)


def copies_of(pairs, sems, base):
    made = []
    for at, (source, target) in enumerate(pairs):
        copy = pltpu.make_async_copy(source, target, sems.at[base + at])
        copy.start()
        made.append(copy)
    return made


def wait_all(made):
    for copy in made:
        copy.wait()


def gather_pairs(blocks, rows, packs, target):
    span = rows * len(blocks)
    return [
        (block.at[pack], target.at[pl.ds(pack * span + at * rows, rows), :])
        for at, block in enumerate(blocks)
        for pack in range(packs)
    ]


def in_lines(shards, subs, dp_size, targets, low=0, high=1 << 30):
    place = (lax.axis_index("seq"), lax.axis_index("dp"))
    pairs = []
    for core in (1, 0):
        for at, (first, rows, hops, growth) in enumerate(subs):
            if not low < first + rows <= high:
                continue
            size = rows // dp_size
            target = targets[2 * at + 1 - core]
            for across in range(2):
                shard = jnp.bitwise_xor(place[0], core + 2 * across)
                for other in range(dp_size):
                    piece = jnp.bitwise_xor(place[1], other)
                    mark = pl.multiple_of(first + piece * size, 16)
                    line = position(hops, across, other) * size
                    pairs.append(
                        (shards.at[shard, pl.ds(mark, size), :], target.at[pl.ds(line, size), :])
                    )
    return pairs


def position(hops, across, other):
    at = 0
    for group in hops:
        index = 0
        for n, (axis, bit) in enumerate(group):
            if across if axis == "seq" else other & bit:
                index += 1 << n
        at = (at << len(group)) + index
    return at


def sub_chunks(rows, split, dp_size):
    step = 16 * dp_size
    total = (rows + step - 1) // step * step
    subs = []
    first = 0
    for at, (share, hops, growth) in enumerate(split):
        size = total - first if at == len(split) - 1 else (share + step - 1) // step * step
        subs.append((first, size, hops, growth))
        first += size
    return tuple(subs)


def total_lines(subs):
    return sum(rows for first, rows, hops, growth in subs)


def pair_shapes(subs):
    return tuple(shape_of((2 * rows, DT), BF16) for first, rows, hops, growth in subs for unused in range(2))


def lane_masks(pair_at):
    lanes = lax.broadcasted_iota(jnp.int32, (1, LANES), 1)
    low_half = lanes < 64
    group_of_16 = lax.shift_right_logical(lanes, 4)
    first = group_of_16 == 2 * lax.rem(pair_at, 4)
    second = group_of_16 == 2 * lax.rem(pair_at, 4) + 1
    return (low_half, first, second)


def stacked_heads(text_rows, layout_rows, masks):
    low_half, first, second = masks
    zero_text = jnp.zeros_like(text_rows)
    zero_layout = jnp.zeros_like(layout_rows)
    top = jnp.concatenate(
        [jnp.where(low_half, text_rows, zero_text), jnp.where(first, layout_rows, zero_layout)],
        axis=1,
    )
    bottom = jnp.concatenate(
        [jnp.where(low_half, zero_text, text_rows), jnp.where(second, layout_rows, zero_layout)],
        axis=1,
    )
    return jnp.concatenate([top, bottom], axis=0)


def normalized(values):
    centre = values - jnp.mean(values, axis=-1, keepdims=True)
    spread = jnp.mean(centre * centre, axis=-1, keepdims=True)
    inverse = lax.rsqrt(spread + EPSILON)
    return (centre * inverse, inverse)


def norm_back(delta, unit, inverse):
    return inverse * (
        delta
        - jnp.mean(delta, axis=-1, keepdims=True)
        - unit * jnp.mean(delta * unit, axis=-1, keepdims=True)
    )


def column_sum(values):
    return jnp.sum(values, axis=0, keepdims=True)


def feed_forward(hidden_low, expand, offsets, shrink, turned, active, slope, chunk, branch_ref):
    width = expand.shape[1]
    for at in range(width // chunk):
        part = pl.ds(at * chunk, chunk)
        before = dot(hidden_low, expand[:, part]) + offsets[:, part].astype(F32)
        share = 0.5 + 0.5 * lax.erf(before * (0.5**0.5))
        density = jnp.exp(-0.5 * (before * before)) * 0.3989422804014327
        active_part = (before * share).astype(BF16)
        active[:, part] = active_part
        slope[:, part] = (share + before * density).astype(BF16)
        product = dot_nt(active_part, shrink[:, part]) if turned else dot(active_part, shrink[part, :])
        if at == 0:
            branch_ref[...] = product
        else:
            branch_ref[...] += product


def prepare_kernel(text_rows, layout_rows, segments, project, offsets_t, offsets_l, joined, padded, line_t, line_l):
    packs, width, rows = layout_rows.shape
    for pack in range(packs):
        marks = jnp.broadcast_to(segments[pack : pack + 1, :].astype(F32), (SLAB - width, rows))
        lines = jnp.concatenate([layout_rows[pack].astype(F32), marks], axis=0)
        joined[pack, :, :DT] = text_rows[pack]
        joined[pack, :, DT:] = lines.T.astype(BF16)
    line_t[...] = offsets_t[...].reshape(line_t.shape)
    line_l[...] = offsets_l[...].reshape(line_l.shape)
    padded[...] = jnp.zeros_like(padded)
    for third in range(3):
        padded[:, third * SLAB : third * SLAB + DL] = project[:, third * DL : (third + 1) * DL]


def prepare_call(text_rows, layout_rows, segments, project, offsets_t, offsets_l):
    packs, rows, unused = text_rows.shape
    return pl.pallas_call(
        prepare_kernel,
        out_shape=(
            shape_of((packs, rows, DT + SLAB), BF16),
            shape_of((DL, 3 * SLAB), BF16),
            shape_of((1, FT), BF16),
            shape_of((1, FL), BF16),
        ),
        in_specs=[VMEM] * 6,
        out_specs=[VMEM] * 4,
        compiler_params=pltpu.CompilerParams(vmem_limit_bytes=LIMIT),
        cost_estimate=COST,
        name="prepare",
    )(text_rows, layout_rows, segments, project, offsets_t, offsets_l)


def forward_kernel(
    packs,
    rows,
    dp_size,
    subs,
    x0,
    x1,
    x2,
    x3,
    wt_in,
    wl_in,
    mt_in,
    et_in,
    st_in,
    ml,
    el,
    sl,
    cot_t,
    cot_l,
    bt,
    gt,
    ot,
    bl,
    gl,
    ol,
    res_t_out,
    res_l_out,
    q_t_out,
    q_l_out,
    kt_out,
    kl_out,
    vt_out,
    vl_out,
    p_out,
    ctx_t_out,
    ctx_l_out,
    hid_t_out,
    unit_t_out,
    inv_t_out,
    sum_t_out,
    slope_t_out,
    hid_l_out,
    unit_l_out,
    inv_l_out,
    sum_l_out,
    slope_l_out,
    act_l_out,
    sv_t_out,
    sv_l_out,
    *rest,
):
    targets, rest = rest[: 2 * len(subs)], rest[2 * len(subs) :]
    (
        xs,
        res_t,
        res_l,
        q_t,
        q_l,
        ctx_t,
        ctx_l,
        hid_t,
        unit_t,
        inv_t,
        sum_t,
        slope_t,
        hid_l,
        unit_l,
        inv_l,
        sum_l,
        slope_l,
        act_l,
        sv_t,
        sv_l,
        layout_bias_ref,
        wt,
        wl,
        mt,
        et,
        st,
        k_t,
        k_l,
        v_t,
        v_l,
        prob,
        bias,
        act_t,
        turned,
        branch_t,
        branch_l,
        grads,
        sems,
    ) = rest
    blocks = (x0, x1, x2, x3)
    keys = rows * len(blocks)
    tokens = packs * rows
    x_copies = copies_of(
        gather_pairs(blocks, rows, packs, xs), sems, 0
    )
    base = len(x_copies)
    w_copies = copies_of(((wt_in, wt), (wl_in, wl)), sems, base)
    base += 2
    pending = []

    def emit(*pairs):
        pending.extend(copies_of(pairs, sems, base + len(pending)))

    text_bias = bt[...].astype(F32)
    layout_bias_ref[...] = jnp.zeros_like(layout_bias_ref)
    layout_bias_ref[:, :DL] = bl[...].astype(F32)
    layout_bias = layout_bias_ref[...]
    wait_all(x_copies)
    wait_all(w_copies)
    w_copies = copies_of(((mt_in, mt), (et_in, et), (st_in, st)), sems, base)
    base += 3

    for pack in range(packs):
        own = pl.ds(pack * keys, rows)
        mine = pl.ds(pack * rows, rows)
        q_t[mine, :] = (dot(xs[own, :DT], wt[:, :DT]) + text_bias[0:1, :]).astype(BF16) * 0.125
        q_l[mine, :] = (dot(xs[own, DT : DT + DL], wl[:, :SLAB]) + layout_bias[0:1, :]).astype(BF16) * 0.25

    step = 256

    def key_rows(at, unused):
        span = pl.ds(pl.multiple_of(at * step, step), step)
        k_t[span, :] = dot(xs[span, :DT], wt[:, DT : 2 * DT]).astype(BF16)
        v_t[span, :] = (dot(xs[span, :DT], wt[:, 2 * DT :]) + text_bias[1:2, :]).astype(BF16)
        k_l[span, :] = dot(xs[span, DT : DT + DL], wl[:, SLAB : 2 * SLAB]).astype(BF16)
        v_l[span, :] = (dot(xs[span, DT : DT + DL], wl[:, 2 * SLAB :]) + layout_bias[1:2, :]).astype(BF16)
        return unused

    lax.fori_loop(0, packs * keys // step, key_rows, 0)
    emit((k_t, kt_out), (k_l, kl_out), (v_t, vt_out), (v_l, vl_out), (q_t, q_t_out), (q_l, q_l_out))

    marks = lax.broadcasted_iota(jnp.int32, (1, LANES), 1) - 64
    for pack in range(packs):
        slab = xs[pl.ds(pack * keys, keys), DT + LANES : DT + 2 * LANES].astype(F32)
        hot = jnp.where((slab == marks.astype(F32)) & (marks >= 0) & (marks < 16), 1.0, 0.0).astype(BF16)
        same = dot_nt(hot[:rows], hot)
        bias[pack] = jnp.where(same > 0.5, 0.0, MASKED)

    ctx_l[...] = jnp.zeros_like(ctx_l)

    def head_pair(pair_at, unused):
        masks = lane_masks(pair_at)
        text_lanes = pl.ds(pl.multiple_of(pair_at * LANES, LANES), LANES)
        layout_lanes = pl.ds(pl.multiple_of(pair_at // 4 * LANES, LANES), LANES)
        for pack in range(packs):
            mine = pl.ds(pack * rows, rows)
            span = pl.ds(pack * keys, keys)
            queries = stacked_heads(q_t[mine, text_lanes], q_l[mine, layout_lanes], masks)
            both_keys = jnp.concatenate([k_t[span, text_lanes], k_l[span, layout_lanes]], axis=1)
            both_values = jnp.concatenate([v_t[span, text_lanes], v_l[span, layout_lanes]], axis=1)
            allowed = bias[pack]
            logit = dot_nt(queries, both_keys) + jnp.concatenate([allowed, allowed], axis=0)
            raised = jnp.exp(logit - jnp.max(logit, axis=1, keepdims=True))
            low = (raised * (1.0 / jnp.sum(raised, axis=1, keepdims=True))).astype(BF16)
            prob[pair_at, pack] = low
            mixed = dot(low, both_values).astype(BF16)
            ctx_t[mine, text_lanes] = jnp.where(masks[0], mixed[:rows, :LANES], mixed[rows:, :LANES])
            kept = ctx_l[mine, layout_lanes]
            kept = jnp.where(masks[1], mixed[:rows, LANES:], kept)
            ctx_l[mine, layout_lanes] = jnp.where(masks[2], mixed[rows:, LANES:], kept)
        return unused

    lax.fori_loop(0, HEADS // 2, head_pair, 0, unroll=UNROLL)
    emit((prob, p_out), (ctx_t, ctx_t_out), (ctx_l, ctx_l_out))
    wait_all(w_copies)

    def own_rows(lanes):
        return jnp.concatenate(
            [xs[pl.ds(pack * keys, rows), lanes].astype(F32) for pack in range(packs)], axis=0
        )

    def tail(x, attended, expand, offsets, shrink, turned, b, g, cotangent, active, slope, branch, chunk, hid, unit, inv, delta, sv, outs):
        width = x.shape[1]
        middle = x + attended + b[2:3, :width]
        unit_first, inverse_first = normalized(middle)
        hidden = unit_first * g[0:1, :] + b[3:4, :width]
        hidden_low = hidden.astype(BF16)
        hid[...] = hidden_low
        unit[...] = unit_first
        inv[...] = inverse_first
        emit((hid, outs[0]), (unit, outs[1]), (inv, outs[2]))
        feed_forward(hidden_low, expand, offsets, shrink, turned, active, slope, chunk, branch)
        emit((slope, outs[3]))
        unit_second, inverse_second = normalized(hidden + branch[...] + b[4:5, :width])
        result = unit_second * g[1:2, :] + b[5:6, :width]
        sv[1:2, :] = column_sum(cotangent)
        sv[2:3, :] = column_sum(cotangent * unit_second)
        sum_delta = norm_back(cotangent * g[1:2, :], unit_second, inverse_second)
        delta[...] = sum_delta
        emit((delta, outs[4]))
        rounded = sum_delta.astype(BF16).astype(F32)
        sv[0:1, :] = column_sum(rounded)
        emit((sv, outs[5]))
        return result, rounded

    result, rounded = tail(
        own_rows(slice(0, DT)), dot(ctx_t[...], mt[...]), et, ot, st, False, text_bias, gt[...].astype(F32),
        jnp.concatenate([cot_t[pack] for pack in range(packs)], axis=0).astype(F32),
        act_t, slope_t, branch_t, 512, hid_t, unit_t, inv_t, sum_t, sv_t,
        (hid_t_out, unit_t_out, inv_t_out, slope_t_out, sum_t_out, sv_t_out),
    )
    res_t[...] = result.astype(BF16)
    emit((res_t, res_t_out))
    turned[...] = rounded.T.astype(BF16)
    share = DT // 4
    for shard in range(4):
        own = turned[shard * share : (shard + 1) * share, :]
        for block in range(FT // DT):
            grads[shard, pl.ds(block * share, share), :] = dot(
                own, act_t[:, block * DT : (block + 1) * DT]
            ).astype(BF16)
    if grads.shape[1] > S_ROWS:
        grads[:, S_ROWS:, :] = jnp.zeros((4, grads.shape[1] - S_ROWS, DT), BF16)
    emit(*in_lines(grads, subs, dp_size, targets))
    result, unused = tail(
        own_rows(slice(DT, DT + DL)), dot(ctx_l[:, :DL], ml[...]), el, ol, sl, True, layout_bias,
        gl[...].astype(F32),
        jnp.concatenate([cot_l[pack].astype(F32).T for pack in range(packs)], axis=0),
        act_l, slope_l, branch_l, 256, hid_l, unit_l, inv_l, sum_l, sv_l,
        (hid_l_out, unit_l_out, inv_l_out, slope_l_out, sum_l_out, sv_l_out),
    )
    for pack in range(packs):
        res_l[pack] = result[pack * rows : (pack + 1) * rows, :].T.astype(BF16)
    emit((res_l, res_l_out), (act_l, act_l_out))
    wait_all(pending)


def forward_call(blocks, wt, wl, mt, et, st, ml, el, sl, cot_t, cot_l, bt, gt, ot, bl, gl, ol, packs, rows, dp_size, subs):
    tokens = packs * rows
    lines = total_lines(subs)
    every = tokens * len(blocks)
    keys = rows * len(blocks)
    pairs = HEADS // 2
    outs = (
        shape_of((tokens, DT), BF16),
        shape_of((packs, DL, rows), BF16),
        shape_of((tokens, DT), BF16),
        shape_of((tokens, SLAB), BF16),
        shape_of((every, DT), BF16),
        shape_of((every, SLAB), BF16),
        shape_of((every, DT), BF16),
        shape_of((every, SLAB), BF16),
        shape_of((pairs, packs, 2 * rows, keys), BF16),
        shape_of((tokens, DT), BF16),
        shape_of((tokens, SLAB), BF16),
        shape_of((tokens, DT), BF16),
        shape_of((tokens, DT), F32),
        shape_of((tokens, 1), F32),
        shape_of((tokens, DT), F32),
        shape_of((tokens, FT), BF16),
        shape_of((tokens, DL), BF16),
        shape_of((tokens, DL), F32),
        shape_of((tokens, 1), F32),
        shape_of((tokens, DL), F32),
        shape_of((tokens, FL), BF16),
        shape_of((tokens, FL), BF16),
        shape_of((8, DT), F32),
        shape_of((8, DL), F32),
    ) + pair_shapes(subs)
    out_specs = [ANY] * len(outs)
    kept = (0, 1, 2, 3, 9, 10) + tuple(range(11, 24))
    scratch = [
        pltpu.VMEM((every, DT + SLAB), BF16),
        *(pltpu.VMEM(outs[at].shape, outs[at].dtype) for at in kept),
        pltpu.VMEM((6, SLAB), F32),
        pltpu.VMEM(wt.shape, BF16),
        pltpu.VMEM(wl.shape, BF16),
        pltpu.VMEM(mt.shape, BF16),
        pltpu.VMEM(et.shape, BF16),
        pltpu.VMEM(st.shape, BF16),
        pltpu.VMEM((every, DT), BF16),
        pltpu.VMEM((every, SLAB), BF16),
        pltpu.VMEM((every, DT), BF16),
        pltpu.VMEM((every, SLAB), BF16),
        pltpu.VMEM((pairs, packs, 2 * rows, keys), BF16),
        pltpu.VMEM((packs, rows, keys), F32),
        pltpu.VMEM((tokens, FT), BF16),
        pltpu.VMEM((DT, tokens), BF16),
        pltpu.VMEM((tokens, DT), F32),
        pltpu.VMEM((tokens, DL), F32),
        pltpu.VMEM((4, lines, DT), BF16),
        pltpu.SemaphoreType.DMA((48 + 4 * dp_size * len(subs),)),
    ]
    return pl.pallas_call(
        functools.partial(forward_kernel, packs, rows, dp_size, subs),
        out_shape=outs,
        in_specs=[ANY] * 9 + [VMEM] * 11,
        out_specs=out_specs,
        scratch_shapes=scratch,
        compiler_params=pltpu.CompilerParams(vmem_limit_bytes=FIRST),
        cost_estimate=COST,
        name="forward",
    )(*blocks, wt, wl, mt, et, st, ml, el, sl, cot_t, cot_l, bt, gt, ot, bl, gl, ol)


def middle_kernel(
    dp_size,
    subs,
    hid_t_in,
    unit_t_in,
    inv_t_in,
    sum_t_in,
    slope_t_in,
    hid_l,
    unit_l,
    inv_l,
    sum_l,
    slope_l,
    act_l,
    ctx_t_in,
    ctx_l,
    st_in,
    et_in,
    mt_in,
    sl,
    el,
    ml,
    gt,
    gl,
    after,
    mid_t,
    mid_l,
    dctx_t,
    dctx_l,
    sv_t,
    sv_l,
    so_t,
    so_l,
    *rest,
):
    targets, rest = rest[: 2 * len(subs)], rest[2 * len(subs) :]
    (
        hid_t,
        unit_t,
        inv_t,
        sum_t,
        slope_t,
        ctx_t,
        st,
        et,
        mt,
        before_t,
        before_l,
        turned,
        grads,
        sems,
    ) = rest
    w_copies = copies_of(
        (
            (sum_t_in, sum_t), (st_in, st), (slope_t_in, slope_t), (hid_t_in, hid_t), (et_in, et),
            (unit_t_in, unit_t), (inv_t_in, inv_t), (ctx_t_in, ctx_t), (mt_in, mt),
        ),
        sems,
        0,
    )
    base = len(w_copies)

    def feed_back(branch_delta, shrink, turned, slope, before, so, chunk):
        for at in range(slope.shape[1] // chunk):
            part = pl.ds(at * chunk, chunk)
            if turned:
                active_delta = dot(branch_delta, shrink[:, part])
            else:
                active_delta = dot_nt(branch_delta, shrink[part, :])
            low = (active_delta * slope[:, part].astype(F32)).astype(BF16)
            before[:, part] = low
            so[:, part] = column_sum(low.astype(F32))

    def front(hidden_delta, total, unit, inv, g, merge, sv):
        delta = total[...] + hidden_delta
        sv[0:1, :] = column_sum(delta * unit[...])
        sv[1:2, :] = column_sum(delta)
        middle = norm_back(delta * g, unit[...], inv[...])
        low = middle.astype(BF16)
        rounded = low.astype(F32)
        sv[2:3, :] = column_sum(rounded)
        back = dot_nt(low, merge).astype(BF16)
        sv[3:4, :] = column_sum(back.astype(F32))
        return middle, rounded.T.astype(BF16), back

    layout_delta = sum_l[...].astype(BF16)
    feed_back(layout_delta, sl, True, slope_l, before_l, so_l, 256)
    turned_l = before_l[...].astype(F32).T.astype(BF16)
    grown_l = dot(turned_l, hid_l[...]).astype(BF16)
    shrunk_l = dot(layout_delta.astype(F32).T.astype(BF16), act_l[...]).astype(BF16)
    middle, low_turned, back = front(
        dot_nt(before_l[...], el[...]), sum_l, unit_l, inv_l, gl[0:1, :].astype(F32), ml[...], sv_l
    )
    for pack in range(mid_l.shape[0]):
        size = mid_l.shape[2]
        mid_l[pack] = middle[pack * size : (pack + 1) * size, :].T
    dctx_l[...] = jnp.zeros_like(dctx_l)
    dctx_l[:, :DL] = back
    merged_l = dot(low_turned, ctx_l[...]).astype(BF16)
    wait_all(w_copies[:3])
    feed_back(sum_t[...].astype(BF16), st, False, slope_t, before_t, so_t, 512)
    wait_all(w_copies[3:4])
    turned[...] = hid_t[...].astype(F32).T.astype(BF16)
    for shard in range(4):
        grads[shard, pl.ds(0, DT), :] = dot(
            turned[...], before_t[:, shard * DT : (shard + 1) * DT]
        ).astype(BF16)
    early = copies_of(in_lines(grads, subs, dp_size, targets, 0, DT), sems, base)
    base += len(early)
    wait_all(w_copies[4:])
    middle, low_turned, back = front(
        dot_nt(before_t[...], et[...]), sum_t, unit_t, inv_t, gt[0:1, :].astype(F32), mt[...], sv_t
    )
    mid_t[...] = middle
    dctx_t[...] = back
    for shard in range(4):
        grads[shard, pl.ds(DT, 192), :] = dot(
            low_turned[shard * 192 : (shard + 1) * 192, :], ctx_t[...]
        ).astype(BF16)
    for shard in range(4):
        grads[shard, 960:, :] = jnp.zeros((grads.shape[1] - 960, DT), BF16)
        for at in range(3):
            lanes = slice(at * SLAB, at * SLAB + DL)
            line = shard * DL + at * 64
            grads[shard, 960:1024, lanes] = grown_l[line : line + 64, :]
            line = shard * 48 + at * 16
            grads[shard, 1072:1088, at * SLAB : (at + 1) * SLAB] = merged_l[line : line + 16, :]
        grads[shard, 1024:1072, :] = shrunk_l[shard * 48 : shard * 48 + 48, :]
    wait_all(copies_of(in_lines(grads, subs, dp_size, targets, DT), sems, base))
    wait_all(early)


def middle_call(operands, packs, rows, dp_size, subs):
    tokens = packs * rows
    lines = total_lines(subs)
    outs = (
        shape_of((tokens, DT), F32),
        shape_of((packs, DL, rows), F32),
        shape_of((tokens, DT), BF16),
        shape_of((tokens, SLAB), BF16),
        shape_of((8, DT), F32),
        shape_of((8, DL), F32),
        shape_of((1, FT), F32),
        shape_of((1, FL), F32),
    ) + pair_shapes(subs)
    scratch = [
        *(pltpu.VMEM(operands[at].shape, operands[at].dtype) for at in (0, 1, 2, 3, 4, 11)),
        pltpu.VMEM((FT, DT), BF16),
        pltpu.VMEM((DT, FT), BF16),
        pltpu.VMEM((DT, DT), BF16),
        pltpu.VMEM((tokens, FT), BF16),
        pltpu.VMEM((tokens, FL), BF16),
        pltpu.VMEM((DT, tokens), BF16),
        pltpu.VMEM((4, lines, DT), BF16),
        pltpu.SemaphoreType.DMA((16 + 4 * dp_size * len(subs),)),
    ]
    return pl.pallas_call(
        functools.partial(middle_kernel, dp_size, subs),
        out_shape=outs,
        in_specs=[ANY] * 5 + [VMEM] * 6 + [ANY, VMEM] + [ANY] * 3 + [VMEM] * 5 + [ANY],
        out_specs=[VMEM] * 8 + [ANY] * (2 * len(subs)),
        scratch_shapes=scratch,
        compiler_params=pltpu.CompilerParams(vmem_limit_bytes=SECOND),
        cost_estimate=COST,
        name="middle",
    )(*operands)


def attention_kernel(
    packs,
    rows,
    dp_size,
    subs,
    x0,
    x1,
    x2,
    x3,
    kt_in,
    kl_in,
    vt_in,
    vl_in,
    p_in,
    q_t,
    q_l,
    dctx_t,
    dctx_l,
    ctx_t,
    ctx_l,
    sf_t,
    sf_l,
    sm_t,
    sm_l,
    so_t,
    so_l,
    after,
    joined_t_out,
    joined_l_out,
    query_t_out,
    query_l_out,
    *rest,
):
    targets, rest = rest[: 2 * len(subs)], rest[2 * len(subs) :]
    (
        xs,
        joined_t,
        joined_l,
        query_t,
        query_l,
        k_t,
        k_l,
        v_t,
        v_l,
        prob,
        dq_t,
        dq_l,
        dk_l,
        dv_l,
        layout_grads,
        grads,
        smalls,
        sems,
    ) = rest
    blocks = (x0, x1, x2, x3)
    keys = rows * len(blocks)
    kv_copies = copies_of(((kt_in, k_t), (vt_in, v_t), (kl_in, k_l), (vl_in, v_l)), sems, 0)

    def chances(at):
        return pltpu.make_async_copy(p_in.at[at], prob.at[at], sems.at[4 + at])

    for at in range(HEADS // 2):
        chances(at).start()
    base = 4 + HEADS // 2
    dq_l[...] = jnp.zeros_like(dq_l)
    dk_l[...] = jnp.zeros_like(dk_l)
    dv_l[...] = jnp.zeros_like(dv_l)
    wait_all(kv_copies)
    x_copies = copies_of(gather_pairs(blocks, rows, packs, xs), sems, base)
    base += len(x_copies)

    def head_pair(pair_at, unused):
        chances(pair_at).wait()
        masks = lane_masks(pair_at)
        text_lanes = pl.ds(pl.multiple_of(pair_at * LANES, LANES), LANES)
        layout_lanes = pl.ds(pl.multiple_of(pair_at // 4 * LANES, LANES), LANES)
        for pack in range(packs):
            mine = pl.ds(pack * rows, rows)
            span = pl.ds(pack * keys, keys)
            queries = stacked_heads(q_t[mine, text_lanes], q_l[mine, layout_lanes], masks)
            deltas = stacked_heads(dctx_t[mine, text_lanes], dctx_l[mine, layout_lanes], masks)
            one = jnp.concatenate([ctx_t[mine, text_lanes], ctx_l[mine, layout_lanes]], axis=1)
            contexts = jnp.concatenate([one, one], axis=0).astype(F32)
            products = deltas.astype(F32) * contexts
            layout_mean = jnp.sum(products[:, LANES:], axis=1, keepdims=True)
            both_mean = jnp.sum(products, axis=1, keepdims=True)
            text_values = v_t[span, text_lanes]
            layout_values = v_l[span, layout_lanes]
            both_values = jnp.concatenate([text_values, layout_values], axis=1)
            low = prob[pair_at, pack]
            chance = low.astype(F32)
            both_change = (chance * (dot_nt(deltas, both_values) - both_mean)).astype(BF16)
            layout_change = (
                chance * (dot_nt(deltas[:, LANES:], layout_values) - layout_mean)
            ).astype(BF16)
            from_text = dot(both_change, k_t[span, text_lanes])
            dq_t[mine, text_lanes] = (
                jnp.where(masks[0], from_text[:rows], from_text[rows:]) * 0.125
            ).astype(BF16)
            from_layout = dot(layout_change, k_l[span, layout_lanes]) * 0.25
            kept = dq_l[mine, layout_lanes]
            kept = jnp.where(masks[1], from_layout[:rows], kept)
            dq_l[mine, layout_lanes] = jnp.where(masks[2], from_layout[rows:], kept)
            turned_queries = queries.T
            turned_deltas = deltas.T
            joined_t[text_lanes, span] = dot(turned_queries[:LANES], both_change).astype(BF16)
            dk_l[layout_lanes, span] += dot(turned_queries[LANES:], layout_change)
            value_change = dot(turned_deltas, low)
            text_at = pl.ds(pl.multiple_of(pair_at * LANES + DT, LANES), LANES)
            joined_t[text_at, span] = value_change[:LANES].astype(BF16)
            dv_l[layout_lanes, span] += value_change[LANES:]
        return unused

    lax.fori_loop(0, HEADS // 2, head_pair, 0, unroll=UNROLL_BACK)
    joined_l[:SLAB, :] = dk_l[...].astype(BF16)
    joined_l[SLAB:, :] = dv_l[...].astype(BF16)
    whole_t = dq_t[...].astype(F32)
    whole_l = dq_l[...]
    low_l = whole_l.astype(BF16)
    query_t[...] = whole_t.T.astype(BF16)
    query_l[...] = whole_l.T.astype(BF16)
    out_copies = copies_of(
        ((joined_t, joined_t_out), (joined_l, joined_l_out), (query_t, query_t_out), (query_l, query_l_out)),
        sems,
        base,
    )
    base += 4
    wait_all(x_copies)
    own = jnp.concatenate([xs[pl.ds(pack * keys, rows), :] for pack in range(packs)], axis=0)
    step = 192
    for at in range(3 * DT // step):
        shard, line = at // 3, at % 3 * step
        if at < DT // step:
            product = dot(query_t[at * step : (at + 1) * step, :], own[:, :DT])
        else:
            product = dot(joined_t[at * step - DT : (at + 1) * step - DT, :], xs[:, :DT])
        grads[shard, line : line + step, :] = product.astype(BF16)
    layout_grads[:DL, :] = dot(query_l[:DL, :], own[:, DT:]).astype(BF16)
    layout_grads[DL : 2 * DL, :] = dot(joined_l[:DL, :], xs[:, DT:]).astype(BF16)
    layout_grads[2 * DL :, :] = dot(joined_l[SLAB : SLAB + DL, :], xs[:, DT:]).astype(BF16)
    text_lines = jnp.concatenate(
        [column_sum(whole_t), sm_t[3:4, :], sm_t[2:3, :], sm_t[1:2, :], sf_t[0:2, :], sm_t[0:1, :], sf_t[2:3, :]],
        axis=0,
    )
    layout_lines = jnp.concatenate(
        [
            column_sum(low_l.astype(F32))[:, :DL],
            sm_l[3:4, :], sm_l[2:3, :], sm_l[1:2, :], sf_l[0:2, :], sm_l[0:1, :], sf_l[2:3, :],
        ],
        axis=0,
    )
    for shard in range(4):
        for at in range(3):
            line = shard * 144 + at * 48
            grads[shard, 576:624, at * SLAB : (at + 1) * SLAB] = layout_grads[line : line + 48, :]
        smalls[...] = jnp.zeros_like(smalls)
        share = DT // 4
        smalls[0:8, 0:share] = text_lines[:, shard * share : (shard + 1) * share]
        smalls[8:9, :] = so_t[:, shard * DT : (shard + 1) * DT]
        share = DL // 4
        smalls[0:8, SLAB : SLAB + share] = layout_lines[:, shard * share : (shard + 1) * share]
        share = FL // 4
        smalls[9:10, 0:share] = so_l[:, shard * share : (shard + 1) * share]
        grads[shard, 624:640, :] = smalls[...].astype(BF16)
        if grads.shape[1] > P_ROWS:
            grads[shard, P_ROWS:, :] = jnp.zeros((grads.shape[1] - P_ROWS, DT), BF16)
    wait_all(copies_of(in_lines(grads, subs, dp_size, targets), sems, base))
    wait_all(out_copies)


def attention_call(operands, packs, rows, dp_size, subs):
    tokens = packs * rows
    every = tokens * 4
    lines = total_lines(subs)
    pairs = HEADS // 2
    outs = (
        shape_of((2 * DT, every), BF16),
        shape_of((2 * SLAB, every), BF16),
        shape_of((DT, tokens), BF16),
        shape_of((SLAB, tokens), BF16),
    ) + pair_shapes(subs)
    scratch = [
        pltpu.VMEM((every, DT + SLAB), BF16),
        *(pltpu.VMEM(outs[at].shape, outs[at].dtype) for at in range(4)),
        pltpu.VMEM((every, DT), BF16),
        pltpu.VMEM((every, SLAB), BF16),
        pltpu.VMEM((every, DT), BF16),
        pltpu.VMEM((every, SLAB), BF16),
        pltpu.VMEM((pairs, packs, 2 * rows, 4 * rows), BF16),
        pltpu.VMEM((tokens, DT), BF16),
        pltpu.VMEM((tokens, SLAB), F32),
        pltpu.VMEM((SLAB, every), F32),
        pltpu.VMEM((SLAB, every), F32),
        pltpu.VMEM((3 * DL, SLAB), BF16),
        pltpu.VMEM((4, lines, DT), BF16),
        pltpu.VMEM((16, DT), F32),
        pltpu.SemaphoreType.DMA((32 + 4 * dp_size * len(subs),)),
    ]
    return pl.pallas_call(
        functools.partial(attention_kernel, packs, rows, dp_size, subs),
        out_shape=outs,
        in_specs=[ANY] * 9 + [VMEM] * 12 + [ANY],
        out_specs=[ANY] * len(outs),
        scratch_shapes=scratch,
        compiler_params=pltpu.CompilerParams(vmem_limit_bytes=LAST),
        cost_estimate=COST,
        name="attention_back",
    )(*operands)


def input_kernel(
    packs, rows, joined_in, joined_l, query_t, query_l, wt_in, wl, after, give, hold, mark, joined_t, wt, totals, sums, sems
):
    keys = joined_t.shape[1] // packs
    pairs = []
    for third in (1, 2):
        lanes = pl.ds(third * DT, DT)
        lines = pl.ds((third - 1) * DT, DT)
        pairs += [(wt_in.at[:, lanes], wt.at[:, lanes]), (joined_in.at[lines, :], joined_t.at[lines, :])]
    pairs.append((wt_in.at[:, pl.ds(0, DT)], wt.at[:, pl.ds(0, DT)]))
    copies = copies_of(pairs, sems, 0)

    def tokens_of(ref, lines, at):
        spans = [slice(pack * keys + at * rows, pack * keys + (at + 1) * rows) for pack in range(packs)]
        return jnp.concatenate([ref[lines, span] for span in spans], axis=1)

    everything = slice(None)
    for at in range(4):
        sums[at, DT:, :] = dot(wl[:, SLAB:], tokens_of(joined_l, everything, at)).astype(BF16)
    layout_own = dot(wl[:, :SLAB], query_l[...])
    sums[0, DT:, :] = (sums[0, DT:, :].astype(F32) + layout_own).astype(BF16)
    mark[...] = layout_own[:8, :LANES]
    wait_all(copies[:2])
    for at in range(4):
        totals[at] = dot(wt[:, DT : 2 * DT], tokens_of(joined_t, slice(0, DT), at))
    wait_all(copies[2:])
    out = []
    for at in (3, 1, 2, 0):
        total = totals[at] + dot(wt[:, 2 * DT :], tokens_of(joined_t, slice(DT, 2 * DT), at))
        if at == 0:
            total += dot(wt[:, :DT], query_t[...])
        sums[at, :DT, :] = total.astype(BF16)
        target = (hold, give)[at % 2].at[at // 2]
        out += copies_of(((sums.at[at], target),), sems, 5 + at)
    wait_all(out)


def input_call(joined_t, joined_l, query_t, query_l, wt, wl, after, packs, rows):
    tokens = packs * rows
    return pl.pallas_call(
        functools.partial(input_kernel, packs, rows),
        out_shape=(shape_of((2, DT + DL, tokens), BF16),) * 2 + (shape_of((8, LANES), F32),),
        in_specs=[ANY] + [VMEM] * 3 + [ANY, VMEM, after[1]],
        out_specs=[ANY] * 2 + [VMEM],
        scratch_shapes=[
            pltpu.VMEM(joined_t.shape, BF16),
            pltpu.VMEM(wt.shape, BF16),
            pltpu.VMEM((4, DT, tokens), F32),
            pltpu.VMEM((4, DT + DL, tokens), BF16),
            pltpu.SemaphoreType.DMA((9,)),
        ],
        compiler_params=pltpu.CompilerParams(vmem_limit_bytes=22 * MIB),
        cost_estimate=COST,
        name="input_back",
    )(joined_t, joined_l, query_t, query_l, wt, wl, after[0])


def sensitivity_kernel(own, far, mid_t, mid_l, after, out_t, out_l, mark):
    mark[...] = mid_t[:8, :LANES]
    total = own[...].astype(F32) + far[...].astype(F32)
    out_t[...] = mid_t[...] + total[:DT, :].T
    packs, unused, rows = mid_l.shape
    for pack in range(packs):
        out_l[pack] = mid_l[pack] + total[DT:, pack * rows : (pack + 1) * rows]


def sensitivity_call(own, far, mid_t, mid_l, after):
    return pl.pallas_call(
        sensitivity_kernel,
        out_shape=(shape_of(mid_t.shape, F32), shape_of(mid_l.shape, F32), shape_of((8, LANES), F32)),
        in_specs=[VMEM] * 4 + [after[1]],
        out_specs=[VMEM] * 3,
        compiler_params=pltpu.CompilerParams(vmem_limit_bytes=SMALL),
        cost_estimate=COST,
        name="sensitivity",
    )(own, far, mid_t, mid_l, after[0])


def lines_in_order(dp_size, sources, subs, whole):
    device = lax.axis_index("dp")
    for at, (first, rows, hops, growth) in enumerate(subs):
        half, other = sources[2 * at : 2 * at + 2]
        size = rows // dp_size
        for index in range(dp_size):
            line = position(growth[::-1], 0, index) * size
            source = half if line < rows // 2 else other
            line = line % (rows // 2)
            mark = pl.multiple_of(first + jnp.bitwise_xor(device, index) * size, 16)
            whole[pl.ds(mark, size), :] = source[line : line + size, :].astype(F32)


def shrink_store(whole, out):
    share = DT // 4
    for block in range(FT // DT):
        out[:, block * DT : (block + 1) * DT] = whole[block * share : (block + 1) * share, :]


def expand_store(whole, out, out_merge, out_grow, out_shrink, out_layout_merge):
    out[...] = whole[:DT, :]
    out_merge[...] = whole[DT:960, :]
    grown = jnp.concatenate(
        [whole[960:1024, at * SLAB : at * SLAB + DL] for at in range(3)], axis=0
    )
    out_grow[...] = grown.T
    out_shrink[...] = whole[1024:1072, :]
    out_layout_merge[...] = jnp.concatenate(
        [whole[1072:1088, at * SLAB : at * SLAB + DL] for at in range(3)], axis=0
    )


def project_store(whole, out, out_layout, biases_t, gains_t, offsets_t, biases_l, gains_l, offsets_l):
    out[...] = whole[:576, :]
    out_layout[...] = jnp.concatenate(
        [whole[576:624, at * SLAB : at * SLAB + DL] for at in range(3)], axis=0
    )
    biases_t[...] = whole[624:630, : DT // 4]
    gains_t[...] = whole[630:632, : DT // 4]
    offsets_t[...] = whole[632:633, :].reshape(DT)
    biases_l[...] = whole[624:630, SLAB : SLAB + DL // 4]
    gains_l[...] = whole[630:632, SLAB : SLAB + DL // 4]
    offsets_l[...] = whole[633:634, : FL // 4].reshape(FL // 4)


def final_kernel(store, dp_size, subs, *refs):
    sources, outs, whole = refs[: 2 * len(subs)], refs[2 * len(subs) + 1 : -1], refs[-1]
    lines_in_order(dp_size, sources, subs, whole)
    store(whole, *outs[:-1])
    outs[-1][...] = whole[:8, :LANES]


def final_call(store, name, sources, after, dp_size, subs, outs):
    return pl.pallas_call(
        functools.partial(final_kernel, store, dp_size, subs),
        out_shape=tuple(shape_of(shape, F32) for shape in outs) + (shape_of((8, LANES), F32),),
        in_specs=[VMEM] * len(sources) + [after[1]],
        out_specs=[VMEM] * (len(outs) + 1),
        scratch_shapes=[pltpu.VMEM((total_lines(subs), DT), F32)],
        compiler_params=pltpu.CompilerParams(vmem_limit_bytes=SMALL),
        cost_estimate=COST,
        name=name,
    )(*sources, after[0])


def add_kernel(count, parts, *refs):
    sources, targets = refs[: count * parts], refs[count * parts + 1 :]
    for at, target in enumerate(targets):
        total = sources[at][...].astype(F32)
        for n in range(1, count):
            total += sources[n * parts + at][...].astype(F32)
        target[...] = total.astype(BF16)


def add_call(sources, parts, after):
    lines, width = sources[0].shape
    size = lines // parts
    steps = max(n for n in (1, 2, 3, 4) if size % (16 * n) == 0 and (n == 1 or lines // n >= 256))
    block = size // steps
    specs = [
        pl.BlockSpec((block, width), functools.partial(lambda at, i: (at * steps + i, 0), at))
        for unused in sources
        for at in range(parts)
    ]
    return pl.pallas_call(
        functools.partial(add_kernel, len(sources), parts),
        grid=(steps,),
        out_shape=(shape_of((size, width), BF16),) * parts,
        in_specs=specs + [after[1]],
        out_specs=[pl.BlockSpec((block, width), lambda i: (i, 0))] * parts,
        compiler_params=pltpu.CompilerParams(vmem_limit_bytes=SMALL),
        cost_estimate=COST,
        name="add",
    )(*[source for source in sources for unused in range(parts)], after[0])


def gate_call(arrays, after):
    count = len(arrays)
    return pl.pallas_call(
        lambda *refs: None,
        out_shape=tuple(shape_of(array.shape, array.dtype) for array in arrays),
        in_specs=[ANY] * count + [after[1]],
        out_specs=[ANY] * count,
        input_output_aliases={at: at for at in range(count)},
        compiler_params=pltpu.CompilerParams(vmem_limit_bytes=SMALL),
        cost_estimate=COST,
        name="gate",
    )(*arrays, after[0])


def join_kernel(count, *refs):
    sources, target = refs[:count], refs[-1]
    size = sources[0].shape[0]
    for at, source in enumerate(sources):
        target[at * size : (at + 1) * size, :] = source[...]


def join_call(sources, after):
    lines, width = sources[0].shape
    return pl.pallas_call(
        functools.partial(join_kernel, len(sources)),
        out_shape=shape_of((len(sources) * lines, width), BF16),
        in_specs=[VMEM] * len(sources) + [after[1]],
        out_specs=VMEM,
        compiler_params=pltpu.CompilerParams(vmem_limit_bytes=SMALL),
        cost_estimate=COST,
        name="join",
    )(*sources, after[0])


def sent(array, group, index, seq_size, dp_size):
    across = other = 0
    for n, (axis, bit) in enumerate(group):
        if index & (1 << n):
            if axis == "seq":
                across |= bit
            else:
                other |= bit
    if not other:
        return lax.ppermute(array, "seq", [(at, at ^ across) for at in range(seq_size)])
    if not across:
        return lax.ppermute(array, "dp", [(at, at ^ other) for at in range(dp_size)])
    pairs = [
        (d * seq_size + s, (d ^ other) * seq_size + (s ^ across))
        for d in range(dp_size)
        for s in range(seq_size)
    ]
    return lax.ppermute(array, ("dp", "seq"), pairs)


def steps_of(give, hold, hops, growth, send):
    parts = [hold, send(give, (("seq", 1),), 1)]
    for group in hops:
        keep, *sends = yield functools.partial(add_call, parts, 1 << len(group))
        parts = [keep] + [send(array, group, at + 1) for at, array in enumerate(sends)]
    (piece,) = yield functools.partial(add_call, parts, 1)
    gathered = [piece]
    for group in growth:
        if len(gathered) > 1:
            piece = yield functools.partial(join_call, gathered)
        gathered = [piece] + [send(piece, group, at) for at in range(1, 1 << len(group))]
    return gathered


X = ("dp", 1)
Y = ("seq", 2)
Z1 = ("dp", 2)
Z2 = ("dp", 4)


def hops_of(text, extra):
    groups = {"x": (X,), "y": (Y,), "1": (Z1,), "2": (Z2,), "d": (Y, X), "z": (Z1, Z2)}
    return tuple(groups[letter] for letter in text) + extra


SPLIT_S = ((768, "y1x2B"), )
SPLIT_E = ((576, "1xy2B"), (576, "xyzB"), )
SPLIT_P = ((256, "xy12B"), (384, "yxzB"), )
ORDER = ('B', 'NE', 'S0', 'E1', 'E0', 'C', 'GP', 'E1', 'S0', 'E0', 'P0', 'P1', 'D', 'E1', 'S0', 'E0', 'GX', 'E1', 'X0', 'E0', 'E1', 'S0', 'P0', 'E0', 'FX', 'E1', 'S0', 'P0', 'E0', 'P0', 'P1', 'S0', 'P0', 'E0', 'P1', 'P0', 'S0', 'P0', 'P1', 'FE', 'HP0', 'P1', 'P1', 'FS', 'FP')


def local(
    dp_size,
    seq_size,
    text_input,
    layout_input,
    segments,
    text_cotangent,
    layout_cotangent,
    text_project,
    text_biases,
    text_gains,
    text_merge,
    text_expand,
    text_offsets,
    text_shrink,
    layout_project,
    layout_biases,
    layout_gains,
    layout_merge,
    layout_expand,
    layout_offsets,
    layout_shrink,
):
    packs, rows, unused = text_input.shape

    def send(array, group, index):
        return sent(array, group, index, seq_size, dp_size)

    core = (("seq", 1),)
    own, wl, line_t, line_l = prepare_call(
        text_input, layout_input.transpose(0, 2, 1), segments, layout_project, text_offsets, layout_offsets
    )
    far, near = send(own, (Y,), 1), send(own, core, 1)
    blocks = (own, near, far, send(far, core, 1))
    turned_shrink = layout_shrink.T

    bits = [1 << at for at in range((dp_size - 1).bit_length())]
    extra = tuple((("dp", bit),) for bit in bits[3:])
    growths = {
        "B": tuple(reversed(extra)) + ((Z2,), (Z1,), (X,)),
        "D": tuple(reversed(extra)) + ((Z1, Z2), (X,)),
        "F": tuple(reversed(extra)) + ((Z2,), (X,), (Z1,)),
    }
    subs = {
        name: sub_chunks(count, [(share, hops_of(text[:-1], extra), growths[text[-1]]) for share, text in split], dp_size)
        for name, count, split in (
            ("S", S_ROWS, SPLIT_S),
            ("E", E_ROWS, SPLIT_E),
            ("P", P_ROWS, SPLIT_P),
        )
    }
    reductions = {}
    calls = {}
    halves = {}
    values = {}
    token = None

    def begin(name, pairs):
        for at, (first, count, hops, growth) in enumerate(subs[name]):
            steps = steps_of(pairs[2 * at], pairs[2 * at + 1], hops, growth, send)
            reductions[name + str(at)] = steps
            calls[name + str(at)] = next(steps)

    def forward(after):
        (
            res_t, res_l, q_t, q_l, kt, kl, vt, vl, p, ctx_t, ctx_l,
            hid_t, unit_t, inv_t, sum_t, slope_t,
            hid_l, unit_l, inv_l, sum_l, slope_l, act_l, sf_t, sf_l,
            *pairs,
        ) = forward_call(
            blocks, text_project, wl, text_merge, text_expand, text_shrink,
            layout_merge, layout_expand, turned_shrink,
            text_cotangent, layout_cotangent.transpose(0, 2, 1),
            text_biases, text_gains, line_t, layout_biases, layout_gains,
            line_l, packs, rows, dp_size, subs["S"],
        )
        begin("S", pairs)
        values.update(
            results=(res_t, res_l),
            tail=(
                hid_t, unit_t, inv_t, sum_t, slope_t, hid_l, unit_l, inv_l, sum_l, slope_l, act_l,
                ctx_t, ctx_l,
            ),
            attended=(kt, kl, vt, vl, p, q_t, q_l),
            contexts=(ctx_t, ctx_l),
            first_sums=(sf_t, sf_l),
        )
        return sf_t, HBM

    def middle(after):
        mid_t, mid_l, dctx_t, dctx_l, sm_t, sm_l, so_t, so_l, *pairs = middle_call(
            (
                *values["tail"], text_shrink, text_expand, text_merge, turned_shrink,
                layout_expand, layout_merge, text_gains, layout_gains, after[0],
            ),
            packs, rows, dp_size, subs["E"],
        )
        values["E pairs"] = pairs
        values.update(
            middles=(mid_t, mid_l), deltas=(dctx_t, dctx_l), second_sums=(sm_t, sm_l, so_t, so_l)
        )
        return sm_t, HBM

    def attention(after):
        joined_t, joined_l, query_t, query_l, *pairs = attention_call(
            (
                *blocks, *values["attended"], *values["deltas"],
                *values["contexts"], *values["first_sums"], *values["second_sums"], after[0],
            ),
            packs, rows, dp_size, subs["P"],
        )
        values["P pairs"] = pairs
        values.update(joined=(joined_t, joined_l, query_t, query_l))
        return query_l, HBM

    def inputs(after):
        give, hold, mark = input_call(*values["joined"], text_project, wl, after, packs, rows)
        values["X pairs"] = [give, hold]
        return mark, ANY

    def inputs_gate(after, gated=True):
        give, hold = gate_call(values["X pairs"], after) if gated else values["X pairs"]
        lines = 2 * (DT + DL)
        values.update(inputs=[hold.reshape(lines, -1), send(give, core, 1).reshape(lines, -1)])
        return (hold, ANY) if gated else after

    def gate(name, gated=True):
        def call(after):
            pairs = gate_call(values[name + " pairs"], after) if gated else values[name + " pairs"]
            begin(name, pairs)
            return (pairs[1], ANY) if gated else after

        return call

    def arrive(name, after):
        while name in calls:
            after = advance(name, after)
        halves[name] = list(gate_call(halves[name], after))
        return halves[name][1], ANY

    def inputs_add(after):
        own, onward = add_call(values["inputs"], 2, after)
        values.update(onward=(own, send(onward, (Y,), 1)))
        return own, ANY

    def inputs_end(after):
        values.update(sens=sensitivity_call(*values["onward"], *values["middles"], after))
        return values["sens"][2], ANY

    def end(name, store, label, outs):
        def call(after):
            sources = [array for at in range(len(subs[name])) for array in halves[name + str(at)]]
            values[name] = final_call(
                store, label, sources, after, dp_size, subs[name], outs
            )
            return values[name][-1], ANY

        return call

    kernels = {
        "A": forward,
        "B": middle,
        "C": attention,
        "D": inputs,
        "GE": gate("E"),
        "GP": gate("P"),
        "GX": inputs_gate,
        "NE": gate("E", False),
        "NP": gate("P", False),
        "NX": functools.partial(inputs_gate, gated=False),
        "HP0": functools.partial(arrive, "P0"),
        "X0": inputs_add,
        "FX": inputs_end,
        "FS": end("S", shrink_store, "shrink_out", [(DT // 4, FT)]),
        "FE": end(
            "E", expand_store, "expand_out",
            [(DT, DT), (DT // 4, DT), (DL, DL), (DL // 4, FL), (DL // 4, DL)],
        ),
        "FP": end(
            "P", project_store, "project_out",
            [
                (576, DT), (144, DL), (6, DT // 4), (2, DT // 4), (DT,),
                (6, DL // 4), (2, DL // 4), (FL // 4,),
            ],
        ),
    }

    def advance(name, after):
        outs = calls[name](after)
        try:
            calls[name] = reductions[name].send(outs)
        except StopIteration as stop:
            halves[name] = stop.value
            del calls[name]
        return (outs[0] if isinstance(outs, (tuple, list)) else outs), ANY

    def finish(name, after):
        for at in range(len(subs[name])):
            while name + str(at) in calls:
                after = advance(name + str(at), after)
        return after

    token = forward(None)
    for label in ORDER:
        if label in kernels:
            if label[0] == "F" and label[1] in subs:
                token = finish(label[1], token)
            token = kernels[label](token)
        elif label in calls:
            token = advance(label, token)

    res_t, res_l = values["results"]
    sens_t, sens_l, unused = values["sens"]
    shrink_t, unused = values["S"]
    expand_t, merge_t, expand_l, shrink_l, merge_l, unused = values["E"]
    project_t, project_l, biases_t, gains_t, offsets_t, biases_l, gains_l, offsets_l, unused = values["P"]
    return (
        res_t.reshape(packs, rows, DT),
        res_l.transpose(0, 2, 1),
        sens_t.reshape(packs, rows, DT),
        sens_l.transpose(0, 2, 1),
        project_t.T,
        biases_t,
        gains_t,
        merge_t.T,
        expand_t,
        offsets_t,
        shrink_t.T,
        project_l.T,
        biases_l,
        gains_l,
        merge_l.T,
        expand_l,
        offsets_l,
        shrink_l.T,
    )


def solution(mesh):
    rows = P("dp", "seq", None)
    columns = P(None, "seq")
    in_specs = (rows, rows, P("dp", "seq"), rows, rows) + (P(),) * 14
    out_specs = (
        (rows,) * 4 + (columns,) * 5 + (P("seq"),) + (columns,) * 6 + (P("seq"),) + (columns,)
    )
    body = functools.partial(local, mesh.shape["dp"], mesh.shape["seq"])
    return jax.shard_map(body, mesh=mesh, in_specs=in_specs, out_specs=out_specs, check_vma=False)
```
